32 devices in a mesh: section: 2 (over core), seq: 8 (over z, y), mp: 2 (over x).
Axes of the slice: x: 2, y: 2, z: 4, core: 2. Of those that a mesh axis runs over, the one named last changes fastest.
Arguments:
- x_in: bfloat16 [2, 512, 8192], P(None, 'mp', 'seq'), may hold values from -14 to 14
- skip_in: float32 [2, 512, 8192], P(None, 'mp', 'seq'), may hold values from -6 to 6
- cot_res: float32 [2, 512, 8192], P(None, 'mp', 'seq'), may hold values from -6 to 6
- cot_skip: float32 [2, 512, 8192], P(None, 'mp', 'seq'), may hold values from -6 to 6
- lengths: int32 [2], replicated, may hold values from 4096 to 8192, as said below
- speakers: int32 [2], replicated, may hold values from 0 to 108
- conv_weight: float32 [2, 2, 512, 2, 512], P('section', None, None, None, 'mp'), may hold values from -0.1875 to 0.1875
- conv_m: float32 [2, 2, 512, 2, 512], P('section', None, None, None, 'mp'), may hold values from -80 to 80
- conv_v: float32 [2, 2, 512, 2, 512], P('section', None, None, None, 'mp'), may hold values from 13.1072 to 52.4288
- out_weight: float32 [2, 512, 1024], P('section', 'mp'), may hold values from -0.75 to 0.75
- out_m: float32 [2, 512, 1024], P('section', 'mp'), may hold values from -24 to 24
- out_v: float32 [2, 512, 1024], P('section', 'mp'), may hold values from 0.98304 to 4.096
- speaker_table: float32 [2, 109, 2, 512], P('section', None, None, 'mp'), may hold values from -3 to 3
- table_m: float32 [2, 109, 2, 512], P('section', None, None, 'mp'), may hold values from -56 to 56
- table_v: float32 [2, 109, 2, 512], P('section', None, None, 'mp'), may hold values from 6.5536 to 26.2144
Outputs:
- res_out: float32 [2, 2, 512, 8192], P('section', None, 'mp', 'seq')
- skip_out: float32 [2, 2, 512, 8192], P('section', None, 'mp', 'seq')
- grad_in: float32 [2, 2, 512, 8192], P('section', None, 'mp', 'seq')
- rms_out: float32 [2, 2], P('section')
- conv_grad: float32 [2, 2, 512, 2, 512], P('section', None, None, None, 'mp')
- conv_new: float32 [2, 2, 512, 2, 512], P('section', None, None, None, 'mp')
- conv_m_new: float32 [2, 2, 512, 2, 512], P('section', None, None, None, 'mp')
- conv_v_new: float32 [2, 2, 512, 2, 512], P('section', None, None, None, 'mp')
- out_grad: float32 [2, 512, 1024], P('section', 'mp')
- out_new: float32 [2, 512, 1024], P('section', 'mp')
- out_m_new: float32 [2, 512, 1024], P('section', 'mp')
- out_v_new: float32 [2, 512, 1024], P('section', 'mp')
- table_grad: float32 [2, 109, 2, 512], P('section', None, None, 'mp')
- table_new: float32 [2, 109, 2, 512], P('section', None, None, 'mp')
- table_m_new: float32 [2, 109, 2, 512], P('section', None, None, 'mp')
- table_v_new: float32 [2, 109, 2, 512], P('section', None, None, 'mp')
The draws below stay inside these ranges and needn't reach their ends.
Inputs may be any that keep to these rules, and one draw needn't show every extreme that they name: lengths[m] counts the valid samples at the start of micro-batch m, after which its tail is masked; some micro-batch is valid over all 8192 samples.
All inputs are finite; a program needn't handle non-finite values.
Results may differ from the reference program's by a relative error of at most 0.0091.
Values may be sent and summed in bfloat16 or wider, within the bound.
A program may use at most 128 MiB of HBM per device.

```python
import math
import jax
import jax.numpy as jnp
import numpy as np
from jax import lax

R = 512
S = 512
G = 512
NSPK = 109
FIRST_DILATION = 512
MB = 2
STEP = 10
L = 8192


def draw_x_in(key, part):
    key = jax.random.fold_in(key, 11)
    times = jnp.arange(L, dtype=jnp.float32) / L
    channels = jnp.arange(R, dtype=jnp.float32) / R
    base = jnp.clip(jax.random.normal(key, (MB, R, L), jnp.float32), -5.0, 5.0)
    ramp = (0.5 + times)[None, None, :] * (0.6 + 1.2 * channels)[None, :, None]
    return (base * ramp).astype(jnp.bfloat16)


def draw_lengths(key, part):
    key = jax.random.fold_in(key, 23)
    drawn = jax.random.randint(key, (MB,), L // 2, L + 1)
    longest = jax.random.randint(jax.random.fold_in(key, 5), (), 0, MB)
    return jnp.where(jnp.arange(MB) == longest, L, drawn).astype(jnp.int32)


def level_of(key, dims, shards, low, high):
    level, own = 1.0, jax.random.fold_in(key, 6)
    for axis_at, shards_of in shards:
        draws = jnp.exp(jax.random.uniform(jax.random.fold_in(own, axis_at), (shards_of,), jnp.float32, low / len(shards), high / len(shards)))
        level = level * jnp.repeat(draws, dims[axis_at] // shards_of).reshape([-1 if axis == axis_at else 1 for axis in range(len(dims))])
    return level


def rank_bounds(amount, slope):
    loads = [(1 << 20) // math.isqrt(rank ** slope) + 1 for rank in range(1, amount + 1)]
    deviation = 1 + sum(loads) // (1 << 30)
    return np.cumsum(np.array([max(1, weight // deviation) for weight in loads]))


def ranked(stream_key, shape, number_of, slope):
    grid = rank_bounds(number_of, slope)
    pick = jax.random.randint(jax.random.fold_in(stream_key, 1), shape, 0, int(grid[number_of - 1]))
    rank = jnp.searchsorted(jnp.asarray(grid, jnp.int32), pick, side="right")
    return jax.random.permutation(jax.random.fold_in(stream_key, 2), number_of)[rank].astype(jnp.int32)


def normal_values(rng, extent, deviation, limit, cuts=(), held_as=jnp.bfloat16):
    result = jax.random.normal(rng, extent, jnp.float32) * deviation
    if len(cuts) > 0:
        result = level_of(rng, extent, cuts, -0.22, 0.18) * result
    return jnp.clip(result, min=-limit, max=limit).astype(held_as)


def setup_inputs(seed: int = 0) -> dict:
    streams_of = jax.random.split(jax.random.key(seed), 16)
    x_in = draw_x_in(jax.random.fold_in(streams_of[15], 71), 0)
    skip_in = normal_values(streams_of[1], (MB, S, L), 1.0, 6.0, ((1, 2), (2, 8)), jnp.float32)
    cot_res = normal_values(streams_of[2], (MB, R, L), 1.0, 6.0, ((1, 2), (2, 8)), jnp.float32)
    cot_skip = normal_values(streams_of[3], (MB, S, L), 1.0, 6.0, ((1, 2), (2, 8)), jnp.float32)
    lengths = draw_lengths(jax.random.fold_in(streams_of[15], 71), 0)
    speakers = ranked(streams_of[5], (MB,), NSPK, 2)
    conv_weight = normal_values(streams_of[6], (2, 2, R, 2, G), (2 * R) ** -0.5, 0.1875, ((0, 2), (4, 2)), jnp.float32)
    conv_m = normal_values(streams_of[7], (2, 2, R, 2, G), (0.1 * (MB * L) ** 0.5), 80.0, ((0, 2), (4, 2)), jnp.float32)
    conv_v = jnp.clip(jnp.exp(math.log(52.4288) - 1.3862944 * jax.random.uniform(streams_of[8], (2, 2, R, 2, G), jnp.float32) ** level_of(streams_of[8], (2, 2, R, 2, G), ((0, 2), (4, 2)), -0.2, 0.2)), 13.1072, 52.4288)
    out_weight = normal_values(streams_of[9], (2, G, R + S), (G // 8) ** -0.5, 0.75, ((0, 2), (1, 2)), jnp.float32)
    out_m = normal_values(streams_of[10], (2, G, R + S), (0.03 * (MB * L) ** 0.5), 24.0, ((0, 2), (1, 2)), jnp.float32)
    out_v = jnp.clip(jnp.exp(math.log(4.096) - 1.4271164 * jax.random.uniform(streams_of[11], (2, G, R + S), jnp.float32) ** level_of(streams_of[11], (2, G, R + S), ((0, 2), (1, 2)), -0.2, 0.2)), 0.98304, 4.096)
    speaker_table = normal_values(streams_of[12], (2, NSPK, 2, G), 0.5, 3.0, ((0, 2), (3, 2)), jnp.float32)
    table_m = normal_values(streams_of[13], (2, NSPK, 2, G), (0.1 * L ** 0.5), 56.0, ((0, 2), (3, 2)), jnp.float32)
    table_v = jnp.clip(jnp.exp(math.log(26.2144) - 1.3862944 * jax.random.uniform(streams_of[14], (2, NSPK, 2, G), jnp.float32) ** level_of(streams_of[14], (2, NSPK, 2, G), ((0, 2), (3, 2)), -0.2, 0.2)), 6.5536, 26.2144)
    return {"x_in": x_in, "skip_in": skip_in, "cot_res": cot_res, "cot_skip": cot_skip, "lengths": lengths, "speakers": speakers, "conv_weight": conv_weight, "conv_m": conv_m, "conv_v": conv_v, "out_weight": out_weight, "out_m": out_m, "out_v": out_v, "speaker_table": speaker_table, "table_m": table_m, "table_v": table_v}


@jax.custom_vjp
def low(v):
    return lax.optimization_barrier(v.astype(jnp.bfloat16)).astype(jnp.float32)

@jax.custom_vjp
def low_back(v):
    return v

def low_keep(v):
    return (low(v), None)

def low_pass(kept, grad):
    return (grad,)

def back_keep(v):
    return (v, None)

def back_low(kept, grad):
    return (low(grad),)
low.defvjp(low_keep, low_pass)
low_back.defvjp(back_keep, back_low)
highest = lax.Precision.HIGHEST
beta_one = 0.9
beta_two = 0.999
adam_eps = 1e-08
decay_rate = 0.01
root_half = math.sqrt(0.5)

def gated_dilated_layer(residual_stream, skip_accumulated, convolution_kernel, output_kernel, speaker_lookup, speaker_ids, dilation_factor):
    input_signal = low(residual_stream)
    delayed_tap = jnp.pad(input_signal, ((0, 0), (dilation_factor, 0), (0, 0)))[:, :input_signal.shape[1], :]
    tap_rows = jnp.concatenate([delayed_tap, input_signal], axis=2)
    conv_matrix = low(convolution_kernel).reshape(2 * R, 2 * G)
    embedding = low(speaker_lookup).reshape(NSPK, 2 * G)[speaker_ids]
    preact = low_back(jnp.einsum('blk,kg->blg', tap_rows, conv_matrix, precision=highest) + embedding[:, None, :])
    hidden = low(jnp.tanh(preact[..., :G]) * jax.nn.sigmoid(preact[..., G:]))
    projected = low_back(jnp.einsum('blg,gk->blk', hidden, low(output_kernel), precision=highest))
    branch = projected[..., :R]
    new_resid = (residual_stream + branch) * root_half
    new_skip = skip_accumulated + projected[..., R:]
    return (new_resid, new_skip, branch)

def adamw(weight, moment, second, gradient, step_rate):
    moment_new = beta_one * moment + (1.0 - beta_one) * gradient
    second_new = beta_two * second + (1.0 - beta_two) * gradient * gradient
    corr_one = 1.0 - beta_one ** STEP
    corr_two = 1.0 - beta_two ** STEP
    update = moment_new / corr_one / (jnp.sqrt(second_new / corr_two) + adam_eps)
    weight_new = weight - step_rate * (update + decay_rate * weight)
    return (weight_new, moment_new, second_new)

def time_last(value):
    return jnp.swapaxes(value, -1, -2)

def reference(x_in, skip_in, cot_res, cot_skip, lengths, speakers, conv_weight, conv_m, conv_v, out_weight, out_m, out_v, speaker_table, table_m, table_v):
    valid_mask = (jnp.arange(L)[None, :] < lengths[:, None]).astype(jnp.float32)[:, :, None]
    resid_in = time_last(x_in.astype(jnp.float32))
    skip_start = time_last(skip_in)
    probe_zero = jnp.zeros_like(resid_in)

    def forward(residual_stream, skip_accumulated, probe_in, convolution_kernel, output_kernel, speaker_lookup):
        first_residual, first_skip_output, first_branch_output = gated_dilated_layer(residual_stream, skip_accumulated, convolution_kernel[0], output_kernel[0], speaker_lookup[0], speakers, FIRST_DILATION)
        first_residual = first_residual + probe_in
        res_two, skip_two, branch_two = gated_dilated_layer(first_residual, first_skip_output, convolution_kernel[1], output_kernel[1], speaker_lookup[1], speakers, 1)
        return ((first_residual, first_skip_output, res_two, skip_two), (first_branch_output, branch_two))
    results, pullback, branches = jax.vjp(forward, resid_in, skip_start, probe_zero, conv_weight, out_weight, speaker_table, has_aux=True)
    first_residual, first_skip_output, res_two, skip_two = results
    cotangents = (jnp.zeros_like(first_residual), jnp.zeros_like(first_skip_output), valid_mask * time_last(cot_res), valid_mask * time_last(cot_skip))
    grad_resid, grad_skip, grad_probe, conv_grad, out_grad, table_grad = pullback(cotangents)
    res_out = time_last(jnp.stack([first_residual, res_two]))
    skip_out = time_last(jnp.stack([first_skip_output, skip_two]))
    grad_in = time_last(jnp.stack([grad_resid, grad_probe]))
    counted = jnp.sum(valid_mask) * R
    rms_rows = []
    for resid_val, branch_val in ((first_residual, branches[0]), (res_two, branches[1])):
        rms_rows.append(jnp.stack([jnp.sqrt(jnp.sum(valid_mask * resid_val * resid_val) / counted), jnp.sqrt(jnp.sum(valid_mask * branch_val * branch_val) / counted)]))
    rms_out = jnp.stack(rms_rows)
    conv_new, conv_m_new, conv_v_new = adamw(conv_weight, conv_m, conv_v, conv_grad, 0.03)
    out_new, out_m_new, out_v_new = adamw(out_weight, out_m, out_v, out_grad, 0.1)
    table_new, table_m_new, table_v_new = adamw(speaker_table, table_m, table_v, table_grad, 0.3)
    return (res_out, skip_out, grad_in, rms_out, conv_grad, conv_new, conv_m_new, conv_v_new, out_grad, out_new, out_m_new, out_v_new, table_grad, table_new, table_m_new, table_v_new)
```

```python
import functools
import math

import jax
import jax.numpy as jnp
from jax import lax
from jax.experimental import pallas as pl
from jax.experimental.pallas import tpu as pltpu
from jax.sharding import PartitionSpec as P

FIRST_DILATION = 512
STEP = 10
MESH = pl.DeviceIdType.MESH
TILE = 256
UNITS = 6
Z_FIRST = 3

beta_one = 0.9
beta_two = 0.999
adam_eps = 1e-08
decay_rate = 0.01
root_half = math.sqrt(0.5)


def passed_along(value, axis, steps):
    count = lax.axis_size(axis)
    first, last = (max(0, -steps), min(count, count - steps))
    return lax.ppermute(value, axis, [(source, source + steps) for source in range(first, last)])


def adamw(weight, moment, second, gradient, step_rate):
    moment_new = beta_one * moment + (1.0 - beta_one) * gradient
    second_new = beta_two * second + (1.0 - beta_two) * gradient * gradient
    corr_one = 1.0 - beta_one**STEP
    corr_two = 1.0 - beta_two**STEP
    update = moment_new / corr_one / (jnp.sqrt(second_new / corr_two) + adam_eps)
    weight_new = weight - step_rate * (update + decay_rate * weight)
    return (weight_new, moment_new, second_new)


def dot(left, right):
    return jnp.dot(left, right, preferred_element_type=jnp.float32)


def dot_last(left, right):
    return lax.dot_general(
        left, right, (((1,), (1,)), ((), ())), preferred_element_type=jnp.float32
    )


def rows_at(start, size):
    return pl.ds(start if isinstance(start, int) else pl.multiple_of(start, 16), size)


def cols_at(start, size):
    return pl.ds(start if isinstance(start, int) else pl.multiple_of(start, 128), size)


def layers_kernel(
    sizes,
    x_ref,
    skip_ref,
    cot_res_ref,
    cot_skip_ref,
    lengths_ref,
    speakers_ref,
    conv_ref,
    out_ref,
    table_ref,
    res_ref,
    skipped_ref,
    grad_ref,
    weight_ref,
    small_ref,
    conv_wide,
    out_wide,
    table_wide,
    xf,
    wc,
    wct,
    wo,
    wot,
    et,
    in1,
    next_out,
    next_in,
    past1,
    act_f,
    act_q,
    hid,
    dproj,
    dres0,
    dpre,
    grad1,
    past_grad1,
    edge_out,
    edge_in,
    res0,
    skip_sum,
    cot_a,
    cot_b,
    skip_low,
    res_low,
    grad1_low,
    grad0,
    past0_out,
    past0_in,
    grad0_low,
    stats,
    acc,
    from_core,
    down,
    final,
    small,
    small_in,
    small_sum,
    send_sem,
    recv_sem,
    local_sem,
):
    full, local, gates, span, n_seq = sizes
    gate_local = gates // 2
    width = 2 * gate_local
    halo = FIRST_DILATION
    n_z = n_seq // 2
    c = lax.axis_index("section")
    s = lax.axis_index("seq")
    x = lax.axis_index("mp")
    z, y = s // 2, s % 2
    oc, ox = 1 - c, 1 - x
    bf16, f32 = jnp.bfloat16, jnp.float32
    counts = {"send": 0, "recv": 0, "local": 0}
    pending = []
    inside = [None]

    def take(kind, amount=1):
        counts[kind] += amount
        return counts[kind] - amount

    def when(cond, action):
        if cond is None:
            action()
        else:
            pl.when(cond)(action)

    def on(cond, action):
        inside[0] = cond
        pl.when(cond)(lambda: action())
        inside[0] = None

    def send(source, target, device, recv_at, cond=None):
        at = take("send")

        def make():
            return pltpu.make_async_remote_copy(
                src_ref=source(),
                dst_ref=target(),
                send_sem=send_sem.at[at],
                recv_sem=recv_sem.at[recv_at()],
                device_id=device(),
                device_id_type=MESH,
            )

        when(cond, lambda: make().start())
        pending.append((lambda: make().wait_send(), inside[0] if cond is None else cond))

    def arrive(target, recv_at, cond=None):
        when(
            cond,
            lambda: pltpu.make_async_remote_copy(
                src_ref=target,
                dst_ref=target,
                send_sem=send_sem.at[0],
                recv_sem=recv_sem.at[recv_at],
                device_id={"section": oc},
                device_id_type=MESH,
            ).wait_recv(),
        )

    def fetch(source, target, cond=None):
        copy = pltpu.make_async_copy(source, target, local_sem.at[take("local")])
        when(cond, copy.start)
        return copy

    def to(axis, index):
        return lambda: {axis: index()}

    core_dev = to("section", lambda: 1 - c)
    mp_dev = to("mp", lambda: 1 - x)
    y_dev = to("seq", lambda: z * 2 + 1 - y)
    prev_dev, next_dev = to("seq", lambda: s - 1), to("seq", lambda: s + 1)
    has_prev, has_next = s > 0, s < n_seq - 1

    z_seqs = [lax.rem(z + step, n_z) * 2 + y for step in range(n_z)]

    def z_seq(step):
        return z_seqs[step]

    def z_dev(step):
        return to("seq", lambda: z_seq(step))

    bits = [y] + [(z // (1 << bit)) % 2 for bit in range((n_seq // 2).bit_length() - 1)]
    pairs = [z * 2 + 1 - y] + [
        (z + (1 - 2 * bits[bit + 1]) * (1 << bit)) * 2 + y for bit in range(len(bits) - 1)
    ]
    depth = len(bits)
    pair_devs = [to("seq", lambda way=way: pairs[way]) for way in range(depth)]

    barrier = pltpu.get_barrier_semaphore()
    for device in [core_dev, mp_dev, y_dev, *[z_dev(step) for step in range(1, n_z)]]:
        pl.semaphore_signal(barrier, inc=1, device_id=device(), device_id_type=MESH)
    before, after = (y == 0) & (z > 0), (y == 1) & (z < n_z - 1)

    @pl.when(before)
    def _():
        pl.semaphore_signal(barrier, inc=1, device_id=prev_dev(), device_id_type=MESH)

    @pl.when(after)
    def _():
        pl.semaphore_signal(barrier, inc=1, device_id=next_dev(), device_id_type=MESH)

    own_rows, other_rows = rows_at(x * local, local), rows_at(ox * local, local)
    got_conv = fetch(conv_ref, conv_wide)
    got_table = fetch(table_ref, table_wide)
    got_out = fetch(out_ref, out_wide)
    got_cot_a = fetch(cot_res_ref.at[c], cot_a)
    got_cot_b = fetch(cot_skip_ref.at[c], cot_b)
    chunks = span // halo
    got_x = [
        fetch(x_ref.at[c, :, pl.ds(chunk * halo, halo)], xf.at[chunk + 1, own_rows])
        for chunk in range(chunks)
    ]
    got_skip = fetch(skip_ref.at[c], skip_sum)

    def cast_conv(step, carry):
        for block in range(width // 128):
            half, lane = block // (gate_local // 128), block % (gate_local // 128)
            first = step * 256 * (width // 128) + lane * 2 + half
            wc[c, x, rows_at(step * 256, 256), pl.ds(block * 128, 128)] = conv_wide[
                pl.ds(first, 256, stride=width // 128), :
            ].astype(bf16)
        return carry

    got_conv.wait()
    lax.fori_loop(0, 2 * full // 256, cast_conv, None)
    got_table.wait()
    marks = lax.broadcasted_iota(jnp.int32, (16, width), 0)
    emb = jnp.zeros((16, width), f32)
    for micro in range(2):
        rows = table_wide[speakers_ref[micro]]
        row = jnp.concatenate([rows[0:1, :], rows[1:2, :]], axis=1)
        emb = jnp.where(marks == micro, row, emb)
    wc[c, x, 2 * full : 2 * full + 16, :] = emb.astype(bf16)
    got_out.wait()
    wo[c, rows_at(x * gate_local, gate_local), :] = out_wide[...].astype(bf16)

    @pl.when(before | after)
    def _():
        pl.semaphore_wait(barrier, 3 + n_z)

    @pl.when(jnp.logical_not(before | after))
    def _():
        pl.semaphore_wait(barrier, 2 + n_z)

    conv_rows, out_rows = 2 * full // n_seq, gate_local // n_seq
    conv_at, conv_core_at = take("recv", n_seq), take("recv", n_seq)
    out_at, emb_at = take("recv", n_seq), take("recv")

    def conv_slice(index, layer, block):
        return wc.at[layer, block, rows_at(index * conv_rows, conv_rows)]

    def out_slice(index, layer, block):
        return wo.at[layer, rows_at(block * gate_local + index * out_rows, out_rows)]

    def emb_part(layer, block):
        return wc.at[layer, block, 2 * full : 2 * full + 16]

    def conv_block(layer, block):
        return wc.at[layer, block, 0 : 2 * full]

    def out_block(layer, block):
        return wo.at[layer, rows_at(block * gate_local, gate_local)]

    def send_same(ref, device, recv_at, cond=None):
        send(ref, ref, device, recv_at, cond)

    def cross_weights():
        send_same(lambda: conv_slice(s, c, x), mp_dev, lambda: conv_at + s)
        send_same(lambda: emb_part(c, x), mp_dev, lambda: emb_at)
        send_same(lambda: out_slice(s, c, x), mp_dev, lambda: out_at + s)

    on(c == 0, cross_weights)
    x_at = [take("recv") for _ in range(chunks)]
    for copy in got_x:
        copy.wait()
    for chunk in reversed(range(chunks)):
        send_same(
            lambda chunk=chunk: xf.at[chunk + 1, own_rows], mp_dev, lambda chunk=chunk: x_at[chunk]
        )
    on(c == 1, cross_weights)
    halo_at = [take("recv"), take("recv")]
    send(
        lambda: xf.at[chunks, own_rows],
        lambda: xf.at[0, own_rows],
        next_dev,
        lambda: halo_at[0],
        has_next,
    )
    core_at = [take("recv") for _ in range(5)]
    send_same(lambda: conv_block(c, x), core_dev, lambda: core_at[0])
    send_same(lambda: emb_part(c, x), core_dev, lambda: core_at[1])
    send_same(lambda: out_block(c, x), core_dev, lambda: core_at[2])

    @pl.when(s == 0)
    def _():
        xf[0] = jnp.zeros((full, halo), bf16)
        next_in[...] = jnp.zeros(next_in.shape, bf16)

    @pl.when(s == n_seq - 1)
    def _():
        past0_in[...] = jnp.zeros(past0_in.shape, bf16)
        edge_in[...] = jnp.zeros(edge_in.shape, bf16)

    stats[...] = jnp.zeros(stats.shape, f32)
    length = lengths_ref[c]

    def valid_at(start, size):
        at = s * span + start + lax.broadcasted_iota(jnp.int32, (1, size), 1)
        return jnp.where(at < length, 1.0, 0.0).astype(f32)

    def cast_cotangents(step, carry):
        at = cols_at(step * TILE, TILE)
        valid = valid_at(step * TILE, TILE)
        dproj[step, own_rows, :] = (cot_a[:, at] * valid * root_half).astype(bf16)
        dproj[step, rows_at(full + x * local, local), :] = (cot_b[:, at] * valid).astype(bf16)
        return carry

    tiles = span // TILE
    got_cot_a.wait()
    got_cot_b.wait()
    lax.fori_loop(0, tiles, cast_cotangents, None)
    cot_at = take("recv", 2 * tiles)

    def cot_piece(tile, part, block):
        return dproj.at[tile, rows_at(part * full + block * local, local)]

    for tile in range(tiles):
        for part in range(2):
            send_same(
                functools.partial(cot_piece, tile, part, x),
                mp_dev,
                lambda tile=tile, part=part: cot_at + tile * 2 + part,
            )

    def turn_conv(layer, block, first, rows):
        wct[layer, rows_at(block * width, width), cols_at(first, rows)] = wc[
            layer, block, rows_at(first, rows), :
        ].T

    def turn_rest(layer, block):
        values = wc[layer, block, 2 * full : 2 * full + 16, :].astype(f32)
        mark_row = lax.broadcasted_iota(jnp.int32, values.shape, 0)
        picked = jnp.sum(jnp.where(mark_row == c, values, 0.0), axis=0, keepdims=True)
        et[layer, rows_at(block * width, width), :] = jnp.broadcast_to(picked, (128, width)).T

        for part, start in enumerate((x * local, full + x * local, ox * local)):
            wot[layer, part * local : (part + 1) * local, cols_at(block * gate_local, gate_local)] = wo[
                layer, rows_at(block * gate_local, gate_local), cols_at(start, local)
            ].T

    def turn_all(layer, block):
        for step in range(2 * full // TILE):
            turn_conv(layer, block, step * TILE, TILE)
        turn_rest(layer, block)

    def spread_first():
        arrive(conv_slice(s, c, ox), conv_at + s)
        for step in range(1, n_z):
            send_same(lambda: conv_slice(s, c, ox), z_dev(step), lambda: conv_at + s)
        send_same(lambda: conv_slice(s, c, ox), y_dev, lambda: conv_at + s)
        send_same(lambda: conv_slice(s, c, ox), core_dev, lambda: conv_core_at + s)
        arrive(emb_part(c, ox), emb_at)
        send_same(lambda: emb_part(c, ox), core_dev, lambda: core_at[3])
        arrive(out_slice(s, c, ox), out_at + s)
        for step in range(1, n_z):
            send_same(lambda: out_slice(s, c, ox), z_dev(step), lambda: out_at + s)
        send_same(lambda: out_slice(s, c, ox), y_dev, lambda: out_at + s)

    def spread_conv():
        for step in range(1, n_z):
            arrive(conv_slice(z_seq(step), c, ox), conv_at + z_seq(step))
            here = functools.partial(lambda step: conv_slice(z_seq(step), c, ox), step)
            send_same(here, y_dev, lambda step=step: conv_at + z_seq(step))
            send_same(here, core_dev, lambda step=step: conv_core_at + z_seq(step))

    def spread_out():
        for step in range(1, n_z):
            arrive(out_slice(z_seq(step), c, ox), out_at + z_seq(step))
            here = functools.partial(lambda step: out_slice(z_seq(step), c, ox), step)
            send_same(here, y_dev, lambda step=step: out_at + z_seq(step))

    def spread_last():
        for step in range(n_z):
            arrive(conv_slice(z_seq(step) + 1 - 2 * y, c, ox), conv_at + z_seq(step) + 1 - 2 * y)
            here = functools.partial(
                lambda step: conv_slice(z_seq(step) + 1 - 2 * y, c, ox), step
            )
            send_same(here, core_dev, lambda step=step: conv_core_at + z_seq(step) + 1 - 2 * y)
        for step in range(n_z):
            arrive(out_slice(z_seq(step) + 1 - 2 * y, c, ox), out_at + z_seq(step) + 1 - 2 * y)
        send_same(lambda: out_block(c, ox), core_dev, lambda: core_at[4])

    def all_from_core():
        for step in range(n_seq):
            arrive(conv_slice(step, oc, ox), conv_core_at + step)
        arrive(emb_part(oc, ox), core_at[3])
        arrive(out_block(oc, ox), core_at[4])

    on(c == 0, spread_first)

    @pl.when(c == 0)
    def _():
        turn_all(0, x)

    arrive(xf.at[chunks, other_rows], x_at[chunks - 1])
    send(
        lambda: xf.at[chunks, other_rows],
        lambda: xf.at[0, other_rows],
        next_dev,
        lambda: halo_at[1],
        has_next,
    )
    on(c == 0, spread_conv)
    arrive(conv_block(oc, x), core_at[0])
    arrive(emb_part(oc, x), core_at[1])
    arrive(out_block(oc, x), core_at[2])

    @pl.when(c == 1)
    def _():
        turn_all(0, x)

    on(c == 0, spread_out)
    on(c == 0, spread_last)

    on(c == 1, all_from_core)
    turn_all(0, ox)

    def fold(values):
        total = jnp.sum(values.reshape(local // 8, 8, TILE), axis=0)
        return sum(total[:, part * 128 : (part + 1) * 128] for part in range(TILE // 128))

    def gated(layer, pre, at):
        halves = []
        for block in range(2):
            base = block * width
            shift = et[layer, base : base + width, :]
            shift = jnp.concatenate([shift] * (TILE // 128), axis=1)
            f = jnp.tanh(pre[base : base + gate_local] + shift[:gate_local])
            q = 0.5 * jnp.tanh(
                0.5 * (pre[base + gate_local : base + width] + shift[gate_local:])
            ) + 0.5
            rows = slice(block * gate_local, (block + 1) * gate_local)
            act_f[layer, rows, at] = f
            act_q[layer, rows, at] = q
            halves.append((f * q).astype(bf16))
            hid[layer, rows, at] = halves[-1]
        return jnp.concatenate(halves, axis=0)

    def forward0(step):
        start = step * TILE
        at = cols_at(start, TILE)
        chunk, inner = start // halo, pl.ds(start % halo, TILE)
        pre = dot(wct[0], jnp.concatenate([xf[chunk, :, inner], xf[chunk + 1, :, inner]], axis=0))
        hidden = gated(0, pre, at)
        valid = valid_at(start, TILE)
        proj = dot(wot[0], hidden)
        branch = proj[0:local]
        res = (xf[chunk + 1, own_rows, inner].astype(f32) + branch) * root_half
        res0[:, at] = res
        in1[own_rows, at] = res.astype(bf16)
        stats[0, 0] += fold(valid * res * res)
        stats[0, 1] += fold(valid * branch * branch)
        res = (xf[chunk + 1, other_rows, inner].astype(f32) + proj[2 * local :]) * root_half
        in1[other_rows, at] = res.astype(bf16)
        total = skip_sum[:, at] + proj[local : 2 * local]
        skip_sum[:, at] = total
        skip_low[0, :, at] = total.astype(bf16)

    late_tiles = (span - halo) // TILE
    got_skip.wait()
    for chunk in range(chunks - 1):
        arrive(xf.at[chunk + 1, other_rows], x_at[chunk])
    on(c == 1, spread_first)
    for step in range(late_tiles, tiles):
        forward0(step)
    in1_at = take("recv")
    next_out[...] = in1[:, span - 128 : span]
    send(
        lambda: next_out,
        lambda: next_in,
        next_dev,
        lambda: in1_at,
        has_next,
    )
    on(c == 1, spread_conv)
    on(c == 1, spread_out)
    arrive(xf.at[0, own_rows], halo_at[0], has_prev)
    arrive(xf.at[0, other_rows], halo_at[1], has_prev)
    for step in range(late_tiles):
        forward0(step)
    on(c == 1, spread_last)

    result_at = [take("recv") for _ in range(3)]
    locals_pending = []

    def give(layer, kind, source, target):
        copy = fetch(source, target.at[c], c == layer)
        locals_pending.append((copy, c == layer))
        send(lambda: source, lambda: target.at[c], core_dev, lambda: result_at[kind], c != layer)

    give(0, 0, in1.at[own_rows], res_ref)
    give(0, 1, skip_low.at[0], skipped_ref)

    turn_all(1, x)
    on(c == 0, all_from_core)
    turn_all(1, ox)

    def forward1(step):
        start = step * TILE
        at = cols_at(start, TILE)
        for base in range(0, full, 256):
            rows = slice(base, base + 256)
            if start == 0:
                wide = jnp.concatenate([next_in[rows, :], in1[rows, 0:TILE]], axis=1).astype(f32)
            else:
                wide = in1[rows, start - 128 : start + TILE].astype(f32)
            past1[base : base + 256, at] = pltpu.roll(wide, 1, 1)[:, 128:].astype(bf16)
        pre = dot(wct[1], jnp.concatenate([past1[:, at], in1[:, at]], axis=0))
        hidden = gated(1, pre, at)
        valid = valid_at(start, TILE)
        proj = dot(wot[1, 0 : 2 * local], hidden)
        branch = proj[0:local]
        res = (res0[:, at] + branch) * root_half
        res_low[:, at] = res.astype(bf16)
        stats[1, 0] += fold(valid * res * res)
        stats[1, 1] += fold(valid * branch * branch)
        total = skip_sum[:, at] + proj[local:]
        skip_low[1, :, at] = total.astype(bf16)

    arrive(next_in, in1_at, has_prev)
    for step in range(tiles):
        forward1(step)
    give(1, 0, res_low, res_ref)
    give(1, 1, skip_low.at[1], skipped_ref)

    def through_gates(layer, dhidden, at):
        for block in range(2):
            rows = slice(block * gate_local, (block + 1) * gate_local)
            f, q = act_f[layer, rows, at], act_q[layer, rows, at]
            d = dhidden[rows] * q
            base = block * width
            dpre[layer, base : base + gate_local, at] = (d * (1.0 - f * f)).astype(bf16)
            dpre[layer, base + gate_local : base + width, at] = (d * f * (1.0 - q)).astype(bf16)

    def backward1(step):
        at = cols_at(step * TILE, TILE)
        through_gates(1, dot(wo[1], dproj[step]), at)
        both = jnp.concatenate([wc[1, block, 0 : 2 * full, :] for block in range(2)], axis=1)
        taps = dot(both, dpre[1, :, at])
        past_grad1[:, at] = taps[0:full]
        grad1[:, at] = taps[full:] + dproj[step, 0:full, :].astype(f32)

    def join1(step):
        start = step * TILE
        at = cols_at(start, TILE)
        for base in range(0, full, 256):
            rows = slice(base, base + 256)
            wide = past_grad1[rows, cols_at(start, TILE + 128)]
            total = grad1[rows, at] + pltpu.roll(wide, TILE + 127, 1)[:, 0:TILE]
            grad1[rows, at] = total
            dres0[rows, at] = (root_half * total).astype(bf16)
        own = grad1[own_rows, at]
        grad1_low[:, at] = own.astype(bf16)
        grad0[:, at] = root_half * own

    def backward0(step):
        start = step * TILE
        at = cols_at(start, TILE)
        dhidden = dot(wo[0], jnp.concatenate([dres0[:, at], dproj[step, full:, :]], axis=0))
        through_gates(0, dhidden, at)
        own = [
            jnp.concatenate([wc[0, block, rows, :] for block in range(2)], axis=1)
            for rows in (own_rows, rows_at(full + x * local, local))
        ]
        taps = dot(jnp.concatenate(own, axis=0), dpre[0, :, at])
        grad0[:, at] += taps[local:]
        return taps[0:local]

    edge_at, past0_at = take("recv"), take("recv")
    early_tiles = halo // TILE

    for step in range(tiles):
        for part in range(2):
            arrive(cot_piece(step, part, ox), cot_at + step * 2 + part)
        tile = step - (tiles - early_tiles)
        if tile >= 0:
            join1(tile)
        backward1(step)
        if tile >= 0:
            past0_out[:, cols_at(tile * TILE, TILE)] = backward0(tile).astype(bf16)
        if step == 0:
            edge_out[...] = past_grad1[:, 0:128].astype(bf16)
            send(lambda: edge_out, lambda: edge_in, prev_dev, lambda: edge_at, has_prev)
    send(lambda: past0_out, lambda: past0_in, prev_dev, lambda: past0_at, has_prev)

    total_rows = 3 * full
    unit_rows = total_rows // UNITS
    unit_core_at = [take("recv") for _ in range(UNITS)]
    down_at = [[take("recv") for _ in range(depth)] for _ in range(UNITS)]
    up_at = [[take("recv") for _ in range(depth)] for _ in range(UNITS)]
    small_at = [take("recv") for _ in range(2 + depth)]
    stored_at = take("local", UNITS + 1)

    def to_core(layer, first, size):
        for unit in range(first // unit_rows, (first + size) // unit_rows):
            rows = pl.ds(unit * unit_rows, unit_rows)
            send(
                lambda rows=rows: acc.at[layer, rows],
                lambda rows=rows: from_core.at[rows],
                core_dev,
                lambda unit=unit: unit_core_at[unit],
                c != layer,
            )

    def unit_conv(layer, past, now):
        taps = jnp.concatenate([past, now, jnp.ones((16, span), bf16)], axis=0)
        product = dot_last(taps, dpre[layer, rows_at(x * width, width), :])
        acc[layer, 0 : 2 * full, :] = product[0 : 2 * full].astype(bf16)
        sums = product[2 * full : 2 * full + 8]
        mark = lax.broadcasted_iota(jnp.int32, sums.shape, 0)
        small[layer, 0:8, :] = jnp.where(mark == c, sums, 0.0)
        small[layer, 8:16, :] = jnp.zeros((8, width), f32)
        small[layer, 8:16, 0:128] = stats[layer, 0]
        small[layer, 8:16, 128:256] = stats[layer, 1]
        to_core(layer, 0, 2 * full)
        send(
            lambda: small.at[layer],
            lambda: small_in.at[0],
            core_dev,
            lambda: small_at[0],
            c != layer,
        )

    def unit_out(layer, parts):
        hidden = hid[layer, rows_at(x * gate_local, gate_local), :]
        product = dot_last(jnp.concatenate(parts, axis=0), hidden)
        for part in range(2):
            acc[layer, pl.ds(2 * full, full), pl.ds(part * gate_local, gate_local)] = product[
                part * full : (part + 1) * full
            ].astype(bf16)
        to_core(layer, 2 * full, full)

    n_stages = 2 * depth + 1

    def order(unit):
        ways = list(range(depth))
        return [1, 0, *ways[2:]] if unit == Z_FIRST and depth > 1 else ways

    def kept(unit, level, flip=False):
        start, size = unit * unit_rows, unit_rows
        for step in range(level):
            size //= 2
            bit = bits[order(unit)[step]]
            if flip and step == level - 1:
                bit = 1 - bit
            start = start + bit * size
        return rows_at(start, size)

    def landing(unit, level):
        size = unit_rows >> level
        return pl.ds(unit * unit_rows + unit_rows - 2 * size, size)

    def unit_stage(layer, unit, stage):
        ways = order(unit)
        if stage <= depth:
            here = kept(unit, stage)
            if stage == 0:
                arrive(from_core.at[here], unit_core_at[unit])
                other = from_core[here, :]
            else:
                place = landing(unit, stage)
                arrive(down.at[place], down_at[unit][stage - 1])
                other = down[place, :]
            total = (acc[layer, here, :].astype(f32) + other.astype(f32)).astype(bf16)
            if stage < depth:
                acc[layer, here, :] = total
                send(
                    lambda: acc.at[layer, kept(unit, stage + 1, True)],
                    lambda: down.at[landing(unit, stage + 1)],
                    pair_devs[ways[stage]],
                    lambda: down_at[unit][stage],
                )
                return
            final[here, :] = total
        if stage > depth:
            level = 2 * depth + 1 - stage
            arrive(final.at[kept(unit, level, True)], up_at[unit][level - 1])
        level = 2 * depth - stage
        if level > 0:
            send_same(
                lambda: final.at[kept(unit, level)],
                pair_devs[ways[level - 1]],
                lambda: up_at[unit][level - 1],
            )
        else:
            here = pl.ds(unit * unit_rows, unit_rows)
            pltpu.make_async_copy(
                final.at[here], weight_ref.at[here], local_sem.at[stored_at + unit]
            ).start()

    def small_stage(layer, stage):
        names = [core_dev, mp_dev, *pair_devs]
        arrive(small_in.at[stage], small_at[stage])
        if stage == 0:
            small_sum[0] = small[layer] + small_in[0]
        else:
            sums = small_sum[stage - 1, 0:8, :]
            small_sum[stage, 0:8, :] = sums if stage == 1 else sums + small_in[stage, 0:8, :]
            small_sum[stage, 8:16, :] = small_sum[stage - 1, 8:16, :] + small_in[stage, 8:16, :]
        if stage < len(names) - 1:
            send(
                lambda: small_sum.at[stage],
                lambda: small_in.at[stage + 1],
                names[stage + 1],
                lambda: small_at[stage + 1],
            )
        else:
            pltpu.make_async_copy(
                small_sum.at[stage], small_ref, local_sem.at[stored_at + UNITS]
            ).start()

    def in_order_of_arrival(layer, first_stage, units):
        ready = [(float(at), at, unit, first_stage) for at, unit in enumerate(units)]
        free = [0.0] * depth
        clock, small_next = 0.0, 0
        while ready:
            ready.sort()
            at, rank, unit, stage = ready.pop(0)
            unit_stage(layer, unit, stage)
            clock = max(clock, at) + 0.25
            if stage < n_stages - 1:
                way = order(unit)[min(stage, 2 * depth - 1 - stage)]
                level = min(stage, 2 * depth - 1 - stage)
                free[way] = max(free[way], clock) + 3.0 / 2**level * (2 if way == 2 else 1)
                ready.append((free[way] + 1.0, rank, unit, stage + 1))
            if stage == n_stages - 1 or stage == 2:
                if small_next < 2 + depth:
                    small_stage(layer, small_next)
                    small_next += 1
        for stage in range(small_next, 2 + depth):
            small_stage(layer, stage)

    unit_order = [4, 5, 0, 1, 2, 3]

    def all_times(first):
        rows = slice(first, first + full)
        return jnp.concatenate([dproj[tile, rows, :] for tile in range(tiles)], axis=1)

    unit_out(1, [all_times(0), all_times(full)])
    unit_conv(1, past1[...], in1[...])

    arrive(edge_in, edge_at, has_next)
    past_grad1[:, span : span + 128] = edge_in[...].astype(f32)

    def start_sums(layer):
        for unit in unit_order:
            unit_stage(layer, unit, 0)

    for step in range(early_tiles, tiles):
        join1(step)
    for step in range(early_tiles, tiles):
        grad0[:, cols_at(step * TILE - halo, TILE)] += backward0(step)
        if step == early_tiles:
            on(c == 1, lambda: start_sums(1))
    give(1, 2, grad1_low, grad_ref)
    unit_out(0, [dres0[...], all_times(full)])
    unit_conv(
        0,
        jnp.concatenate([xf[chunk] for chunk in range(chunks)], axis=1),
        jnp.concatenate([xf[chunk + 1] for chunk in range(chunks)], axis=1),
    )

    arrive(past0_in, past0_at, has_next)

    def join0(step, carry):
        at = cols_at(step * TILE, TILE)
        grad0_low[:, at] = grad0[:, at].astype(bf16)
        return carry

    lax.fori_loop(0, (span - halo) // TILE, join0, None)

    def join0_late(step, carry):
        at = cols_at(step * TILE + span - halo, TILE)
        grad0_low[:, at] = (
            grad0[:, at] + past0_in[:, cols_at(step * TILE, TILE)].astype(f32)
        ).astype(bf16)
        return carry

    lax.fori_loop(0, halo // TILE, join0_late, None)
    give(0, 2, grad0_low, grad_ref)

    on(c == 0, lambda: in_order_of_arrival(0, 0, unit_order))
    on(c == 1, lambda: in_order_of_arrival(1, 1, unit_order))
    for unit in range(UNITS):
        here = pl.ds(unit * unit_rows, unit_rows)
        pltpu.make_async_copy(
            final.at[here], weight_ref.at[here], local_sem.at[stored_at + unit]
        ).wait()
    pltpu.make_async_copy(
        small_sum.at[1 + depth], small_ref, local_sem.at[stored_at + UNITS]
    ).wait()
    for kind, target in enumerate((res_ref, skipped_ref, grad_ref)):
        arrive(target.at[oc], result_at[kind])
    for copy, cond in locals_pending:
        when(cond, copy.wait)
    for wait, cond in pending:
        when(cond, wait)
    assert counts["send"] <= send_sem.shape[0], counts
    assert counts["recv"] <= recv_sem.shape[0], counts
    assert counts["local"] <= local_sem.shape[0], counts


def run_layers(
    x_in, skip_in, cot_res, cot_skip, lengths, speakers, conv_view, out_weight, table, n_seq
):
    micro, local, span = x_in.shape
    full = out_weight.shape[1] // 2
    gate_local = out_weight.shape[0]
    gates = 2 * gate_local
    bf16, f32 = jnp.bfloat16, jnp.float32
    halo = FIRST_DILATION
    rows = 3 * full
    depth = (n_seq // 2).bit_length()
    width = 2 * gate_local
    any_spec = pl.BlockSpec(memory_space=pl.ANY)
    scratch = [
        (conv_view.shape, f32),
        (out_weight.shape, f32),
        (table.shape, f32),
        ((span // halo + 1, full, halo), bf16),
        ((2, 2, 2 * full + 16, width), bf16),
        ((2, 2 * width, 2 * full), bf16),
        ((2, gates, 2 * full), bf16),
        ((2, 3 * local, gates), bf16),
        ((2, 2 * width, 128), f32),
        ((full, span), bf16),
        ((full, 128), bf16),
        ((full, 128), bf16),
        ((full, span), bf16),
        ((2, gates, span), f32),
        ((2, gates, span), f32),
        ((2, gates, span), bf16),
        ((span // TILE, 2 * full, TILE), bf16),
        ((full, span), bf16),
        ((2, 2 * width, span), bf16),
        ((full, span), f32),
        ((full, span + 128), f32),
        ((full, 128), bf16),
        ((full, 128), bf16),
        ((local, span), f32),
        ((local, span), f32),
        ((local, span), f32),
        ((local, span), f32),
        ((2, local, span), bf16),
        ((local, span), bf16),
        ((local, span), bf16),
        ((local, span), f32),
        ((local, halo), bf16),
        ((local, halo), bf16),
        ((local, span), bf16),
        ((2, 2, 8, 128), f32),
        ((2, rows, width), bf16),
        ((rows, width), bf16),
        ((rows, width), bf16),
        ((rows, width), bf16),
        ((2, 16, width), f32),
        ((2 + depth, 16, width), f32),
        ((2 + depth, 16, width), f32),
    ]
    result = jax.ShapeDtypeStruct((micro, local, span), bf16)
    return pl.pallas_call(
        functools.partial(layers_kernel, (full, local, gates, span, n_seq)),
        out_shape=(
            result,
            result,
            result,
            jax.ShapeDtypeStruct((rows, width), bf16),
            jax.ShapeDtypeStruct((16, width), f32),
        ),
        in_specs=[any_spec] * 4 + [pl.BlockSpec(memory_space=pltpu.SMEM)] * 2 + [any_spec] * 3,
        out_specs=[any_spec] * 5,
        scratch_shapes=[pltpu.VMEM(shape, kind) for shape, kind in scratch]
        + [
            pltpu.SemaphoreType.DMA((224,)),
            pltpu.SemaphoreType.DMA((144,)),
            pltpu.SemaphoreType.DMA((32,)),
        ],
        compiler_params=pltpu.CompilerParams(
            collective_id=0, has_side_effects=True, vmem_limit_bytes=62 * 1024 * 1024
        ),
        cost_estimate=pl.CostEstimate(
            flops=14_000_000_000, bytes_accessed=20_000_000, transcendentals=2_000_000
        ),
    )(x_in, skip_in, cot_res, cot_skip, lengths, speakers, conv_view, out_weight, table)


def lane_view(value):
    _, taps, full, halves, gate_local = value.shape
    blocks = gate_local // 128
    value = value.reshape(taps * full, halves, blocks, 128).transpose(0, 2, 1, 3)
    return value.reshape(taps * full * halves * blocks, 128)


def lane_back(value, shape):
    _, taps, full, halves, gate_local = shape
    blocks = gate_local // 128
    value = value.reshape(taps * full, blocks, halves, 128).transpose(0, 2, 1, 3)
    return value.reshape(shape)


def update_kernel(
    full,
    lengths_ref,
    speakers_ref,
    small_ref,
    conv_grad_in,
    out_grad_in,
    conv_w,
    conv_m,
    conv_v,
    out_w,
    out_m,
    out_v,
    table_w,
    table_m,
    table_v,
    res_in,
    skip_in,
    grad_in,
    res_out,
    skip_out,
    grad_out,
    rms_out,
    conv_g,
    conv_w_new,
    conv_m_new,
    conv_v_new,
    out_g,
    out_w_new,
    out_m_new,
    out_v_new,
    table_g,
    table_w_new,
    table_m_new,
    table_v_new,
):
    f32 = jnp.float32

    def update(gradient, weight, moment, second, rate, targets):
        new = adamw(weight[...], moment[...], second[...], gradient, rate)
        for target, value in zip(targets, new):
            target[...] = value

    for source, target in ((res_in, res_out), (skip_in, skip_out), (grad_in, grad_out)):
        target[...] = source[...].astype(f32)

    taps, width = conv_grad_in.shape
    blocks = width // 128
    for block in range(blocks):
        half, lane = block // (blocks // 2), block % (blocks // 2)
        conv_g[pl.ds(lane * 2 + half, taps, stride=blocks), :] = conv_grad_in[
            :, block * 128 : (block + 1) * 128
        ].astype(f32)
    update(conv_g[...], conv_w, conv_m, conv_v, 0.03, (conv_w_new, conv_m_new, conv_v_new))

    out_g[...] = out_grad_in[...].astype(f32).T
    update(out_g[...], out_w, out_m, out_v, 0.1, (out_w_new, out_m_new, out_v_new))

    half = width // 2
    row = lax.broadcasted_iota(jnp.int32, table_w.shape, 0) + pl.program_id(0) * table_w.shape[0]
    total = jnp.zeros(table_w.shape, f32)
    for micro in range(2):
        sums = jnp.concatenate(
            [small_ref[micro : micro + 1, 0:half], small_ref[micro : micro + 1, half:]], axis=0
        )
        total = total + jnp.where(row == speakers_ref[micro], sums[None], 0.0)
    table_g[...] = total
    update(total, table_w, table_m, table_v, 0.3, (table_w_new, table_m_new, table_v_new))

    @pl.when(pl.program_id(0) == 0)
    def _():
        counted = (lengths_ref[0] + lengths_ref[1]).astype(f32) * full
        squares = [
            jnp.sum(small_ref[8:16, part * 128 : (part + 1) * 128], axis=(0, 1), keepdims=True)
            for part in range(2)
        ]
        at = lax.broadcasted_iota(jnp.int32, (1, 2), 1)
        rms_out[...] = jnp.sqrt(jnp.where(at == 0, squares[0], squares[1]) / counted)


def run_update(lengths, speakers, small, weights, conv_parts, out_parts, table_parts, results):
    steps = 8
    width = weights.shape[1]
    gate_local, full = out_parts[0].shape[0], out_parts[0].shape[1] // 2
    f32 = jnp.float32

    def rows(value, axis=0):
        shape = list(value.shape)
        shape[axis] = pl.cdiv(shape[axis], steps)
        return pl.BlockSpec(tuple(shape), lambda i: tuple(i if at == axis else 0 for at in range(len(shape))))

    def whole(shape):
        return pl.BlockSpec(tuple(shape), lambda i: (0,) * len(shape))

    conv_block, out_block = 2 * full // steps, 2 * full // steps
    out_first = 2 * full // out_block
    smem = pl.BlockSpec(memory_space=pltpu.SMEM)
    like = [jax.ShapeDtypeStruct(value.shape, f32) for value in (results[0], conv_parts[0], out_parts[0], table_parts[0])]
    specs = [rows(results[0], 1), rows(conv_parts[0]), rows(out_parts[0], 1), rows(table_parts[0])]
    return pl.pallas_call(
        functools.partial(update_kernel, full),
        grid=(steps,),
        out_shape=(
            *[like[0]] * 3,
            jax.ShapeDtypeStruct((1, 2), f32),
            *[like[1]] * 4,
            *[like[2]] * 4,
            *[like[3]] * 4,
        ),
        in_specs=[
            smem,
            smem,
            whole(small.shape),
            pl.BlockSpec((conv_block, width), lambda i: (i, 0)),
            pl.BlockSpec(
                (out_block, gate_local),
                lambda i: (out_first + i % (steps // 2), i // (steps // 2)),
            ),
            *[specs[1]] * 3,
            *[specs[2]] * 3,
            *[specs[3]] * 3,
            *[specs[0]] * 3,
        ],
        out_specs=(
            *[specs[0]] * 3,
            whole((1, 2)),
            *[specs[1]] * 4,
            *[specs[2]] * 4,
            *[specs[3]] * 4,
        ),
        compiler_params=pltpu.CompilerParams(
            dimension_semantics=("arbitrary",), vmem_limit_bytes=62 * 1024 * 1024
        ),
        cost_estimate=pl.CostEstimate(
            flops=20_000_000, bytes_accessed=32_000_000, transcendentals=1_000_000
        ),
    )(
        lengths,
        speakers,
        small,
        weights,
        weights,
        *conv_parts,
        *out_parts,
        *table_parts,
        *results,
    )


def fast_shards(
    n_seq,
    x_in,
    skip_in,
    cot_res,
    cot_skip,
    lengths,
    speakers,
    conv_weight,
    conv_m,
    conv_v,
    out_weight,
    out_m,
    out_v,
    speaker_table,
    table_m,
    table_v,
):
    views = [lane_view(value) for value in (conv_weight, conv_m, conv_v)]
    res, skipped, grads, weights, small = run_layers(
        x_in,
        skip_in,
        cot_res,
        cot_skip,
        lengths,
        speakers,
        views[0],
        out_weight[0],
        speaker_table[0],
        n_seq,
    )
    results = run_update(
        lengths,
        speakers,
        small,
        weights,
        views,
        [out_weight[0], out_m[0], out_v[0]],
        [speaker_table[0], table_m[0], table_v[0]],
        [res, skipped, grads],
    )
    wide, rms_out = results[0:3], results[3]
    conv_parts = [lane_back(value, conv_weight.shape) for value in results[4:8]]
    return (
        *[value[None] for value in wide],
        rms_out,
        *conv_parts,
        *[value[None] for value in results[8:12]],
        *[value[None] for value in results[12:16]],
    )


def shards(
    x_in,
    skip_in,
    cot_res,
    cot_skip,
    lengths,
    speakers,
    conv_weight,
    conv_m,
    conv_v,
    out_weight,
    out_m,
    out_v,
    speaker_table,
    table_m,
    table_v,
):
    micro_count, residual_local, block_length_rows = x_in.shape
    leading_section = lax.axis_index("section") == 0
    seq_index = lax.axis_index("seq")
    dilation_factor = jnp.where(leading_section, FIRST_DILATION, 1).astype(jnp.int32)
    conv_low = conv_weight[0].astype(jnp.bfloat16)
    full_res = conv_low.shape[1]
    gate_dev = conv_low.shape[3]
    speaker_rows = speaker_table.shape[1]
    conv_matrix = conv_low.reshape(2 * full_res, 2 * gate_dev)
    output_low = out_weight[0].astype(jnp.bfloat16)
    table_low = speaker_table[0].astype(jnp.bfloat16).reshape(speaker_rows, 2 * gate_dev)
    positions = seq_index * block_length_rows + jnp.arange(block_length_rows)
    contract_first = (((0,), (0,)), ((), ()))
    contract_last = (((1,), (1,)), ((), ()))
    recv_resid = jnp.zeros((residual_local, block_length_rows), jnp.float32)
    recv_skip = jnp.zeros((residual_local, block_length_rows), jnp.float32)
    kept_list = []
    resid_list = []
    skip_list = []
    square_res = jnp.float32(0.0)
    square_branch = jnp.float32(0.0)
    counted = jnp.float32(0.0)
    for tick_num in range(micro_count + 1):
        index_zero = min(tick_num, micro_count - 1)
        index_one = max(tick_num - 1, 0)
        batch_idx = jnp.where(leading_section, index_zero, index_one)
        is_live = jnp.where(leading_section, tick_num < micro_count, tick_num >= 1).astype(
            jnp.float32
        )
        residual_stream = jnp.where(
            leading_section, x_in[index_zero].astype(jnp.float32), recv_resid
        )
        skip_accumulated = jnp.where(leading_section, skip_in[index_zero], recv_skip)
        onehot = (jnp.arange(speaker_rows) == speakers[batch_idx]).astype(jnp.bfloat16)
        input_signal = residual_stream.astype(jnp.bfloat16)
        preceding_state = passed_along(
            input_signal[:, block_length_rows - FIRST_DILATION :], "seq", 1
        )
        joined_taps = jnp.concatenate([preceding_state, input_signal], axis=1)
        delayed_tap = lax.dynamic_slice_in_dim(
            joined_taps, FIRST_DILATION - dilation_factor, block_length_rows, 1
        )
        tap_rows = jnp.stack([delayed_tap, input_signal], axis=0)
        forward_tap_full = lax.all_gather(tap_rows, "mp", axis=1, tiled=True).reshape(
            2 * full_res, block_length_rows
        )
        embedding = jnp.dot(onehot, table_low, preferred_element_type=jnp.float32)
        forward_preact = (
            lax.dot_general(
                conv_matrix, forward_tap_full, contract_first, preferred_element_type=jnp.float32
            )
            + embedding[:, None]
        )
        hidden = (
            jnp.tanh(forward_preact[:gate_dev]) * jax.nn.sigmoid(forward_preact[gate_dev:])
        ).astype(jnp.bfloat16)
        partial_sums = lax.dot_general(
            output_low, hidden, contract_first, preferred_element_type=jnp.float32
        ).reshape(2, full_res, block_length_rows)
        projected = lax.psum_scatter(partial_sums, "mp", scatter_dimension=1, tiled=True)
        branch = projected[0]
        new_resid = (residual_stream + branch) * root_half
        new_skip = skip_accumulated + projected[1]
        new_resid, new_skip, branch, kept_data = (
            new_resid,
            new_skip,
            branch,
            (forward_tap_full, forward_preact, hidden),
        )
        valid_rows = (positions < lengths[batch_idx]).astype(jnp.float32)[None, :] * is_live
        square_res = square_res + jnp.sum(valid_rows * new_resid * new_resid)
        square_branch = square_branch + jnp.sum(valid_rows * branch * branch)
        counted = counted + jnp.sum(valid_rows) * residual_local
        kept_list.append(kept_data)
        resid_list.append(new_resid)
        skip_list.append(new_skip)
        if tick_num < micro_count:
            recv_resid, recv_skip = passed_along((new_resid, new_skip), "section", 1)
    square_res, square_branch, counted = lax.psum(
        (square_res, square_branch, counted), ("seq", "mp")
    )
    rms_out = jnp.stack([jnp.sqrt(square_res / counted), jnp.sqrt(square_branch / counted)])[None]
    res_out = jnp.stack(
        [
            jnp.where(leading_section, resid_list[m_idx], resid_list[m_idx + 1])
            for m_idx in range(micro_count)
        ]
    )[None]
    skip_out = jnp.stack(
        [
            jnp.where(leading_section, skip_list[m_idx], skip_list[m_idx + 1])
            for m_idx in range(micro_count)
        ]
    )[None]
    conv_acc = jnp.zeros((2 * full_res, 2 * gate_dev), jnp.float32)
    table_acc = jnp.zeros((speaker_rows, 2 * gate_dev), jnp.float32)
    out_acc = jnp.zeros((gate_dev, 2 * full_res), jnp.float32)
    recv_grad = jnp.zeros((residual_local, block_length_rows), jnp.float32)
    input_grads = []
    for tick_num in range(micro_count + 1):
        index_one = min(tick_num, micro_count - 1)
        index_zero = max(tick_num - 1, 0)
        batch_idx = jnp.where(leading_section, index_zero, index_one)
        is_live = jnp.where(leading_section, tick_num >= 1, tick_num < micro_count).astype(
            jnp.float32
        )
        valid_rows = (positions < lengths[batch_idx]).astype(jnp.float32)[None, :] * is_live
        onehot = (jnp.arange(speaker_rows) == speakers[batch_idx]).astype(jnp.bfloat16)
        kept_data = jax.tree.map(
            lambda zero_side, one_side: jnp.where(leading_section, zero_side, one_side),
            kept_list[index_zero],
            kept_list[index_one + 1],
        )
        skip_grad = (
            jnp.where(leading_section, cot_skip[index_zero], cot_skip[index_one]) * valid_rows
        )
        resid_grad = jnp.where(
            leading_section, recv_grad * is_live, cot_res[index_one] * valid_rows
        )
        tap_full, preact, hidden_used = kept_data
        proj_grad = jnp.stack([resid_grad * root_half, skip_grad], axis=0).astype(jnp.bfloat16)
        full_grad = lax.all_gather(proj_grad, "mp", axis=1, tiled=True).reshape(
            2 * full_res, block_length_rows
        )
        hidden_grad = jnp.dot(output_low, full_grad, preferred_element_type=jnp.float32)
        weight_term = lax.dot_general(
            hidden_used, full_grad, contract_last, preferred_element_type=jnp.float32
        )
        filter_act = jnp.tanh(preact[:gate_dev])
        gate_act = jax.nn.sigmoid(preact[gate_dev:])
        filter_grad = hidden_grad * gate_act * (1.0 - filter_act * filter_act)
        gate_grad = hidden_grad * filter_act * gate_act * (1.0 - gate_act)
        preact_grad = jnp.concatenate([filter_grad, gate_grad], axis=0).astype(jnp.bfloat16)
        conv_term = lax.dot_general(
            tap_full, preact_grad, contract_last, preferred_element_type=jnp.float32
        )
        column_sums = jnp.sum(preact_grad.astype(jnp.float32), axis=1)
        table_term = onehot.astype(jnp.float32)[:, None] * column_sums[None, :]
        tap_terms = jnp.dot(conv_matrix, preact_grad, preferred_element_type=jnp.float32)
        tap_gradient = lax.psum_scatter(
            tap_terms.reshape(2, full_res, block_length_rows), "mp", scatter_dimension=1, tiled=True
        )
        joined_taps_gradient = lax.dynamic_update_slice_in_dim(
            jnp.zeros((residual_local, FIRST_DILATION + block_length_rows), jnp.float32),
            tap_gradient[0],
            FIRST_DILATION - dilation_factor,
            1,
        )
        border_gradient = passed_along(joined_taps_gradient[:, :FIRST_DILATION], "seq", -1)
        input_gradient_rows = tap_gradient[1] + joined_taps_gradient[:, FIRST_DILATION:]
        input_gradient_rows = input_gradient_rows.at[:, block_length_rows - FIRST_DILATION :].add(
            border_gradient
        )
        resid_back, conv_term, weight_term, table_term = (
            resid_grad * root_half + input_gradient_rows,
            conv_term,
            weight_term,
            table_term,
        )
        conv_acc = conv_acc + conv_term
        out_acc = out_acc + weight_term
        table_acc = table_acc + table_term
        input_grads.append(resid_back)
        if tick_num < micro_count:
            recv_grad = passed_along(resid_back, "section", -1)
    grad_in = jnp.stack(
        [
            jnp.where(leading_section, input_grads[m_idx + 1], input_grads[m_idx])
            for m_idx in range(micro_count)
        ]
    )[None]
    conv_total, out_total, table_total = lax.psum((conv_acc, out_acc, table_acc), "seq")
    conv_grad = conv_total.reshape(conv_weight.shape)
    out_grad = out_total.reshape(out_weight.shape)
    table_grad = table_total.reshape(speaker_table.shape)
    conv_new, conv_m_new, conv_v_new = adamw(conv_weight, conv_m, conv_v, conv_grad, 0.03)
    out_new, out_m_new, out_v_new = adamw(out_weight, out_m, out_v, out_grad, 0.1)
    table_new, table_m_new, table_v_new = adamw(speaker_table, table_m, table_v, table_grad, 0.3)
    return (
        res_out,
        skip_out,
        grad_in,
        rms_out,
        conv_grad,
        conv_new,
        conv_m_new,
        conv_v_new,
        out_grad,
        out_new,
        out_m_new,
        out_v_new,
        table_grad,
        table_new,
        table_m_new,
        table_v_new,
    )


def solution(mesh):
    in_specs = (
        P(None, "mp", "seq"),
        P(None, "mp", "seq"),
        P(None, "mp", "seq"),
        P(None, "mp", "seq"),
        P(),
        P(),
        P("section", None, None, None, "mp"),
        P("section", None, None, None, "mp"),
        P("section", None, None, None, "mp"),
        P("section", "mp", None),
        P("section", "mp", None),
        P("section", "mp", None),
        P("section", None, None, "mp"),
        P("section", None, None, "mp"),
        P("section", None, None, "mp"),
    )
    out_specs = (
        P("section", None, "mp", "seq"),
        P("section", None, "mp", "seq"),
        P("section", None, "mp", "seq"),
        P("section", None),
        P("section", None, None, None, "mp"),
        P("section", None, None, None, "mp"),
        P("section", None, None, None, "mp"),
        P("section", None, None, None, "mp"),
        P("section", "mp", None),
        P("section", "mp", None),
        P("section", "mp", None),
        P("section", "mp", None),
        P("section", None, None, "mp"),
        P("section", None, None, "mp"),
        P("section", None, None, "mp"),
        P("section", None, None, "mp"),
    )
    n_seq = mesh.shape["seq"]
    fits = mesh.shape["mp"] == 2 and n_seq in (4, 8, 16)
    return jax.shard_map(
        functools.partial(fast_shards, n_seq) if fits else shards,
        mesh=mesh,
        in_specs=in_specs,
        out_specs=out_specs,
        check_vma=False,
    )
```

```python
import functools
import math

import jax
import jax.numpy as jnp
from jax import lax
from jax.experimental import pallas as pl
from jax.experimental.pallas import tpu as pltpu
from jax.sharding import PartitionSpec as P

FIRST_DILATION = 512
STEP = 10
MESH = pl.DeviceIdType.MESH
TILE = 256
UNITS = 3
Z_FIRST = 1

beta_one = 0.9
beta_two = 0.999
adam_eps = 1e-08
decay_rate = 0.01
root_half = math.sqrt(0.5)


def passed_along(value, axis, steps):
    count = lax.axis_size(axis)
    first, last = (max(0, -steps), min(count, count - steps))
    return lax.ppermute(value, axis, [(source, source + steps) for source in range(first, last)])


def adamw(weight, moment, second, gradient, step_rate):
    moment_new = beta_one * moment + (1.0 - beta_one) * gradient
    second_new = beta_two * second + (1.0 - beta_two) * gradient * gradient
    corr_one = 1.0 - beta_one**STEP
    corr_two = 1.0 - beta_two**STEP
    update = moment_new / corr_one / (jnp.sqrt(second_new / corr_two) + adam_eps)
    weight_new = weight - step_rate * (update + decay_rate * weight)
    return (weight_new, moment_new, second_new)


def dot(left, right):
    return jnp.dot(left, right, preferred_element_type=jnp.float32)


def dot_last(left, right):
    return lax.dot_general(
        left, right, (((1,), (1,)), ((), ())), preferred_element_type=jnp.float32
    )


def rows_at(start, size):
    return pl.ds(start if isinstance(start, int) else pl.multiple_of(start, 16), size)


def cols_at(start, size):
    return pl.ds(start if isinstance(start, int) else pl.multiple_of(start, 128), size)


def layers_kernel(
    sizes,
    x_ref,
    skip_ref,
    cot_res_ref,
    cot_skip_ref,
    lengths_ref,
    speakers_ref,
    conv_ref,
    out_ref,
    table_ref,
    res_ref,
    skipped_ref,
    grad_ref,
    weight_ref,
    small_ref,
    conv_wide,
    out_wide,
    table_wide,
    xf,
    wc,
    wct,
    wo,
    wot,
    et,
    in1,
    next_out,
    next_in,
    past1,
    act_f,
    act_q,
    hid,
    dproj,
    dres0,
    dpre,
    grad1,
    past_grad1,
    edge_out,
    edge_in,
    res0,
    skip_sum,
    cot_a,
    cot_b,
    skip_low,
    res_low,
    grad1_low,
    grad0,
    past0_out,
    past0_in,
    grad0_low,
    stats,
    acc,
    from_core,
    down,
    final,
    small,
    small_in,
    small_sum,
    send_sem,
    recv_sem,
    local_sem,
):
    full, local, gates, span, n_seq = sizes
    gate_local = gates // 2
    width = 2 * gate_local
    halo = FIRST_DILATION
    n_z = n_seq // 2
    c = lax.axis_index("section")
    s = lax.axis_index("seq")
    x = lax.axis_index("mp")
    z, y = s // 2, s % 2
    oc, ox = 1 - c, 1 - x
    bf16, f32 = jnp.bfloat16, jnp.float32
    counts = {"send": 0, "recv": 0, "local": 0}
    pending = []
    inside = [None]

    def take(kind, amount=1):
        counts[kind] += amount
        return counts[kind] - amount

    def when(cond, action):
        if cond is None:
            action()
        else:
            pl.when(cond)(action)

    def on(cond, action):
        inside[0] = cond
        pl.when(cond)(lambda: action())
        inside[0] = None

    def send(source, target, device, recv_at, cond=None):
        at = take("send")

        def make():
            return pltpu.make_async_remote_copy(
                src_ref=source(),
                dst_ref=target(),
                send_sem=send_sem.at[at],
                recv_sem=recv_sem.at[recv_at()],
                device_id=device(),
                device_id_type=MESH,
            )

        when(cond, lambda: make().start())
        pending.append((lambda: make().wait_send(), inside[0] if cond is None else cond))

    def arrive(target, recv_at, cond=None):
        when(
            cond,
            lambda: pltpu.make_async_remote_copy(
                src_ref=target,
                dst_ref=target,
                send_sem=send_sem.at[0],
                recv_sem=recv_sem.at[recv_at],
                device_id={"section": oc},
                device_id_type=MESH,
            ).wait_recv(),
        )

    def fetch(source, target, cond=None):
        copy = pltpu.make_async_copy(source, target, local_sem.at[take("local")])
        when(cond, copy.start)
        return copy

    def to(axis, index):
        return lambda: {axis: index()}

    core_dev = to("section", lambda: 1 - c)
    mp_dev = to("mp", lambda: 1 - x)
    y_dev = to("seq", lambda: z * 2 + 1 - y)
    prev_dev, next_dev = to("seq", lambda: s - 1), to("seq", lambda: s + 1)
    has_prev, has_next = s > 0, s < n_seq - 1

    z_seqs = [lax.rem(z + step, n_z) * 2 + y for step in range(n_z)]

    def z_seq(step):
        return z_seqs[step]

    def z_dev(step):
        return to("seq", lambda: z_seq(step))

    bits = [y] + [(z // (1 << bit)) % 2 for bit in range((n_seq // 2).bit_length() - 1)]
    pairs = [z * 2 + 1 - y] + [
        (z + (1 - 2 * bits[bit + 1]) * (1 << bit)) * 2 + y for bit in range(len(bits) - 1)
    ]
    depth = len(bits)
    pair_devs = [to("seq", lambda way=way: pairs[way]) for way in range(depth)]

    barrier = pltpu.get_barrier_semaphore()
    for device in [core_dev, mp_dev, y_dev, *[z_dev(step) for step in range(1, n_z)]]:
        pl.semaphore_signal(barrier, inc=1, device_id=device(), device_id_type=MESH)
    before, after = (y == 0) & (z > 0), (y == 1) & (z < n_z - 1)

    @pl.when(before)
    def _():
        pl.semaphore_signal(barrier, inc=1, device_id=prev_dev(), device_id_type=MESH)

    @pl.when(after)
    def _():
        pl.semaphore_signal(barrier, inc=1, device_id=next_dev(), device_id_type=MESH)

    own_rows, other_rows = rows_at(x * local, local), rows_at(ox * local, local)
    got_conv = fetch(conv_ref, conv_wide)
    got_table = fetch(table_ref, table_wide)
    got_out = fetch(out_ref, out_wide)
    got_cot_a = fetch(cot_res_ref.at[c], cot_a)
    got_cot_b = fetch(cot_skip_ref.at[c], cot_b)
    chunks = span // halo
    got_x = [
        fetch(x_ref.at[c, :, pl.ds(chunk * halo, halo)], xf.at[chunk + 1, own_rows])
        for chunk in range(chunks)
    ]
    got_skip = fetch(skip_ref.at[c], skip_sum)

    def cast_conv(step, carry):
        for block in range(width // 128):
            half, lane = block // (gate_local // 128), block % (gate_local // 128)
            first = step * 256 * (width // 128) + lane * 2 + half
            wc[c, x, rows_at(step * 256, 256), pl.ds(block * 128, 128)] = conv_wide[
                pl.ds(first, 256, stride=width // 128), :
            ].astype(bf16)
        return carry

    got_conv.wait()
    lax.fori_loop(0, 2 * full // 256, cast_conv, None)
    got_table.wait()
    marks = lax.broadcasted_iota(jnp.int32, (16, width), 0)
    emb = jnp.zeros((16, width), f32)
    for micro in range(2):
        rows = table_wide[speakers_ref[micro]]
        row = jnp.concatenate([rows[0:1, :], rows[1:2, :]], axis=1)
        emb = jnp.where(marks == micro, row, emb)
    wc[c, x, 2 * full : 2 * full + 16, :] = emb.astype(bf16)
    got_out.wait()
    wo[c, rows_at(x * gate_local, gate_local), :] = out_wide[...].astype(bf16)

    @pl.when(before | after)
    def _():
        pl.semaphore_wait(barrier, 3 + n_z)

    @pl.when(jnp.logical_not(before | after))
    def _():
        pl.semaphore_wait(barrier, 2 + n_z)

    conv_rows, out_rows = 2 * full // n_seq, gate_local // n_seq
    conv_at, conv_core_at = take("recv", n_seq), take("recv", n_seq)
    out_at, emb_at = take("recv", n_seq), take("recv")

    def conv_slice(index, layer, block):
        return wc.at[layer, block, rows_at(index * conv_rows, conv_rows)]

    def out_slice(index, layer, block):
        return wo.at[layer, rows_at(block * gate_local + index * out_rows, out_rows)]

    def emb_part(layer, block):
        return wc.at[layer, block, 2 * full : 2 * full + 16]

    def conv_block(layer, block):
        return wc.at[layer, block, 0 : 2 * full]

    def out_block(layer, block):
        return wo.at[layer, rows_at(block * gate_local, gate_local)]

    def send_same(ref, device, recv_at, cond=None):
        send(ref, ref, device, recv_at, cond)

    def cross_weights():
        send_same(lambda: conv_slice(s, c, x), mp_dev, lambda: conv_at + s)
        send_same(lambda: emb_part(c, x), mp_dev, lambda: emb_at)
        send_same(lambda: out_slice(s, c, x), mp_dev, lambda: out_at + s)

    on(c == 0, cross_weights)
    x_at = [take("recv") for _ in range(chunks)]
    for copy in got_x:
        copy.wait()
    for chunk in reversed(range(chunks)):
        send_same(
            lambda chunk=chunk: xf.at[chunk + 1, own_rows], mp_dev, lambda chunk=chunk: x_at[chunk]
        )
    on(c == 1, cross_weights)
    halo_at = [take("recv"), take("recv")]
    send(
        lambda: xf.at[chunks, own_rows],
        lambda: xf.at[0, own_rows],
        next_dev,
        lambda: halo_at[0],
        has_next,
    )
    core_at = [take("recv") for _ in range(5)]
    send_same(lambda: conv_block(c, x), core_dev, lambda: core_at[0])
    send_same(lambda: emb_part(c, x), core_dev, lambda: core_at[1])
    send_same(lambda: out_block(c, x), core_dev, lambda: core_at[2])

    @pl.when(s == 0)
    def _():
        xf[0] = jnp.zeros((full, halo), bf16)
        next_in[...] = jnp.zeros(next_in.shape, bf16)

    @pl.when(s == n_seq - 1)
    def _():
        past0_in[...] = jnp.zeros(past0_in.shape, bf16)
        edge_in[...] = jnp.zeros(edge_in.shape, bf16)

    stats[...] = jnp.zeros(stats.shape, f32)
    length = lengths_ref[c]

    def valid_at(start, size):
        at = s * span + start + lax.broadcasted_iota(jnp.int32, (1, size), 1)
        return jnp.where(at < length, 1.0, 0.0).astype(f32)

    def cast_cotangents(step, carry):
        at = cols_at(step * TILE, TILE)
        valid = valid_at(step * TILE, TILE)
        dproj[step, own_rows, :] = (cot_a[:, at] * valid * root_half).astype(bf16)
        dproj[step, rows_at(full + x * local, local), :] = (cot_b[:, at] * valid).astype(bf16)
        return carry

    tiles = span // TILE
    got_cot_a.wait()
    got_cot_b.wait()
    lax.fori_loop(0, tiles, cast_cotangents, None)
    cot_at = take("recv", 2 * tiles)

    def cot_piece(tile, part, block):
        return dproj.at[tile, rows_at(part * full + block * local, local)]

    for tile in range(tiles):
        for part in range(2):
            send_same(
                functools.partial(cot_piece, tile, part, x),
                mp_dev,
                lambda tile=tile, part=part: cot_at + tile * 2 + part,
            )

    def turn_conv(layer, block, first, rows):
        wct[layer, rows_at(block * width, width), cols_at(first, rows)] = wc[
            layer, block, rows_at(first, rows), :
        ].T

    def turn_rest(layer, block):
        values = wc[layer, block, 2 * full : 2 * full + 16, :].astype(f32)
        mark_row = lax.broadcasted_iota(jnp.int32, values.shape, 0)
        picked = jnp.sum(jnp.where(mark_row == c, values, 0.0), axis=0, keepdims=True)
        et[layer, rows_at(block * width, width), :] = jnp.broadcast_to(picked, (128, width)).T

        for part, start in enumerate((x * local, full + x * local, ox * local)):
            wot[layer, part * local : (part + 1) * local, cols_at(block * gate_local, gate_local)] = wo[
                layer, rows_at(block * gate_local, gate_local), cols_at(start, local)
            ].T

    def turn_all(layer, block):
        for step in range(2 * full // TILE):
            turn_conv(layer, block, step * TILE, TILE)
        turn_rest(layer, block)

    def spread_first():
        arrive(conv_slice(s, c, ox), conv_at + s)
        for step in range(1, n_z):
            send_same(lambda: conv_slice(s, c, ox), z_dev(step), lambda: conv_at + s)
        send_same(lambda: conv_slice(s, c, ox), y_dev, lambda: conv_at + s)
        send_same(lambda: conv_slice(s, c, ox), core_dev, lambda: conv_core_at + s)
        arrive(emb_part(c, ox), emb_at)
        send_same(lambda: emb_part(c, ox), core_dev, lambda: core_at[3])
        arrive(out_slice(s, c, ox), out_at + s)
        for step in range(1, n_z):
            send_same(lambda: out_slice(s, c, ox), z_dev(step), lambda: out_at + s)
        send_same(lambda: out_slice(s, c, ox), y_dev, lambda: out_at + s)

    def spread_conv():
        for step in range(1, n_z):
            arrive(conv_slice(z_seq(step), c, ox), conv_at + z_seq(step))
            here = functools.partial(lambda step: conv_slice(z_seq(step), c, ox), step)
            send_same(here, y_dev, lambda step=step: conv_at + z_seq(step))
            send_same(here, core_dev, lambda step=step: conv_core_at + z_seq(step))

    def spread_out():
        for step in range(1, n_z):
            arrive(out_slice(z_seq(step), c, ox), out_at + z_seq(step))
            here = functools.partial(lambda step: out_slice(z_seq(step), c, ox), step)
            send_same(here, y_dev, lambda step=step: out_at + z_seq(step))

    def spread_last():
        for step in range(n_z):
            arrive(conv_slice(z_seq(step) + 1 - 2 * y, c, ox), conv_at + z_seq(step) + 1 - 2 * y)
            here = functools.partial(
                lambda step: conv_slice(z_seq(step) + 1 - 2 * y, c, ox), step
            )
            send_same(here, core_dev, lambda step=step: conv_core_at + z_seq(step) + 1 - 2 * y)
        for step in range(n_z):
            arrive(out_slice(z_seq(step) + 1 - 2 * y, c, ox), out_at + z_seq(step) + 1 - 2 * y)
        send_same(lambda: out_block(c, ox), core_dev, lambda: core_at[4])

    def all_from_core():
        for step in range(n_seq):
            arrive(conv_slice(step, oc, ox), conv_core_at + step)
        arrive(emb_part(oc, ox), core_at[3])
        arrive(out_block(oc, ox), core_at[4])

    on(c == 0, spread_first)

    @pl.when(c == 0)
    def _():
        turn_all(0, x)

    arrive(xf.at[chunks, other_rows], x_at[chunks - 1])
    send(
        lambda: xf.at[chunks, other_rows],
        lambda: xf.at[0, other_rows],
        next_dev,
        lambda: halo_at[1],
        has_next,
    )
    on(c == 0, spread_conv)
    arrive(conv_block(oc, x), core_at[0])
    arrive(emb_part(oc, x), core_at[1])
    arrive(out_block(oc, x), core_at[2])

    @pl.when(c == 1)
    def _():
        turn_all(0, x)

    on(c == 0, spread_out)
    on(c == 0, spread_last)

    on(c == 1, all_from_core)
    turn_all(0, ox)

    def fold(values):
        total = jnp.sum(values.reshape(local // 8, 8, TILE), axis=0)
        return sum(total[:, part * 128 : (part + 1) * 128] for part in range(TILE // 128))

    def gated(layer, pre, at):
        halves = []
        for block in range(2):
            base = block * width
            shift = et[layer, base : base + width, :]
            shift = jnp.concatenate([shift] * (TILE // 128), axis=1)
            f = jnp.tanh(pre[base : base + gate_local] + shift[:gate_local])
            q = 0.5 * jnp.tanh(
                0.5 * (pre[base + gate_local : base + width] + shift[gate_local:])
            ) + 0.5
            rows = slice(block * gate_local, (block + 1) * gate_local)
            act_f[layer, rows, at] = f
            act_q[layer, rows, at] = q
            halves.append((f * q).astype(bf16))
            hid[layer, rows, at] = halves[-1]
        return jnp.concatenate(halves, axis=0)

    def forward0(step):
        start = step * TILE
        at = cols_at(start, TILE)
        chunk, inner = start // halo, pl.ds(start % halo, TILE)
        pre = dot(wct[0], jnp.concatenate([xf[chunk, :, inner], xf[chunk + 1, :, inner]], axis=0))
        hidden = gated(0, pre, at)
        valid = valid_at(start, TILE)
        proj = dot(wot[0], hidden)
        branch = proj[0:local]
        res = (xf[chunk + 1, own_rows, inner].astype(f32) + branch) * root_half
        res0[:, at] = res
        in1[own_rows, at] = res.astype(bf16)
        stats[0, 0] += fold(valid * res * res)
        stats[0, 1] += fold(valid * branch * branch)
        res = (xf[chunk + 1, other_rows, inner].astype(f32) + proj[2 * local :]) * root_half
        in1[other_rows, at] = res.astype(bf16)
        total = skip_sum[:, at] + proj[local : 2 * local]
        skip_sum[:, at] = total
        skip_low[0, :, at] = total.astype(bf16)

    late_tiles = (span - halo) // TILE
    got_skip.wait()
    for chunk in range(chunks - 1):
        arrive(xf.at[chunk + 1, other_rows], x_at[chunk])
    on(c == 1, spread_first)
    for step in range(late_tiles, tiles):
        forward0(step)
    in1_at = take("recv")
    next_out[...] = in1[:, span - 128 : span]
    send(
        lambda: next_out,
        lambda: next_in,
        next_dev,
        lambda: in1_at,
        has_next,
    )
    on(c == 1, spread_conv)
    on(c == 1, spread_out)
    arrive(xf.at[0, own_rows], halo_at[0], has_prev)
    arrive(xf.at[0, other_rows], halo_at[1], has_prev)
    for step in range(late_tiles):
        forward0(step)
    on(c == 1, spread_last)

    result_at = [take("recv") for _ in range(3)]
    locals_pending = []

    def give(layer, kind, source, target):
        copy = fetch(source, target.at[c], c == layer)
        locals_pending.append((copy, c == layer))
        send(lambda: source, lambda: target.at[c], core_dev, lambda: result_at[kind], c != layer)

    give(0, 0, in1.at[own_rows], res_ref)
    give(0, 1, skip_low.at[0], skipped_ref)

    turn_all(1, x)
    on(c == 0, all_from_core)
    turn_all(1, ox)

    def forward1(step):
        start = step * TILE
        at = cols_at(start, TILE)
        for base in range(0, full, 256):
            rows = slice(base, base + 256)
            if start == 0:
                wide = jnp.concatenate([next_in[rows, :], in1[rows, 0:TILE]], axis=1).astype(f32)
            else:
                wide = in1[rows, start - 128 : start + TILE].astype(f32)
            past1[base : base + 256, at] = pltpu.roll(wide, 1, 1)[:, 128:].astype(bf16)
        pre = dot(wct[1], jnp.concatenate([past1[:, at], in1[:, at]], axis=0))
        hidden = gated(1, pre, at)
        valid = valid_at(start, TILE)
        proj = dot(wot[1, 0 : 2 * local], hidden)
        branch = proj[0:local]
        res = (res0[:, at] + branch) * root_half
        res_low[:, at] = res.astype(bf16)
        stats[1, 0] += fold(valid * res * res)
        stats[1, 1] += fold(valid * branch * branch)
        total = skip_sum[:, at] + proj[local:]
        skip_low[1, :, at] = total.astype(bf16)

    arrive(next_in, in1_at, has_prev)
    for step in range(tiles):
        forward1(step)
    give(1, 0, res_low, res_ref)
    give(1, 1, skip_low.at[1], skipped_ref)

    def through_gates(layer, dhidden, at):
        for block in range(2):
            rows = slice(block * gate_local, (block + 1) * gate_local)
            f, q = act_f[layer, rows, at], act_q[layer, rows, at]
            d = dhidden[rows] * q
            base = block * width
            dpre[layer, base : base + gate_local, at] = (d * (1.0 - f * f)).astype(bf16)
            dpre[layer, base + gate_local : base + width, at] = (d * f * (1.0 - q)).astype(bf16)

    def backward1(step):
        at = cols_at(step * TILE, TILE)
        through_gates(1, dot(wo[1], dproj[step]), at)
        both = jnp.concatenate([wc[1, block, 0 : 2 * full, :] for block in range(2)], axis=1)
        taps = dot(both, dpre[1, :, at])
        past_grad1[:, at] = taps[0:full]
        grad1[:, at] = taps[full:] + dproj[step, 0:full, :].astype(f32)

    def join1(step):
        start = step * TILE
        at = cols_at(start, TILE)
        for base in range(0, full, 256):
            rows = slice(base, base + 256)
            wide = past_grad1[rows, cols_at(start, TILE + 128)]
            total = grad1[rows, at] + pltpu.roll(wide, TILE + 127, 1)[:, 0:TILE]
            grad1[rows, at] = total
            dres0[rows, at] = (root_half * total).astype(bf16)
        own = grad1[own_rows, at]
        grad1_low[:, at] = own.astype(bf16)
        grad0[:, at] = root_half * own

    def backward0(step):
        start = step * TILE
        at = cols_at(start, TILE)
        dhidden = dot(wo[0], jnp.concatenate([dres0[:, at], dproj[step, full:, :]], axis=0))
        through_gates(0, dhidden, at)
        own = [
            jnp.concatenate([wc[0, block, rows, :] for block in range(2)], axis=1)
            for rows in (own_rows, rows_at(full + x * local, local))
        ]
        taps = dot(jnp.concatenate(own, axis=0), dpre[0, :, at])
        grad0[:, at] += taps[local:]
        return taps[0:local]

    edge_at, past0_at = take("recv"), take("recv")
    early_tiles = halo // TILE

    for step in range(tiles):
        for part in range(2):
            arrive(cot_piece(step, part, ox), cot_at + step * 2 + part)
        tile = step - (tiles - early_tiles)
        if tile >= 0:
            join1(tile)
        backward1(step)
        if tile >= 0:
            past0_out[:, cols_at(tile * TILE, TILE)] = backward0(tile).astype(bf16)
        if step == 0:
            edge_out[...] = past_grad1[:, 0:128].astype(bf16)
            send(lambda: edge_out, lambda: edge_in, prev_dev, lambda: edge_at, has_prev)
    send(lambda: past0_out, lambda: past0_in, prev_dev, lambda: past0_at, has_prev)

    total_rows = 3 * full
    unit_rows = total_rows // UNITS
    unit_core_at = [take("recv") for _ in range(UNITS)]
    down_at = [[take("recv") for _ in range(depth)] for _ in range(UNITS)]
    up_at = [[take("recv") for _ in range(depth)] for _ in range(UNITS)]
    small_at = [take("recv") for _ in range(2 + depth)]
    stored_at = take("local", UNITS + 1)

    def to_core(layer, first, size):
        for unit in range(first // unit_rows, (first + size) // unit_rows):
            rows = pl.ds(unit * unit_rows, unit_rows)
            send(
                lambda rows=rows: acc.at[layer, rows],
                lambda rows=rows: from_core.at[rows],
                core_dev,
                lambda unit=unit: unit_core_at[unit],
                c != layer,
            )

    def unit_conv(layer, past, now):
        taps = jnp.concatenate([past, now, jnp.ones((16, span), bf16)], axis=0)
        product = dot_last(taps, dpre[layer, rows_at(x * width, width), :])
        acc[layer, 0 : 2 * full, :] = product[0 : 2 * full].astype(bf16)
        sums = product[2 * full : 2 * full + 8]
        mark = lax.broadcasted_iota(jnp.int32, sums.shape, 0)
        small[layer, 0:8, :] = jnp.where(mark == c, sums, 0.0)
        small[layer, 8:16, :] = jnp.zeros((8, width), f32)
        small[layer, 8:16, 0:128] = stats[layer, 0]
        small[layer, 8:16, 128:256] = stats[layer, 1]
        to_core(layer, 0, 2 * full)
        send(
            lambda: small.at[layer],
            lambda: small_in.at[0],
            core_dev,
            lambda: small_at[0],
            c != layer,
        )

    def unit_out(layer, parts):
        hidden = hid[layer, rows_at(x * gate_local, gate_local), :]
        product = dot_last(jnp.concatenate(parts, axis=0), hidden)
        for part in range(2):
            acc[layer, pl.ds(2 * full, full), pl.ds(part * gate_local, gate_local)] = product[
                part * full : (part + 1) * full
            ].astype(bf16)
        to_core(layer, 2 * full, full)

    n_stages = 2 * depth + 1

    def order(unit):
        ways = list(range(depth))
        return [1, 0, *ways[2:]] if unit == Z_FIRST and depth > 1 else ways

    def kept(unit, level, flip=False):
        start, size = unit * unit_rows, unit_rows
        for step in range(level):
            size //= 2
            bit = bits[order(unit)[step]]
            if flip and step == level - 1:
                bit = 1 - bit
            start = start + bit * size
        return rows_at(start, size)

    def landing(unit, level):
        size = unit_rows >> level
        return pl.ds(unit * unit_rows + unit_rows - 2 * size, size)

    def unit_stage(layer, unit, stage):
        ways = order(unit)
        if stage <= depth:
            here = kept(unit, stage)
            if stage == 0:
                arrive(from_core.at[here], unit_core_at[unit])
                other = from_core[here, :]
            else:
                place = landing(unit, stage)
                arrive(down.at[place], down_at[unit][stage - 1])
                other = down[place, :]
            total = (acc[layer, here, :].astype(f32) + other.astype(f32)).astype(bf16)
            if stage < depth:
                acc[layer, here, :] = total
                send(
                    lambda: acc.at[layer, kept(unit, stage + 1, True)],
                    lambda: down.at[landing(unit, stage + 1)],
                    pair_devs[ways[stage]],
                    lambda: down_at[unit][stage],
                )
                return
            final[here, :] = total
        if stage > depth:
            level = 2 * depth + 1 - stage
            arrive(final.at[kept(unit, level, True)], up_at[unit][level - 1])
        level = 2 * depth - stage
        if level > 0:
            send_same(
                lambda: final.at[kept(unit, level)],
                pair_devs[ways[level - 1]],
                lambda: up_at[unit][level - 1],
            )
        else:
            here = pl.ds(unit * unit_rows, unit_rows)
            pltpu.make_async_copy(
                final.at[here], weight_ref.at[here], local_sem.at[stored_at + unit]
            ).start()

    def small_stage(layer, stage):
        names = [core_dev, mp_dev, *pair_devs]
        arrive(small_in.at[stage], small_at[stage])
        if stage == 0:
            small_sum[0] = small[layer] + small_in[0]
        else:
            sums = small_sum[stage - 1, 0:8, :]
            small_sum[stage, 0:8, :] = sums if stage == 1 else sums + small_in[stage, 0:8, :]
            small_sum[stage, 8:16, :] = small_sum[stage - 1, 8:16, :] + small_in[stage, 8:16, :]
        if stage < len(names) - 1:
            send(
                lambda: small_sum.at[stage],
                lambda: small_in.at[stage + 1],
                names[stage + 1],
                lambda: small_at[stage + 1],
            )
        else:
            pltpu.make_async_copy(
                small_sum.at[stage], small_ref, local_sem.at[stored_at + UNITS]
            ).start()

    def in_order_of_arrival(layer, first_stage, units):
        ready = [(float(at), at, unit, first_stage) for at, unit in enumerate(units)]
        free = [0.0] * depth
        clock, small_next = 0.0, 0
        while ready:
            ready.sort()
            at, rank, unit, stage = ready.pop(0)
            unit_stage(layer, unit, stage)
            clock = max(clock, at) + 0.25
            if stage < n_stages - 1:
                way = order(unit)[min(stage, 2 * depth - 1 - stage)]
                level = min(stage, 2 * depth - 1 - stage)
                free[way] = max(free[way], clock) + 3.0 / 2**level * (2 if way == 2 else 1)
                ready.append((free[way] + 1.0, rank, unit, stage + 1))
            if stage == n_stages - 1 or stage == 2:
                if small_next < 2 + depth:
                    small_stage(layer, small_next)
                    small_next += 1
        for stage in range(small_next, 2 + depth):
            small_stage(layer, stage)

    unit_order = [2, 0, 1]

    def all_times(first):
        rows = slice(first, first + full)
        return jnp.concatenate([dproj[tile, rows, :] for tile in range(tiles)], axis=1)

    unit_out(1, [all_times(0), all_times(full)])
    unit_conv(1, past1[...], in1[...])

    arrive(edge_in, edge_at, has_next)
    past_grad1[:, span : span + 128] = edge_in[...].astype(f32)

    def start_sums(layer):
        for unit in unit_order:
            unit_stage(layer, unit, 0)

    for step in range(early_tiles, tiles):
        join1(step)
    for step in range(early_tiles, tiles):
        grad0[:, cols_at(step * TILE - halo, TILE)] += backward0(step)
        if step == early_tiles:
            on(c == 1, lambda: start_sums(1))
    give(1, 2, grad1_low, grad_ref)
    unit_out(0, [dres0[...], all_times(full)])
    unit_conv(
        0,
        jnp.concatenate([xf[chunk] for chunk in range(chunks)], axis=1),
        jnp.concatenate([xf[chunk + 1] for chunk in range(chunks)], axis=1),
    )

    arrive(past0_in, past0_at, has_next)

    def join0(step, carry):
        at = cols_at(step * TILE, TILE)
        grad0_low[:, at] = grad0[:, at].astype(bf16)
        return carry

    lax.fori_loop(0, (span - halo) // TILE, join0, None)

    def join0_late(step, carry):
        at = cols_at(step * TILE + span - halo, TILE)
        grad0_low[:, at] = (
            grad0[:, at] + past0_in[:, cols_at(step * TILE, TILE)].astype(f32)
        ).astype(bf16)
        return carry

    lax.fori_loop(0, halo // TILE, join0_late, None)
    give(0, 2, grad0_low, grad_ref)

    on(c == 0, lambda: start_sums(0))
    for wait, cond in pending:
        when(cond, wait)
    pending.clear()
    on(c == 0, lambda: in_order_of_arrival(0, 1, unit_order))
    on(c == 1, lambda: in_order_of_arrival(1, 1, unit_order))
    for unit in range(UNITS):
        here = pl.ds(unit * unit_rows, unit_rows)
        pltpu.make_async_copy(
            final.at[here], weight_ref.at[here], local_sem.at[stored_at + unit]
        ).wait()
    pltpu.make_async_copy(
        small_sum.at[1 + depth], small_ref, local_sem.at[stored_at + UNITS]
    ).wait()
    for kind, target in enumerate((res_ref, skipped_ref, grad_ref)):
        arrive(target.at[oc], result_at[kind])
    for copy, cond in locals_pending:
        when(cond, copy.wait)
    for wait, cond in pending:
        when(cond, wait)
    assert counts["send"] <= send_sem.shape[0], counts
    assert counts["recv"] <= recv_sem.shape[0], counts
    assert counts["local"] <= local_sem.shape[0], counts


def run_layers(
    x_in, skip_in, cot_res, cot_skip, lengths, speakers, conv_view, out_weight, table, n_seq
):
    micro, local, span = x_in.shape
    full = out_weight.shape[1] // 2
    gate_local = out_weight.shape[0]
    gates = 2 * gate_local
    bf16, f32 = jnp.bfloat16, jnp.float32
    halo = FIRST_DILATION
    rows = 3 * full
    depth = (n_seq // 2).bit_length()
    width = 2 * gate_local
    any_spec = pl.BlockSpec(memory_space=pl.ANY)
    scratch = [
        (conv_view.shape, f32),
        (out_weight.shape, f32),
        (table.shape, f32),
        ((span // halo + 1, full, halo), bf16),
        ((2, 2, 2 * full + 16, width), bf16),
        ((2, 2 * width, 2 * full), bf16),
        ((2, gates, 2 * full), bf16),
        ((2, 3 * local, gates), bf16),
        ((2, 2 * width, 128), f32),
        ((full, span), bf16),
        ((full, 128), bf16),
        ((full, 128), bf16),
        ((full, span), bf16),
        ((2, gates, span), f32),
        ((2, gates, span), f32),
        ((2, gates, span), bf16),
        ((span // TILE, 2 * full, TILE), bf16),
        ((full, span), bf16),
        ((2, 2 * width, span), bf16),
        ((full, span), f32),
        ((full, span + 128), f32),
        ((full, 128), bf16),
        ((full, 128), bf16),
        ((local, span), f32),
        ((local, span), f32),
        ((local, span), f32),
        ((local, span), f32),
        ((2, local, span), bf16),
        ((local, span), bf16),
        ((local, span), bf16),
        ((local, span), f32),
        ((local, halo), bf16),
        ((local, halo), bf16),
        ((local, span), bf16),
        ((2, 2, 8, 128), f32),
        ((2, rows, width), bf16),
        ((rows, width), bf16),
        ((rows, width), bf16),
        ((rows, width), bf16),
        ((2, 16, width), f32),
        ((2 + depth, 16, width), f32),
        ((2 + depth, 16, width), f32),
    ]
    result = jax.ShapeDtypeStruct((micro, local, span), bf16)
    return pl.pallas_call(
        functools.partial(layers_kernel, (full, local, gates, span, n_seq)),
        out_shape=(
            result,
            result,
            result,
            jax.ShapeDtypeStruct((rows, width), bf16),
            jax.ShapeDtypeStruct((16, width), f32),
        ),
        in_specs=[any_spec] * 4 + [pl.BlockSpec(memory_space=pltpu.SMEM)] * 2 + [any_spec] * 3,
        out_specs=[any_spec] * 5,
        scratch_shapes=[pltpu.VMEM(shape, kind) for shape, kind in scratch]
        + [
            pltpu.SemaphoreType.DMA((224,)),
            pltpu.SemaphoreType.DMA((144,)),
            pltpu.SemaphoreType.DMA((32,)),
        ],
        compiler_params=pltpu.CompilerParams(
            collective_id=0, has_side_effects=True, vmem_limit_bytes=62 * 1024 * 1024
        ),
        cost_estimate=pl.CostEstimate(
            flops=14_000_000_000, bytes_accessed=20_000_000, transcendentals=2_000_000
        ),
    )(x_in, skip_in, cot_res, cot_skip, lengths, speakers, conv_view, out_weight, table)


def lane_view(value):
    _, taps, full, halves, gate_local = value.shape
    blocks = gate_local // 128
    value = value.reshape(taps * full, halves, blocks, 128).transpose(0, 2, 1, 3)
    return value.reshape(taps * full * halves * blocks, 128)


def lane_back(value, shape):
    _, taps, full, halves, gate_local = shape
    blocks = gate_local // 128
    value = value.reshape(taps * full, blocks, halves, 128).transpose(0, 2, 1, 3)
    return value.reshape(shape)


def update_kernel(
    full,
    lengths_ref,
    speakers_ref,
    small_ref,
    conv_grad_in,
    out_grad_in,
    conv_w,
    conv_m,
    conv_v,
    out_w,
    out_m,
    out_v,
    table_w,
    table_m,
    table_v,
    res_in,
    skip_in,
    grad_in,
    res_out,
    skip_out,
    grad_out,
    rms_out,
    conv_g,
    conv_w_new,
    conv_m_new,
    conv_v_new,
    out_g,
    out_w_new,
    out_m_new,
    out_v_new,
    table_g,
    table_w_new,
    table_m_new,
    table_v_new,
):
    f32 = jnp.float32

    def update(gradient, weight, moment, second, rate, targets):
        new = adamw(weight[...], moment[...], second[...], gradient, rate)
        for target, value in zip(targets, new):
            target[...] = value

    for source, target in ((res_in, res_out), (skip_in, skip_out), (grad_in, grad_out)):
        target[...] = source[...].astype(f32)

    taps, width = conv_grad_in.shape
    blocks = width // 128
    for block in range(blocks):
        half, lane = block // (blocks // 2), block % (blocks // 2)
        conv_g[pl.ds(lane * 2 + half, taps, stride=blocks), :] = conv_grad_in[
            :, block * 128 : (block + 1) * 128
        ].astype(f32)
    update(conv_g[...], conv_w, conv_m, conv_v, 0.03, (conv_w_new, conv_m_new, conv_v_new))

    out_g[...] = out_grad_in[...].astype(f32).T
    update(out_g[...], out_w, out_m, out_v, 0.1, (out_w_new, out_m_new, out_v_new))

    half = width // 2
    row = lax.broadcasted_iota(jnp.int32, table_w.shape, 0) + pl.program_id(0) * table_w.shape[0]
    total = jnp.zeros(table_w.shape, f32)
    for micro in range(2):
        sums = jnp.concatenate(
            [small_ref[micro : micro + 1, 0:half], small_ref[micro : micro + 1, half:]], axis=0
        )
        total = total + jnp.where(row == speakers_ref[micro], sums[None], 0.0)
    table_g[...] = total
    update(total, table_w, table_m, table_v, 0.3, (table_w_new, table_m_new, table_v_new))

    @pl.when(pl.program_id(0) == 0)
    def _():
        counted = (lengths_ref[0] + lengths_ref[1]).astype(f32) * full
        squares = [
            jnp.sum(small_ref[8:16, part * 128 : (part + 1) * 128], axis=(0, 1), keepdims=True)
            for part in range(2)
        ]
        at = lax.broadcasted_iota(jnp.int32, (1, 2), 1)
        rms_out[...] = jnp.sqrt(jnp.where(at == 0, squares[0], squares[1]) / counted)


def run_update(lengths, speakers, small, weights, conv_parts, out_parts, table_parts, results):
    steps = 8
    width = weights.shape[1]
    gate_local, full = out_parts[0].shape[0], out_parts[0].shape[1] // 2
    f32 = jnp.float32

    def rows(value, axis=0):
        shape = list(value.shape)
        shape[axis] = pl.cdiv(shape[axis], steps)
        return pl.BlockSpec(tuple(shape), lambda i: tuple(i if at == axis else 0 for at in range(len(shape))))

    def whole(shape):
        return pl.BlockSpec(tuple(shape), lambda i: (0,) * len(shape))

    conv_block, out_block = 2 * full // steps, 2 * full // steps
    out_first = 2 * full // out_block
    smem = pl.BlockSpec(memory_space=pltpu.SMEM)
    like = [jax.ShapeDtypeStruct(value.shape, f32) for value in (results[0], conv_parts[0], out_parts[0], table_parts[0])]
    specs = [rows(results[0], 1), rows(conv_parts[0]), rows(out_parts[0], 1), rows(table_parts[0])]
    return pl.pallas_call(
        functools.partial(update_kernel, full),
        grid=(steps,),
        out_shape=(
            *[like[0]] * 3,
            jax.ShapeDtypeStruct((1, 2), f32),
            *[like[1]] * 4,
            *[like[2]] * 4,
            *[like[3]] * 4,
        ),
        in_specs=[
            smem,
            smem,
            whole(small.shape),
            pl.BlockSpec((conv_block, width), lambda i: (i, 0)),
            pl.BlockSpec(
                (out_block, gate_local),
                lambda i: (out_first + i % (steps // 2), i // (steps // 2)),
            ),
            *[specs[1]] * 3,
            *[specs[2]] * 3,
            *[specs[3]] * 3,
            *[specs[0]] * 3,
        ],
        out_specs=(
            *[specs[0]] * 3,
            whole((1, 2)),
            *[specs[1]] * 4,
            *[specs[2]] * 4,
            *[specs[3]] * 4,
        ),
        compiler_params=pltpu.CompilerParams(
            dimension_semantics=("arbitrary",), vmem_limit_bytes=62 * 1024 * 1024
        ),
        cost_estimate=pl.CostEstimate(
            flops=20_000_000, bytes_accessed=32_000_000, transcendentals=1_000_000
        ),
    )(
        lengths,
        speakers,
        small,
        weights,
        weights,
        *conv_parts,
        *out_parts,
        *table_parts,
        *results,
    )


def fast_shards(
    n_seq,
    x_in,
    skip_in,
    cot_res,
    cot_skip,
    lengths,
    speakers,
    conv_weight,
    conv_m,
    conv_v,
    out_weight,
    out_m,
    out_v,
    speaker_table,
    table_m,
    table_v,
):
    views = [lane_view(value) for value in (conv_weight, conv_m, conv_v)]
    res, skipped, grads, weights, small = run_layers(
        x_in,
        skip_in,
        cot_res,
        cot_skip,
        lengths,
        speakers,
        views[0],
        out_weight[0],
        speaker_table[0],
        n_seq,
    )
    results = run_update(
        lengths,
        speakers,
        small,
        weights,
        views,
        [out_weight[0], out_m[0], out_v[0]],
        [speaker_table[0], table_m[0], table_v[0]],
        [res, skipped, grads],
    )
    wide, rms_out = results[0:3], results[3]
    conv_parts = [lane_back(value, conv_weight.shape) for value in results[4:8]]
    return (
        *[value[None] for value in wide],
        rms_out,
        *conv_parts,
        *[value[None] for value in results[8:12]],
        *[value[None] for value in results[12:16]],
    )


def shards(
    x_in,
    skip_in,
    cot_res,
    cot_skip,
    lengths,
    speakers,
    conv_weight,
    conv_m,
    conv_v,
    out_weight,
    out_m,
    out_v,
    speaker_table,
    table_m,
    table_v,
):
    micro_count, residual_local, block_length_rows = x_in.shape
    leading_section = lax.axis_index("section") == 0
    seq_index = lax.axis_index("seq")
    dilation_factor = jnp.where(leading_section, FIRST_DILATION, 1).astype(jnp.int32)
    conv_low = conv_weight[0].astype(jnp.bfloat16)
    full_res = conv_low.shape[1]
    gate_dev = conv_low.shape[3]
    speaker_rows = speaker_table.shape[1]
    conv_matrix = conv_low.reshape(2 * full_res, 2 * gate_dev)
    output_low = out_weight[0].astype(jnp.bfloat16)
    table_low = speaker_table[0].astype(jnp.bfloat16).reshape(speaker_rows, 2 * gate_dev)
    positions = seq_index * block_length_rows + jnp.arange(block_length_rows)
    contract_first = (((0,), (0,)), ((), ()))
    contract_last = (((1,), (1,)), ((), ()))
    recv_resid = jnp.zeros((residual_local, block_length_rows), jnp.float32)
    recv_skip = jnp.zeros((residual_local, block_length_rows), jnp.float32)
    kept_list = []
    resid_list = []
    skip_list = []
    square_res = jnp.float32(0.0)
    square_branch = jnp.float32(0.0)
    counted = jnp.float32(0.0)
    for tick_num in range(micro_count + 1):
        index_zero = min(tick_num, micro_count - 1)
        index_one = max(tick_num - 1, 0)
        batch_idx = jnp.where(leading_section, index_zero, index_one)
        is_live = jnp.where(leading_section, tick_num < micro_count, tick_num >= 1).astype(
            jnp.float32
        )
        residual_stream = jnp.where(
            leading_section, x_in[index_zero].astype(jnp.float32), recv_resid
        )
        skip_accumulated = jnp.where(leading_section, skip_in[index_zero], recv_skip)
        onehot = (jnp.arange(speaker_rows) == speakers[batch_idx]).astype(jnp.bfloat16)
        input_signal = residual_stream.astype(jnp.bfloat16)
        preceding_state = passed_along(
            input_signal[:, block_length_rows - FIRST_DILATION :], "seq", 1
        )
        joined_taps = jnp.concatenate([preceding_state, input_signal], axis=1)
        delayed_tap = lax.dynamic_slice_in_dim(
            joined_taps, FIRST_DILATION - dilation_factor, block_length_rows, 1
        )
        tap_rows = jnp.stack([delayed_tap, input_signal], axis=0)
        forward_tap_full = lax.all_gather(tap_rows, "mp", axis=1, tiled=True).reshape(
            2 * full_res, block_length_rows
        )
        embedding = jnp.dot(onehot, table_low, preferred_element_type=jnp.float32)
        forward_preact = (
            lax.dot_general(
                conv_matrix, forward_tap_full, contract_first, preferred_element_type=jnp.float32
            )
            + embedding[:, None]
        )
        hidden = (
            jnp.tanh(forward_preact[:gate_dev]) * jax.nn.sigmoid(forward_preact[gate_dev:])
        ).astype(jnp.bfloat16)
        partial_sums = lax.dot_general(
            output_low, hidden, contract_first, preferred_element_type=jnp.float32
        ).reshape(2, full_res, block_length_rows)
        projected = lax.psum_scatter(partial_sums, "mp", scatter_dimension=1, tiled=True)
        branch = projected[0]
        new_resid = (residual_stream + branch) * root_half
        new_skip = skip_accumulated + projected[1]
        new_resid, new_skip, branch, kept_data = (
            new_resid,
            new_skip,
            branch,
            (forward_tap_full, forward_preact, hidden),
        )
        valid_rows = (positions < lengths[batch_idx]).astype(jnp.float32)[None, :] * is_live
        square_res = square_res + jnp.sum(valid_rows * new_resid * new_resid)
        square_branch = square_branch + jnp.sum(valid_rows * branch * branch)
        counted = counted + jnp.sum(valid_rows) * residual_local
        kept_list.append(kept_data)
        resid_list.append(new_resid)
        skip_list.append(new_skip)
        if tick_num < micro_count:
            recv_resid, recv_skip = passed_along((new_resid, new_skip), "section", 1)
    square_res, square_branch, counted = lax.psum(
        (square_res, square_branch, counted), ("seq", "mp")
    )
    rms_out = jnp.stack([jnp.sqrt(square_res / counted), jnp.sqrt(square_branch / counted)])[None]
    res_out = jnp.stack(
        [
            jnp.where(leading_section, resid_list[m_idx], resid_list[m_idx + 1])
            for m_idx in range(micro_count)
        ]
    )[None]
    skip_out = jnp.stack(
        [
            jnp.where(leading_section, skip_list[m_idx], skip_list[m_idx + 1])
            for m_idx in range(micro_count)
        ]
    )[None]
    conv_acc = jnp.zeros((2 * full_res, 2 * gate_dev), jnp.float32)
    table_acc = jnp.zeros((speaker_rows, 2 * gate_dev), jnp.float32)
    out_acc = jnp.zeros((gate_dev, 2 * full_res), jnp.float32)
    recv_grad = jnp.zeros((residual_local, block_length_rows), jnp.float32)
    input_grads = []
    for tick_num in range(micro_count + 1):
        index_one = min(tick_num, micro_count - 1)
        index_zero = max(tick_num - 1, 0)
        batch_idx = jnp.where(leading_section, index_zero, index_one)
        is_live = jnp.where(leading_section, tick_num >= 1, tick_num < micro_count).astype(
            jnp.float32
        )
        valid_rows = (positions < lengths[batch_idx]).astype(jnp.float32)[None, :] * is_live
        onehot = (jnp.arange(speaker_rows) == speakers[batch_idx]).astype(jnp.bfloat16)
        kept_data = jax.tree.map(
            lambda zero_side, one_side: jnp.where(leading_section, zero_side, one_side),
            kept_list[index_zero],
            kept_list[index_one + 1],
        )
        skip_grad = (
            jnp.where(leading_section, cot_skip[index_zero], cot_skip[index_one]) * valid_rows
        )
        resid_grad = jnp.where(
            leading_section, recv_grad * is_live, cot_res[index_one] * valid_rows
        )
        tap_full, preact, hidden_used = kept_data
        proj_grad = jnp.stack([resid_grad * root_half, skip_grad], axis=0).astype(jnp.bfloat16)
        full_grad = lax.all_gather(proj_grad, "mp", axis=1, tiled=True).reshape(
            2 * full_res, block_length_rows
        )
        hidden_grad = jnp.dot(output_low, full_grad, preferred_element_type=jnp.float32)
        weight_term = lax.dot_general(
            hidden_used, full_grad, contract_last, preferred_element_type=jnp.float32
        )
        filter_act = jnp.tanh(preact[:gate_dev])
        gate_act = jax.nn.sigmoid(preact[gate_dev:])
        filter_grad = hidden_grad * gate_act * (1.0 - filter_act * filter_act)
        gate_grad = hidden_grad * filter_act * gate_act * (1.0 - gate_act)
        preact_grad = jnp.concatenate([filter_grad, gate_grad], axis=0).astype(jnp.bfloat16)
        conv_term = lax.dot_general(
            tap_full, preact_grad, contract_last, preferred_element_type=jnp.float32
        )
        column_sums = jnp.sum(preact_grad.astype(jnp.float32), axis=1)
        table_term = onehot.astype(jnp.float32)[:, None] * column_sums[None, :]
        tap_terms = jnp.dot(conv_matrix, preact_grad, preferred_element_type=jnp.float32)
        tap_gradient = lax.psum_scatter(
            tap_terms.reshape(2, full_res, block_length_rows), "mp", scatter_dimension=1, tiled=True
        )
        joined_taps_gradient = lax.dynamic_update_slice_in_dim(
            jnp.zeros((residual_local, FIRST_DILATION + block_length_rows), jnp.float32),
            tap_gradient[0],
            FIRST_DILATION - dilation_factor,
            1,
        )
        border_gradient = passed_along(joined_taps_gradient[:, :FIRST_DILATION], "seq", -1)
        input_gradient_rows = tap_gradient[1] + joined_taps_gradient[:, FIRST_DILATION:]
        input_gradient_rows = input_gradient_rows.at[:, block_length_rows - FIRST_DILATION :].add(
            border_gradient
        )
        resid_back, conv_term, weight_term, table_term = (
            resid_grad * root_half + input_gradient_rows,
            conv_term,
            weight_term,
            table_term,
        )
        conv_acc = conv_acc + conv_term
        out_acc = out_acc + weight_term
        table_acc = table_acc + table_term
        input_grads.append(resid_back)
        if tick_num < micro_count:
            recv_grad = passed_along(resid_back, "section", -1)
    grad_in = jnp.stack(
        [
            jnp.where(leading_section, input_grads[m_idx + 1], input_grads[m_idx])
            for m_idx in range(micro_count)
        ]
    )[None]
    conv_total, out_total, table_total = lax.psum((conv_acc, out_acc, table_acc), "seq")
    conv_grad = conv_total.reshape(conv_weight.shape)
    out_grad = out_total.reshape(out_weight.shape)
    table_grad = table_total.reshape(speaker_table.shape)
    conv_new, conv_m_new, conv_v_new = adamw(conv_weight, conv_m, conv_v, conv_grad, 0.03)
    out_new, out_m_new, out_v_new = adamw(out_weight, out_m, out_v, out_grad, 0.1)
    table_new, table_m_new, table_v_new = adamw(speaker_table, table_m, table_v, table_grad, 0.3)
    return (
        res_out,
        skip_out,
        grad_in,
        rms_out,
        conv_grad,
        conv_new,
        conv_m_new,
        conv_v_new,
        out_grad,
        out_new,
        out_m_new,
        out_v_new,
        table_grad,
        table_new,
        table_m_new,
        table_v_new,
    )


def solution(mesh):
    in_specs = (
        P(None, "mp", "seq"),
        P(None, "mp", "seq"),
        P(None, "mp", "seq"),
        P(None, "mp", "seq"),
        P(),
        P(),
        P("section", None, None, None, "mp"),
        P("section", None, None, None, "mp"),
        P("section", None, None, None, "mp"),
        P("section", "mp", None),
        P("section", "mp", None),
        P("section", "mp", None),
        P("section", None, None, "mp"),
        P("section", None, None, "mp"),
        P("section", None, None, "mp"),
    )
    out_specs = (
        P("section", None, "mp", "seq"),
        P("section", None, "mp", "seq"),
        P("section", None, "mp", "seq"),
        P("section", None),
        P("section", None, None, None, "mp"),
        P("section", None, None, None, "mp"),
        P("section", None, None, None, "mp"),
        P("section", None, None, None, "mp"),
        P("section", "mp", None),
        P("section", "mp", None),
        P("section", "mp", None),
        P("section", "mp", None),
        P("section", None, None, "mp"),
        P("section", None, None, "mp"),
        P("section", None, None, "mp"),
        P("section", None, None, "mp"),
    )
    n_seq = mesh.shape["seq"]
    fits = mesh.shape["mp"] == 2 and n_seq in (4, 8, 16)
    return jax.shard_map(
        functools.partial(fast_shards, n_seq) if fits else shards,
        mesh=mesh,
        in_specs=in_specs,
        out_specs=out_specs,
        check_vma=False,
    )
```

```python
import functools
import math

import jax
import jax.numpy as jnp
from jax import lax
from jax.experimental import pallas as pl
from jax.experimental.pallas import tpu as pltpu
from jax.sharding import PartitionSpec as P

FIRST_DILATION = 512
STEP = 10
MESH = pl.DeviceIdType.MESH
TILE = 512
UNITS = 6
Z_FIRST = 3

beta_one = 0.9
beta_two = 0.999
adam_eps = 1e-08
decay_rate = 0.01
root_half = math.sqrt(0.5)


def passed_along(value, axis, steps):
    count = lax.axis_size(axis)
    first, last = (max(0, -steps), min(count, count - steps))
    return lax.ppermute(value, axis, [(source, source + steps) for source in range(first, last)])


def adamw(weight, moment, second, gradient, step_rate):
    moment_new = beta_one * moment + (1.0 - beta_one) * gradient
    second_new = beta_two * second + (1.0 - beta_two) * gradient * gradient
    corr_one = 1.0 - beta_one**STEP
    corr_two = 1.0 - beta_two**STEP
    update = moment_new / corr_one / (jnp.sqrt(second_new / corr_two) + adam_eps)
    weight_new = weight - step_rate * (update + decay_rate * weight)
    return (weight_new, moment_new, second_new)


def dot(left, right):
    return jnp.dot(left, right, preferred_element_type=jnp.float32)


def dot_last(left, right):
    return lax.dot_general(
        left, right, (((1,), (1,)), ((), ())), preferred_element_type=jnp.float32
    )


def rows_at(start, size):
    return pl.ds(start if isinstance(start, int) else pl.multiple_of(start, 16), size)


def cols_at(start, size):
    return pl.ds(start if isinstance(start, int) else pl.multiple_of(start, 128), size)


def layers_kernel(
    sizes,
    x_ref,
    skip_ref,
    cot_res_ref,
    cot_skip_ref,
    lengths_ref,
    speakers_ref,
    conv_ref,
    out_ref,
    table_ref,
    res_ref,
    skipped_ref,
    grad_ref,
    weight_ref,
    small_ref,
    conv_wide,
    out_wide,
    table_wide,
    xf,
    wc,
    wct,
    wo,
    wot,
    et,
    in1,
    next_out,
    next_in,
    past1,
    act_f,
    act_q,
    hid,
    dproj,
    dres0,
    dpre,
    grad1,
    past_grad1,
    edge_out,
    edge_in,
    res0,
    skip_sum,
    cot_a,
    cot_b,
    skip_low,
    res_low,
    grad1_low,
    grad0,
    past0_out,
    past0_in,
    grad0_low,
    stats,
    acc,
    from_core,
    down,
    final,
    small,
    small_in,
    small_sum,
    send_sem,
    recv_sem,
    local_sem,
):
    full, local, gates, span, n_seq = sizes
    gate_local = gates // 2
    width = 2 * gate_local
    halo = FIRST_DILATION
    n_z = n_seq // 2
    c = lax.axis_index("section")
    s = lax.axis_index("seq")
    x = lax.axis_index("mp")
    z, y = s // 2, s % 2
    oc, ox = 1 - c, 1 - x
    bf16, f32 = jnp.bfloat16, jnp.float32
    counts = {"send": 0, "recv": 0, "local": 0}
    pending = []
    inside = [None]

    def take(kind, amount=1):
        counts[kind] += amount
        return counts[kind] - amount

    def when(cond, action):
        if cond is None:
            action()
        else:
            pl.when(cond)(action)

    def on(cond, action):
        inside[0] = cond
        pl.when(cond)(lambda: action())
        inside[0] = None

    def send(source, target, device, recv_at, cond=None):
        at = take("send")

        def make():
            return pltpu.make_async_remote_copy(
                src_ref=source(),
                dst_ref=target(),
                send_sem=send_sem.at[at],
                recv_sem=recv_sem.at[recv_at()],
                device_id=device(),
                device_id_type=MESH,
            )

        when(cond, lambda: make().start())
        pending.append((lambda: make().wait_send(), inside[0] if cond is None else cond))

    def arrive(target, recv_at, cond=None):
        when(
            cond,
            lambda: pltpu.make_async_remote_copy(
                src_ref=target,
                dst_ref=target,
                send_sem=send_sem.at[0],
                recv_sem=recv_sem.at[recv_at],
                device_id={"section": oc},
                device_id_type=MESH,
            ).wait_recv(),
        )

    def fetch(source, target, cond=None):
        copy = pltpu.make_async_copy(source, target, local_sem.at[take("local")])
        when(cond, copy.start)
        return copy

    def to(axis, index):
        return lambda: {axis: index()}

    core_dev = to("section", lambda: 1 - c)
    mp_dev = to("mp", lambda: 1 - x)
    y_dev = to("seq", lambda: z * 2 + 1 - y)
    prev_dev, next_dev = to("seq", lambda: s - 1), to("seq", lambda: s + 1)
    has_prev, has_next = s > 0, s < n_seq - 1

    z_seqs = [lax.rem(z + step, n_z) * 2 + y for step in range(n_z)]

    def z_seq(step):
        return z_seqs[step]

    def z_dev(step):
        return to("seq", lambda: z_seq(step))

    bits = [y] + [(z // (1 << bit)) % 2 for bit in range((n_seq // 2).bit_length() - 1)]
    pairs = [z * 2 + 1 - y] + [
        (z + (1 - 2 * bits[bit + 1]) * (1 << bit)) * 2 + y for bit in range(len(bits) - 1)
    ]
    depth = len(bits)
    pair_devs = [to("seq", lambda way=way: pairs[way]) for way in range(depth)]

    barrier = pltpu.get_barrier_semaphore()
    for device in [core_dev, mp_dev, y_dev, *[z_dev(step) for step in range(1, n_z)]]:
        pl.semaphore_signal(barrier, inc=1, device_id=device(), device_id_type=MESH)
    before, after = (y == 0) & (z > 0), (y == 1) & (z < n_z - 1)

    @pl.when(before)
    def _():
        pl.semaphore_signal(barrier, inc=1, device_id=prev_dev(), device_id_type=MESH)

    @pl.when(after)
    def _():
        pl.semaphore_signal(barrier, inc=1, device_id=next_dev(), device_id_type=MESH)

    own_rows, other_rows = rows_at(x * local, local), rows_at(ox * local, local)
    got_conv = fetch(conv_ref, conv_wide)
    got_table = fetch(table_ref, table_wide)
    got_out = fetch(out_ref, out_wide)
    got_cot_a = fetch(cot_res_ref.at[c], cot_a)
    got_cot_b = fetch(cot_skip_ref.at[c], cot_b)
    chunks = span // halo
    got_x = [
        fetch(x_ref.at[c, :, pl.ds(chunk * halo, halo)], xf.at[chunk + 1, own_rows])
        for chunk in range(chunks)
    ]
    got_skip = fetch(skip_ref.at[c], skip_sum)

    def cast_conv(step, carry):
        for block in range(width // 128):
            half, lane = block // (gate_local // 128), block % (gate_local // 128)
            first = step * 256 * (width // 128) + lane * 2 + half
            wc[c, x, rows_at(step * 256, 256), pl.ds(block * 128, 128)] = conv_wide[
                pl.ds(first, 256, stride=width // 128), :
            ].astype(bf16)
        return carry

    got_conv.wait()
    lax.fori_loop(0, 2 * full // 256, cast_conv, None)
    got_table.wait()
    marks = lax.broadcasted_iota(jnp.int32, (16, width), 0)
    emb = jnp.zeros((16, width), f32)
    for micro in range(2):
        rows = table_wide[speakers_ref[micro]]
        row = jnp.concatenate([rows[0:1, :], rows[1:2, :]], axis=1)
        emb = jnp.where(marks == micro, row, emb)
    wc[c, x, 2 * full : 2 * full + 16, :] = emb.astype(bf16)
    got_out.wait()
    wo[c, rows_at(x * gate_local, gate_local), :] = out_wide[...].astype(bf16)

    @pl.when(before | after)
    def _():
        pl.semaphore_wait(barrier, 3 + n_z)

    @pl.when(jnp.logical_not(before | after))
    def _():
        pl.semaphore_wait(barrier, 2 + n_z)

    conv_rows, out_rows = 2 * full // n_seq, gate_local // n_seq
    conv_at, conv_core_at = take("recv", n_seq), take("recv", n_seq)
    out_at, emb_at = take("recv", n_seq), take("recv")

    def conv_slice(index, layer, block):
        return wc.at[layer, block, rows_at(index * conv_rows, conv_rows)]

    def out_slice(index, layer, block):
        return wo.at[layer, rows_at(block * gate_local + index * out_rows, out_rows)]

    def emb_part(layer, block):
        return wc.at[layer, block, 2 * full : 2 * full + 16]

    def conv_block(layer, block):
        return wc.at[layer, block, 0 : 2 * full]

    def out_block(layer, block):
        return wo.at[layer, rows_at(block * gate_local, gate_local)]

    def send_same(ref, device, recv_at, cond=None):
        send(ref, ref, device, recv_at, cond)

    def cross_weights():
        send_same(lambda: conv_slice(s, c, x), mp_dev, lambda: conv_at + s)
        send_same(lambda: emb_part(c, x), mp_dev, lambda: emb_at)
        send_same(lambda: out_slice(s, c, x), mp_dev, lambda: out_at + s)

    on(c == 0, cross_weights)
    x_at = [take("recv") for _ in range(chunks)]
    for copy in got_x:
        copy.wait()
    for chunk in reversed(range(chunks)):
        send_same(
            lambda chunk=chunk: xf.at[chunk + 1, own_rows], mp_dev, lambda chunk=chunk: x_at[chunk]
        )
    on(c == 1, cross_weights)
    halo_at = [take("recv"), take("recv")]
    send(
        lambda: xf.at[chunks, own_rows],
        lambda: xf.at[0, own_rows],
        next_dev,
        lambda: halo_at[0],
        has_next,
    )
    core_at = [take("recv") for _ in range(5)]
    send_same(lambda: conv_block(c, x), core_dev, lambda: core_at[0])
    send_same(lambda: emb_part(c, x), core_dev, lambda: core_at[1])
    send_same(lambda: out_block(c, x), core_dev, lambda: core_at[2])

    @pl.when(s == 0)
    def _():
        xf[0] = jnp.zeros((full, halo), bf16)
        next_in[...] = jnp.zeros(next_in.shape, bf16)

    @pl.when(s == n_seq - 1)
    def _():
        past0_in[...] = jnp.zeros(past0_in.shape, bf16)
        edge_in[...] = jnp.zeros(edge_in.shape, bf16)

    stats[...] = jnp.zeros(stats.shape, f32)
    length = lengths_ref[c]

    def valid_at(start, size):
        at = s * span + start + lax.broadcasted_iota(jnp.int32, (1, size), 1)
        return jnp.where(at < length, 1.0, 0.0).astype(f32)

    def cast_cotangents(step, carry):
        at = cols_at(step * TILE, TILE)
        valid = valid_at(step * TILE, TILE)
        dproj[step, own_rows, :] = (cot_a[:, at] * valid * root_half).astype(bf16)
        dproj[step, rows_at(full + x * local, local), :] = (cot_b[:, at] * valid).astype(bf16)
        return carry

    tiles = span // TILE
    got_cot_a.wait()
    got_cot_b.wait()
    lax.fori_loop(0, tiles, cast_cotangents, None)
    cot_at = take("recv", 2 * tiles)

    def cot_piece(tile, part, block):
        return dproj.at[tile, rows_at(part * full + block * local, local)]

    for tile in range(tiles):
        for part in range(2):
            send_same(
                functools.partial(cot_piece, tile, part, x),
                mp_dev,
                lambda tile=tile, part=part: cot_at + tile * 2 + part,
            )

    def turn_conv(layer, block, first, rows):
        wct[layer, rows_at(block * width, width), cols_at(first, rows)] = wc[
            layer, block, rows_at(first, rows), :
        ].T

    def turn_rest(layer, block):
        values = wc[layer, block, 2 * full : 2 * full + 16, :].astype(f32)
        mark_row = lax.broadcasted_iota(jnp.int32, values.shape, 0)
        picked = jnp.sum(jnp.where(mark_row == c, values, 0.0), axis=0, keepdims=True)
        et[layer, rows_at(block * width, width), :] = jnp.broadcast_to(picked, (128, width)).T

        for part, start in enumerate((x * local, full + x * local, ox * local)):
            wot[layer, part * local : (part + 1) * local, cols_at(block * gate_local, gate_local)] = wo[
                layer, rows_at(block * gate_local, gate_local), cols_at(start, local)
            ].T

    def turn_all(layer, block):
        for step in range(2 * full // TILE):
            turn_conv(layer, block, step * TILE, TILE)
        turn_rest(layer, block)

    def spread_first():
        arrive(conv_slice(s, c, ox), conv_at + s)
        for step in range(1, n_z):
            send_same(lambda: conv_slice(s, c, ox), z_dev(step), lambda: conv_at + s)
        send_same(lambda: conv_slice(s, c, ox), y_dev, lambda: conv_at + s)
        send_same(lambda: conv_slice(s, c, ox), core_dev, lambda: conv_core_at + s)
        arrive(emb_part(c, ox), emb_at)
        send_same(lambda: emb_part(c, ox), core_dev, lambda: core_at[3])
        arrive(out_slice(s, c, ox), out_at + s)
        for step in range(1, n_z):
            send_same(lambda: out_slice(s, c, ox), z_dev(step), lambda: out_at + s)
        send_same(lambda: out_slice(s, c, ox), y_dev, lambda: out_at + s)

    def spread_conv():
        for step in range(1, n_z):
            arrive(conv_slice(z_seq(step), c, ox), conv_at + z_seq(step))
            here = functools.partial(lambda step: conv_slice(z_seq(step), c, ox), step)
            send_same(here, y_dev, lambda step=step: conv_at + z_seq(step))
            send_same(here, core_dev, lambda step=step: conv_core_at + z_seq(step))

    def spread_out():
        for step in range(1, n_z):
            arrive(out_slice(z_seq(step), c, ox), out_at + z_seq(step))
            here = functools.partial(lambda step: out_slice(z_seq(step), c, ox), step)
            send_same(here, y_dev, lambda step=step: out_at + z_seq(step))

    def spread_last():
        for step in range(n_z):
            arrive(conv_slice(z_seq(step) + 1 - 2 * y, c, ox), conv_at + z_seq(step) + 1 - 2 * y)
            here = functools.partial(
                lambda step: conv_slice(z_seq(step) + 1 - 2 * y, c, ox), step
            )
            send_same(here, core_dev, lambda step=step: conv_core_at + z_seq(step) + 1 - 2 * y)
        for step in range(n_z):
            arrive(out_slice(z_seq(step) + 1 - 2 * y, c, ox), out_at + z_seq(step) + 1 - 2 * y)
        send_same(lambda: out_block(c, ox), core_dev, lambda: core_at[4])

    def all_from_core():
        for step in range(n_seq):
            arrive(conv_slice(step, oc, ox), conv_core_at + step)
        arrive(emb_part(oc, ox), core_at[3])
        arrive(out_block(oc, ox), core_at[4])

    on(c == 0, spread_first)

    @pl.when(c == 0)
    def _():
        turn_all(0, x)

    arrive(xf.at[chunks, other_rows], x_at[chunks - 1])
    send(
        lambda: xf.at[chunks, other_rows],
        lambda: xf.at[0, other_rows],
        next_dev,
        lambda: halo_at[1],
        has_next,
    )
    on(c == 0, spread_conv)
    arrive(conv_block(oc, x), core_at[0])
    arrive(emb_part(oc, x), core_at[1])
    arrive(out_block(oc, x), core_at[2])

    @pl.when(c == 1)
    def _():
        turn_all(0, x)

    on(c == 0, spread_out)
    on(c == 0, spread_last)

    on(c == 1, all_from_core)
    turn_all(0, ox)

    def fold(values):
        total = jnp.sum(values.reshape(local // 8, 8, TILE), axis=0)
        return sum(total[:, part * 128 : (part + 1) * 128] for part in range(TILE // 128))

    def gated(layer, pre, at):
        halves = []
        for block in range(2):
            base = block * width
            shift = et[layer, base : base + width, :]
            shift = jnp.concatenate([shift] * (TILE // 128), axis=1)
            f = jnp.tanh(pre[base : base + gate_local] + shift[:gate_local])
            q = 0.5 * jnp.tanh(
                0.5 * (pre[base + gate_local : base + width] + shift[gate_local:])
            ) + 0.5
            rows = slice(block * gate_local, (block + 1) * gate_local)
            act_f[layer, rows, at] = f
            act_q[layer, rows, at] = q
            halves.append((f * q).astype(bf16))
            hid[layer, rows, at] = halves[-1]
        return jnp.concatenate(halves, axis=0)

    def forward0(step):
        start = step * TILE
        at = cols_at(start, TILE)
        chunk, inner = start // halo, pl.ds(start % halo, TILE)
        pre = dot(wct[0], jnp.concatenate([xf[chunk, :, inner], xf[chunk + 1, :, inner]], axis=0))
        hidden = gated(0, pre, at)
        valid = valid_at(start, TILE)
        proj = dot(wot[0], hidden)
        branch = proj[0:local]
        res = (xf[chunk + 1, own_rows, inner].astype(f32) + branch) * root_half
        res0[:, at] = res
        in1[own_rows, at] = res.astype(bf16)
        stats[0, 0] += fold(valid * res * res)
        stats[0, 1] += fold(valid * branch * branch)
        res = (xf[chunk + 1, other_rows, inner].astype(f32) + proj[2 * local :]) * root_half
        in1[other_rows, at] = res.astype(bf16)
        total = skip_sum[:, at] + proj[local : 2 * local]
        skip_sum[:, at] = total
        skip_low[0, :, at] = total.astype(bf16)

    late_tiles = (span - halo) // TILE
    got_skip.wait()
    for chunk in range(chunks - 1):
        arrive(xf.at[chunk + 1, other_rows], x_at[chunk])
    on(c == 1, spread_first)
    for step in range(late_tiles, tiles):
        forward0(step)
    in1_at = take("recv")
    next_out[...] = in1[:, span - 128 : span]
    send(
        lambda: next_out,
        lambda: next_in,
        next_dev,
        lambda: in1_at,
        has_next,
    )
    on(c == 1, spread_conv)
    on(c == 1, spread_out)
    arrive(xf.at[0, own_rows], halo_at[0], has_prev)
    arrive(xf.at[0, other_rows], halo_at[1], has_prev)
    for step in range(late_tiles):
        forward0(step)
    on(c == 1, spread_last)

    result_at = [take("recv") for _ in range(3)]
    locals_pending = []

    def give(layer, kind, source, target):
        copy = fetch(source, target.at[c], c == layer)
        locals_pending.append((copy, c == layer))
        send(lambda: source, lambda: target.at[c], core_dev, lambda: result_at[kind], c != layer)

    give(0, 0, in1.at[own_rows], res_ref)
    give(0, 1, skip_low.at[0], skipped_ref)

    turn_all(1, x)
    on(c == 0, all_from_core)
    turn_all(1, ox)

    def forward1(step):
        start = step * TILE
        at = cols_at(start, TILE)
        for base in range(0, full, 256):
            rows = slice(base, base + 256)
            if start == 0:
                wide = jnp.concatenate([next_in[rows, :], in1[rows, 0:TILE]], axis=1).astype(f32)
            else:
                wide = in1[rows, start - 128 : start + TILE].astype(f32)
            past1[base : base + 256, at] = pltpu.roll(wide, 1, 1)[:, 128:].astype(bf16)
        pre = dot(wct[1], jnp.concatenate([past1[:, at], in1[:, at]], axis=0))
        hidden = gated(1, pre, at)
        valid = valid_at(start, TILE)
        proj = dot(wot[1, 0 : 2 * local], hidden)
        branch = proj[0:local]
        res = (res0[:, at] + branch) * root_half
        res_low[:, at] = res.astype(bf16)
        stats[1, 0] += fold(valid * res * res)
        stats[1, 1] += fold(valid * branch * branch)
        total = skip_sum[:, at] + proj[local:]
        skip_low[1, :, at] = total.astype(bf16)

    arrive(next_in, in1_at, has_prev)
    for step in range(tiles):
        forward1(step)
    give(1, 0, res_low, res_ref)
    give(1, 1, skip_low.at[1], skipped_ref)

    def through_gates(layer, dhidden, at):
        for block in range(2):
            rows = slice(block * gate_local, (block + 1) * gate_local)
            f, q = act_f[layer, rows, at], act_q[layer, rows, at]
            d = dhidden[rows] * q
            base = block * width
            dpre[layer, base : base + gate_local, at] = (d * (1.0 - f * f)).astype(bf16)
            dpre[layer, base + gate_local : base + width, at] = (d * f * (1.0 - q)).astype(bf16)

    def backward1(step):
        at = cols_at(step * TILE, TILE)
        through_gates(1, dot(wo[1], dproj[step]), at)
        both = jnp.concatenate([wc[1, block, 0 : 2 * full, :] for block in range(2)], axis=1)
        taps = dot(both, dpre[1, :, at])
        past_grad1[:, at] = taps[0:full]
        grad1[:, at] = taps[full:] + dproj[step, 0:full, :].astype(f32)

    def join1(step):
        start = step * TILE
        at = cols_at(start, TILE)
        for base in range(0, full, 256):
            rows = slice(base, base + 256)
            wide = past_grad1[rows, cols_at(start, TILE + 128)]
            total = grad1[rows, at] + pltpu.roll(wide, TILE + 127, 1)[:, 0:TILE]
            grad1[rows, at] = total
            dres0[rows, at] = (root_half * total).astype(bf16)
        own = grad1[own_rows, at]
        grad1_low[:, at] = own.astype(bf16)
        grad0[:, at] = root_half * own

    def backward0(step):
        start = step * TILE
        at = cols_at(start, TILE)
        dhidden = dot(wo[0], jnp.concatenate([dres0[:, at], dproj[step, full:, :]], axis=0))
        through_gates(0, dhidden, at)
        own = [
            jnp.concatenate([wc[0, block, rows, :] for block in range(2)], axis=1)
            for rows in (own_rows, rows_at(full + x * local, local))
        ]
        taps = dot(jnp.concatenate(own, axis=0), dpre[0, :, at])
        grad0[:, at] += taps[local:]
        return taps[0:local]

    edge_at, past0_at = take("recv"), take("recv")
    early_tiles = halo // TILE

    for step in range(tiles):
        for part in range(2):
            arrive(cot_piece(step, part, ox), cot_at + step * 2 + part)
        backward1(step)
        if step == 0:
            edge_out[...] = past_grad1[:, 0:128].astype(bf16)
            send(lambda: edge_out, lambda: edge_in, prev_dev, lambda: edge_at, has_prev)

    total_rows = 3 * full
    unit_rows = total_rows // UNITS
    unit_core_at = [take("recv") for _ in range(UNITS)]
    down_at = [[take("recv") for _ in range(depth)] for _ in range(UNITS)]
    up_at = [[take("recv") for _ in range(depth)] for _ in range(UNITS)]
    small_at = [take("recv") for _ in range(2 + depth)]
    stored_at = take("local", UNITS + 1)

    def to_core(layer, first, size):
        for unit in range(first // unit_rows, (first + size) // unit_rows):
            rows = pl.ds(unit * unit_rows, unit_rows)
            send(
                lambda rows=rows: acc.at[layer, rows],
                lambda rows=rows: from_core.at[rows],
                core_dev,
                lambda unit=unit: unit_core_at[unit],
                c != layer,
            )

    def unit_conv(layer, past, now):
        taps = jnp.concatenate([past, now, jnp.ones((16, span), bf16)], axis=0)
        product = dot_last(taps, dpre[layer, rows_at(x * width, width), :])
        acc[layer, 0 : 2 * full, :] = product[0 : 2 * full].astype(bf16)
        sums = product[2 * full : 2 * full + 8]
        mark = lax.broadcasted_iota(jnp.int32, sums.shape, 0)
        small[layer, 0:8, :] = jnp.where(mark == c, sums, 0.0)
        small[layer, 8:16, :] = jnp.zeros((8, width), f32)
        small[layer, 8:16, 0:128] = stats[layer, 0]
        small[layer, 8:16, 128:256] = stats[layer, 1]
        to_core(layer, 0, 2 * full)
        send(
            lambda: small.at[layer],
            lambda: small_in.at[0],
            core_dev,
            lambda: small_at[0],
            c != layer,
        )

    def unit_out(layer, parts):
        hidden = hid[layer, rows_at(x * gate_local, gate_local), :]
        product = dot_last(hidden, jnp.concatenate(parts, axis=0))
        for part in range(2 * full // width):
            acc[layer, pl.ds(2 * full + part * gate_local, gate_local), :] = product[
                :, part * width : (part + 1) * width
            ].astype(bf16)
        to_core(layer, 2 * full, full)

    n_stages = 2 * depth + 1

    def order(unit):
        ways = list(range(depth))
        return [1, 0, *ways[2:]] if unit == Z_FIRST and depth > 1 else ways

    def kept(unit, level, flip=False):
        start, size = unit * unit_rows, unit_rows
        for step in range(level):
            size //= 2
            bit = bits[order(unit)[step]]
            if flip and step == level - 1:
                bit = 1 - bit
            start = start + bit * size
        return rows_at(start, size)

    def landing(unit, level):
        size = unit_rows >> level
        return pl.ds(unit * unit_rows + unit_rows - 2 * size, size)

    def unit_stage(layer, unit, stage):
        ways = order(unit)
        if stage <= depth:
            here = kept(unit, stage)
            if stage == 0:
                arrive(from_core.at[here], unit_core_at[unit])
                other = from_core[here, :]
            else:
                place = landing(unit, stage)
                arrive(down.at[place], down_at[unit][stage - 1])
                other = down[place, :]
            total = (acc[layer, here, :].astype(f32) + other.astype(f32)).astype(bf16)
            if stage < depth:
                acc[layer, here, :] = total
                send(
                    lambda: acc.at[layer, kept(unit, stage + 1, True)],
                    lambda: down.at[landing(unit, stage + 1)],
                    pair_devs[ways[stage]],
                    lambda: down_at[unit][stage],
                )
                return
            final[here, :] = total
        if stage > depth:
            level = 2 * depth + 1 - stage
            arrive(final.at[kept(unit, level, True)], up_at[unit][level - 1])
        level = 2 * depth - stage
        if level > 0:
            send_same(
                lambda: final.at[kept(unit, level)],
                pair_devs[ways[level - 1]],
                lambda: up_at[unit][level - 1],
            )
        else:
            here = pl.ds(unit * unit_rows, unit_rows)
            pltpu.make_async_copy(
                final.at[here], weight_ref.at[here], local_sem.at[stored_at + unit]
            ).start()

    def small_stage(layer, stage):
        names = [core_dev, mp_dev, *pair_devs]
        arrive(small_in.at[stage], small_at[stage])
        if stage == 0:
            small_sum[0] = small[layer] + small_in[0]
        else:
            sums = small_sum[stage - 1, 0:8, :]
            small_sum[stage, 0:8, :] = sums if stage == 1 else sums + small_in[stage, 0:8, :]
            small_sum[stage, 8:16, :] = small_sum[stage - 1, 8:16, :] + small_in[stage, 8:16, :]
        if stage < len(names) - 1:
            send(
                lambda: small_sum.at[stage],
                lambda: small_in.at[stage + 1],
                names[stage + 1],
                lambda: small_at[stage + 1],
            )
        else:
            pltpu.make_async_copy(
                small_sum.at[stage], small_ref, local_sem.at[stored_at + UNITS]
            ).start()

    def in_order_of_arrival(layer, first_stage, units):
        ready = [(float(at), at, unit, first_stage) for at, unit in enumerate(units)]
        free = [0.0] * depth
        clock, small_next = 0.0, 0
        while ready:
            ready.sort()
            at, rank, unit, stage = ready.pop(0)
            unit_stage(layer, unit, stage)
            clock = max(clock, at) + 0.25
            if stage < n_stages - 1:
                way = order(unit)[min(stage, 2 * depth - 1 - stage)]
                level = min(stage, 2 * depth - 1 - stage)
                free[way] = max(free[way], clock) + 3.0 / 2**level * (2 if way == 2 else 1)
                ready.append((free[way] + 1.0, rank, unit, stage + 1))
            if stage == n_stages - 1 or stage == 2:
                if small_next < 2 + depth:
                    small_stage(layer, small_next)
                    small_next += 1
        for stage in range(small_next, 2 + depth):
            small_stage(layer, stage)

    unit_order = [4, 5, 0, 1, 2, 3]

    def all_times(first):
        rows = slice(first, first + full)
        return jnp.concatenate([dproj[tile, rows, :] for tile in range(tiles)], axis=1)

    unit_out(1, [all_times(0), all_times(full)])
    unit_conv(1, past1[...], in1[...])

    arrive(edge_in, edge_at, has_next)
    past_grad1[:, span : span + 128] = edge_in[...].astype(f32)

    def start_sums(layer):
        for unit in unit_order:
            unit_stage(layer, unit, 0)

    for step in range(tiles):
        join1(step)
    for step in range(early_tiles):
        past0_out[:, cols_at(step * TILE, TILE)] = backward0(step).astype(bf16)
    send(lambda: past0_out, lambda: past0_in, prev_dev, lambda: past0_at, has_prev)
    on(c == 1, lambda: start_sums(1))
    for step in range(early_tiles, tiles):
        grad0[:, cols_at(step * TILE - halo, TILE)] += backward0(step)
    give(1, 2, grad1_low, grad_ref)
    unit_out(0, [dres0[...], all_times(full)])
    unit_conv(
        0,
        jnp.concatenate([xf[chunk] for chunk in range(chunks)], axis=1),
        jnp.concatenate([xf[chunk + 1] for chunk in range(chunks)], axis=1),
    )

    arrive(past0_in, past0_at, has_next)

    def join0(step, carry):
        at = cols_at(step * TILE, TILE)
        grad0_low[:, at] = grad0[:, at].astype(bf16)
        return carry

    lax.fori_loop(0, (span - halo) // TILE, join0, None)

    def join0_late(step, carry):
        at = cols_at(step * TILE + span - halo, TILE)
        grad0_low[:, at] = (
            grad0[:, at] + past0_in[:, cols_at(step * TILE, TILE)].astype(f32)
        ).astype(bf16)
        return carry

    lax.fori_loop(0, halo // TILE, join0_late, None)
    give(0, 2, grad0_low, grad_ref)

    on(c == 0, lambda: start_sums(0))
    for wait, cond in pending:
        when(cond, wait)
    pending.clear()
    on(c == 0, lambda: in_order_of_arrival(0, 1, unit_order))
    on(c == 1, lambda: in_order_of_arrival(1, 1, unit_order))
    for unit in range(UNITS):
        here = pl.ds(unit * unit_rows, unit_rows)
        pltpu.make_async_copy(
            final.at[here], weight_ref.at[here], local_sem.at[stored_at + unit]
        ).wait()
    pltpu.make_async_copy(
        small_sum.at[1 + depth], small_ref, local_sem.at[stored_at + UNITS]
    ).wait()
    for kind, target in enumerate((res_ref, skipped_ref, grad_ref)):
        arrive(target.at[oc], result_at[kind])
    for copy, cond in locals_pending:
        when(cond, copy.wait)
    for wait, cond in pending:
        when(cond, wait)
    assert counts["send"] <= send_sem.shape[0], counts
    assert counts["recv"] <= recv_sem.shape[0], counts
    assert counts["local"] <= local_sem.shape[0], counts


def run_layers(
    x_in, skip_in, cot_res, cot_skip, lengths, speakers, conv_view, out_weight, table, n_seq
):
    micro, local, span = x_in.shape
    full = out_weight.shape[1] // 2
    gate_local = out_weight.shape[0]
    gates = 2 * gate_local
    bf16, f32 = jnp.bfloat16, jnp.float32
    halo = FIRST_DILATION
    rows = 3 * full
    depth = (n_seq // 2).bit_length()
    width = 2 * gate_local
    any_spec = pl.BlockSpec(memory_space=pl.ANY)
    scratch = [
        (conv_view.shape, f32),
        (out_weight.shape, f32),
        (table.shape, f32),
        ((span // halo + 1, full, halo), bf16),
        ((2, 2, 2 * full + 16, width), bf16),
        ((2, 2 * width, 2 * full), bf16),
        ((2, gates, 2 * full), bf16),
        ((2, 3 * local, gates), bf16),
        ((2, 2 * width, 128), f32),
        ((full, span), bf16),
        ((full, 128), bf16),
        ((full, 128), bf16),
        ((full, span), bf16),
        ((2, gates, span), f32),
        ((2, gates, span), f32),
        ((2, gates, span), bf16),
        ((span // TILE, 2 * full, TILE), bf16),
        ((full, span), bf16),
        ((2, 2 * width, span), bf16),
        ((full, span), f32),
        ((full, span + 128), f32),
        ((full, 128), bf16),
        ((full, 128), bf16),
        ((local, span), f32),
        ((local, span), f32),
        ((local, span), f32),
        ((local, span), f32),
        ((2, local, span), bf16),
        ((local, span), bf16),
        ((local, span), bf16),
        ((local, span), f32),
        ((local, halo), bf16),
        ((local, halo), bf16),
        ((local, span), bf16),
        ((2, 2, 8, 128), f32),
        ((2, rows, width), bf16),
        ((rows, width), bf16),
        ((rows, width), bf16),
        ((rows, width), bf16),
        ((2, 16, width), f32),
        ((2 + depth, 16, width), f32),
        ((2 + depth, 16, width), f32),
    ]
    result = jax.ShapeDtypeStruct((micro, local, span), bf16)
    return pl.pallas_call(
        functools.partial(layers_kernel, (full, local, gates, span, n_seq)),
        out_shape=(
            result,
            result,
            result,
            jax.ShapeDtypeStruct((rows, width), bf16),
            jax.ShapeDtypeStruct((16, width), f32),
        ),
        in_specs=[any_spec] * 4 + [pl.BlockSpec(memory_space=pltpu.SMEM)] * 2 + [any_spec] * 3,
        out_specs=[any_spec] * 5,
        scratch_shapes=[pltpu.VMEM(shape, kind) for shape, kind in scratch]
        + [
            pltpu.SemaphoreType.DMA((224,)),
            pltpu.SemaphoreType.DMA((144,)),
            pltpu.SemaphoreType.DMA((32,)),
        ],
        compiler_params=pltpu.CompilerParams(
            collective_id=0, has_side_effects=True, vmem_limit_bytes=62 * 1024 * 1024
        ),
        cost_estimate=pl.CostEstimate(
            flops=14_000_000_000, bytes_accessed=20_000_000, transcendentals=2_000_000
        ),
    )(x_in, skip_in, cot_res, cot_skip, lengths, speakers, conv_view, out_weight, table)


def lane_view(value):
    _, taps, full, halves, gate_local = value.shape
    blocks = gate_local // 128
    value = value.reshape(taps * full, halves, blocks, 128).transpose(0, 2, 1, 3)
    return value.reshape(taps * full * halves * blocks, 128)


def lane_back(value, shape):
    _, taps, full, halves, gate_local = shape
    blocks = gate_local // 128
    value = value.reshape(taps * full, blocks, halves, 128).transpose(0, 2, 1, 3)
    return value.reshape(shape)


def update_kernel(
    full,
    lengths_ref,
    speakers_ref,
    small_ref,
    conv_grad_in,
    out_left,
    out_right,
    conv_w,
    conv_m,
    conv_v,
    out_w,
    out_m,
    out_v,
    table_w,
    table_m,
    table_v,
    res_in,
    skip_in,
    grad_in,
    res_out,
    skip_out,
    grad_out,
    rms_out,
    conv_g,
    conv_w_new,
    conv_m_new,
    conv_v_new,
    out_g,
    out_w_new,
    out_m_new,
    out_v_new,
    table_g,
    table_w_new,
    table_m_new,
    table_v_new,
):
    f32 = jnp.float32

    def update(gradient, weight, moment, second, rate, targets):
        new = adamw(weight[...], moment[...], second[...], gradient, rate)
        for target, value in zip(targets, new):
            target[...] = value

    for source, target in ((res_in, res_out), (skip_in, skip_out), (grad_in, grad_out)):
        target[...] = source[...].astype(f32)

    taps, width = conv_grad_in.shape
    blocks = width // 128
    for block in range(blocks):
        half, lane = block // (blocks // 2), block % (blocks // 2)
        conv_g[pl.ds(lane * 2 + half, taps, stride=blocks), :] = conv_grad_in[
            :, block * 128 : (block + 1) * 128
        ].astype(f32)
    update(conv_g[...], conv_w, conv_m, conv_v, 0.03, (conv_w_new, conv_m_new, conv_v_new))

    out_g[:, 0:width] = out_left[...].astype(f32)
    out_g[:, width:] = out_right[...].astype(f32)
    update(out_g[...], out_w, out_m, out_v, 0.1, (out_w_new, out_m_new, out_v_new))

    half = width // 2
    row = lax.broadcasted_iota(jnp.int32, table_w.shape, 0) + pl.program_id(0) * table_w.shape[0]
    total = jnp.zeros(table_w.shape, f32)
    for micro in range(2):
        sums = jnp.concatenate(
            [small_ref[micro : micro + 1, 0:half], small_ref[micro : micro + 1, half:]], axis=0
        )
        total = total + jnp.where(row == speakers_ref[micro], sums[None], 0.0)
    table_g[...] = total
    update(total, table_w, table_m, table_v, 0.3, (table_w_new, table_m_new, table_v_new))

    @pl.when(pl.program_id(0) == 0)
    def _():
        counted = (lengths_ref[0] + lengths_ref[1]).astype(f32) * full
        squares = [
            jnp.sum(small_ref[8:16, part * 128 : (part + 1) * 128], axis=(0, 1), keepdims=True)
            for part in range(2)
        ]
        at = lax.broadcasted_iota(jnp.int32, (1, 2), 1)
        rms_out[...] = jnp.sqrt(jnp.where(at == 0, squares[0], squares[1]) / counted)


def run_update(lengths, speakers, small, weights, conv_parts, out_parts, table_parts, results):
    steps = 8
    width = weights.shape[1]
    gate_local, full = out_parts[0].shape[0], out_parts[0].shape[1] // 2
    f32 = jnp.float32

    def rows(value, axis=0):
        shape = list(value.shape)
        shape[axis] = pl.cdiv(shape[axis], steps)
        return pl.BlockSpec(tuple(shape), lambda i: tuple(i if at == axis else 0 for at in range(len(shape))))

    def whole(shape):
        return pl.BlockSpec(tuple(shape), lambda i: (0,) * len(shape))

    conv_block, out_block = 2 * full // steps, gate_local // steps
    left, right = 2 * full // out_block, (2 * full + gate_local) // out_block
    smem = pl.BlockSpec(memory_space=pltpu.SMEM)
    like = [jax.ShapeDtypeStruct(value.shape, f32) for value in (results[0], conv_parts[0], out_parts[0], table_parts[0])]
    specs = [rows(results[0], 1), rows(conv_parts[0]), rows(out_parts[0]), rows(table_parts[0])]
    return pl.pallas_call(
        functools.partial(update_kernel, full),
        grid=(steps,),
        out_shape=(
            *[like[0]] * 3,
            jax.ShapeDtypeStruct((1, 2), f32),
            *[like[1]] * 4,
            *[like[2]] * 4,
            *[like[3]] * 4,
        ),
        in_specs=[
            smem,
            smem,
            whole(small.shape),
            pl.BlockSpec((conv_block, width), lambda i: (i, 0)),
            pl.BlockSpec((out_block, width), lambda i: (left + i, 0)),
            pl.BlockSpec((out_block, width), lambda i: (right + i, 0)),
            *[specs[1]] * 3,
            *[specs[2]] * 3,
            *[specs[3]] * 3,
            *[specs[0]] * 3,
        ],
        out_specs=(
            *[specs[0]] * 3,
            whole((1, 2)),
            *[specs[1]] * 4,
            *[specs[2]] * 4,
            *[specs[3]] * 4,
        ),
        compiler_params=pltpu.CompilerParams(
            dimension_semantics=("arbitrary",), vmem_limit_bytes=62 * 1024 * 1024
        ),
        cost_estimate=pl.CostEstimate(
            flops=20_000_000, bytes_accessed=32_000_000, transcendentals=1_000_000
        ),
    )(
        lengths,
        speakers,
        small,
        weights,
        weights,
        weights,
        *conv_parts,
        *out_parts,
        *table_parts,
        *results,
    )


def fast_shards(
    n_seq,
    x_in,
    skip_in,
    cot_res,
    cot_skip,
    lengths,
    speakers,
    conv_weight,
    conv_m,
    conv_v,
    out_weight,
    out_m,
    out_v,
    speaker_table,
    table_m,
    table_v,
):
    views = [lane_view(value) for value in (conv_weight, conv_m, conv_v)]
    res, skipped, grads, weights, small = run_layers(
        x_in,
        skip_in,
        cot_res,
        cot_skip,
        lengths,
        speakers,
        views[0],
        out_weight[0],
        speaker_table[0],
        n_seq,
    )
    results = run_update(
        lengths,
        speakers,
        small,
        weights,
        views,
        [out_weight[0], out_m[0], out_v[0]],
        [speaker_table[0], table_m[0], table_v[0]],
        [res, skipped, grads],
    )
    wide, rms_out = results[0:3], results[3]
    conv_parts = [lane_back(value, conv_weight.shape) for value in results[4:8]]
    return (
        *[value[None] for value in wide],
        rms_out,
        *conv_parts,
        *[value[None] for value in results[8:12]],
        *[value[None] for value in results[12:16]],
    )


def shards(
    x_in,
    skip_in,
    cot_res,
    cot_skip,
    lengths,
    speakers,
    conv_weight,
    conv_m,
    conv_v,
    out_weight,
    out_m,
    out_v,
    speaker_table,
    table_m,
    table_v,
):
    micro_count, residual_local, block_length_rows = x_in.shape
    leading_section = lax.axis_index("section") == 0
    seq_index = lax.axis_index("seq")
    dilation_factor = jnp.where(leading_section, FIRST_DILATION, 1).astype(jnp.int32)
    conv_low = conv_weight[0].astype(jnp.bfloat16)
    full_res = conv_low.shape[1]
    gate_dev = conv_low.shape[3]
    speaker_rows = speaker_table.shape[1]
    conv_matrix = conv_low.reshape(2 * full_res, 2 * gate_dev)
    output_low = out_weight[0].astype(jnp.bfloat16)
    table_low = speaker_table[0].astype(jnp.bfloat16).reshape(speaker_rows, 2 * gate_dev)
    positions = seq_index * block_length_rows + jnp.arange(block_length_rows)
    contract_first = (((0,), (0,)), ((), ()))
    contract_last = (((1,), (1,)), ((), ()))
    recv_resid = jnp.zeros((residual_local, block_length_rows), jnp.float32)
    recv_skip = jnp.zeros((residual_local, block_length_rows), jnp.float32)
    kept_list = []
    resid_list = []
    skip_list = []
    square_res = jnp.float32(0.0)
    square_branch = jnp.float32(0.0)
    counted = jnp.float32(0.0)
    for tick_num in range(micro_count + 1):
        index_zero = min(tick_num, micro_count - 1)
        index_one = max(tick_num - 1, 0)
        batch_idx = jnp.where(leading_section, index_zero, index_one)
        is_live = jnp.where(leading_section, tick_num < micro_count, tick_num >= 1).astype(
            jnp.float32
        )
        residual_stream = jnp.where(
            leading_section, x_in[index_zero].astype(jnp.float32), recv_resid
        )
        skip_accumulated = jnp.where(leading_section, skip_in[index_zero], recv_skip)
        onehot = (jnp.arange(speaker_rows) == speakers[batch_idx]).astype(jnp.bfloat16)
        input_signal = residual_stream.astype(jnp.bfloat16)
        preceding_state = passed_along(
            input_signal[:, block_length_rows - FIRST_DILATION :], "seq", 1
        )
        joined_taps = jnp.concatenate([preceding_state, input_signal], axis=1)
        delayed_tap = lax.dynamic_slice_in_dim(
            joined_taps, FIRST_DILATION - dilation_factor, block_length_rows, 1
        )
        tap_rows = jnp.stack([delayed_tap, input_signal], axis=0)
        forward_tap_full = lax.all_gather(tap_rows, "mp", axis=1, tiled=True).reshape(
            2 * full_res, block_length_rows
        )
        embedding = jnp.dot(onehot, table_low, preferred_element_type=jnp.float32)
        forward_preact = (
            lax.dot_general(
                conv_matrix, forward_tap_full, contract_first, preferred_element_type=jnp.float32
            )
            + embedding[:, None]
        )
        hidden = (
            jnp.tanh(forward_preact[:gate_dev]) * jax.nn.sigmoid(forward_preact[gate_dev:])
        ).astype(jnp.bfloat16)
        partial_sums = lax.dot_general(
            output_low, hidden, contract_first, preferred_element_type=jnp.float32
        ).reshape(2, full_res, block_length_rows)
        projected = lax.psum_scatter(partial_sums, "mp", scatter_dimension=1, tiled=True)
        branch = projected[0]
        new_resid = (residual_stream + branch) * root_half
        new_skip = skip_accumulated + projected[1]
        new_resid, new_skip, branch, kept_data = (
            new_resid,
            new_skip,
            branch,
            (forward_tap_full, forward_preact, hidden),
        )
        valid_rows = (positions < lengths[batch_idx]).astype(jnp.float32)[None, :] * is_live
        square_res = square_res + jnp.sum(valid_rows * new_resid * new_resid)
        square_branch = square_branch + jnp.sum(valid_rows * branch * branch)
        counted = counted + jnp.sum(valid_rows) * residual_local
        kept_list.append(kept_data)
        resid_list.append(new_resid)
        skip_list.append(new_skip)
        if tick_num < micro_count:
            recv_resid, recv_skip = passed_along((new_resid, new_skip), "section", 1)
    square_res, square_branch, counted = lax.psum(
        (square_res, square_branch, counted), ("seq", "mp")
    )
    rms_out = jnp.stack([jnp.sqrt(square_res / counted), jnp.sqrt(square_branch / counted)])[None]
    res_out = jnp.stack(
        [
            jnp.where(leading_section, resid_list[m_idx], resid_list[m_idx + 1])
            for m_idx in range(micro_count)
        ]
    )[None]
    skip_out = jnp.stack(
        [
            jnp.where(leading_section, skip_list[m_idx], skip_list[m_idx + 1])
            for m_idx in range(micro_count)
        ]
    )[None]
    conv_acc = jnp.zeros((2 * full_res, 2 * gate_dev), jnp.float32)
    table_acc = jnp.zeros((speaker_rows, 2 * gate_dev), jnp.float32)
    out_acc = jnp.zeros((gate_dev, 2 * full_res), jnp.float32)
    recv_grad = jnp.zeros((residual_local, block_length_rows), jnp.float32)
    input_grads = []
    for tick_num in range(micro_count + 1):
        index_one = min(tick_num, micro_count - 1)
        index_zero = max(tick_num - 1, 0)
        batch_idx = jnp.where(leading_section, index_zero, index_one)
        is_live = jnp.where(leading_section, tick_num >= 1, tick_num < micro_count).astype(
            jnp.float32
        )
        valid_rows = (positions < lengths[batch_idx]).astype(jnp.float32)[None, :] * is_live
        onehot = (jnp.arange(speaker_rows) == speakers[batch_idx]).astype(jnp.bfloat16)
        kept_data = jax.tree.map(
            lambda zero_side, one_side: jnp.where(leading_section, zero_side, one_side),
            kept_list[index_zero],
            kept_list[index_one + 1],
        )
        skip_grad = (
            jnp.where(leading_section, cot_skip[index_zero], cot_skip[index_one]) * valid_rows
        )
        resid_grad = jnp.where(
            leading_section, recv_grad * is_live, cot_res[index_one] * valid_rows
        )
        tap_full, preact, hidden_used = kept_data
        proj_grad = jnp.stack([resid_grad * root_half, skip_grad], axis=0).astype(jnp.bfloat16)
        full_grad = lax.all_gather(proj_grad, "mp", axis=1, tiled=True).reshape(
            2 * full_res, block_length_rows
        )
        hidden_grad = jnp.dot(output_low, full_grad, preferred_element_type=jnp.float32)
        weight_term = lax.dot_general(
            hidden_used, full_grad, contract_last, preferred_element_type=jnp.float32
        )
        filter_act = jnp.tanh(preact[:gate_dev])
        gate_act = jax.nn.sigmoid(preact[gate_dev:])
        filter_grad = hidden_grad * gate_act * (1.0 - filter_act * filter_act)
        gate_grad = hidden_grad * filter_act * gate_act * (1.0 - gate_act)
        preact_grad = jnp.concatenate([filter_grad, gate_grad], axis=0).astype(jnp.bfloat16)
        conv_term = lax.dot_general(
            tap_full, preact_grad, contract_last, preferred_element_type=jnp.float32
        )
        column_sums = jnp.sum(preact_grad.astype(jnp.float32), axis=1)
        table_term = onehot.astype(jnp.float32)[:, None] * column_sums[None, :]
        tap_terms = jnp.dot(conv_matrix, preact_grad, preferred_element_type=jnp.float32)
        tap_gradient = lax.psum_scatter(
            tap_terms.reshape(2, full_res, block_length_rows), "mp", scatter_dimension=1, tiled=True
        )
        joined_taps_gradient = lax.dynamic_update_slice_in_dim(
            jnp.zeros((residual_local, FIRST_DILATION + block_length_rows), jnp.float32),
            tap_gradient[0],
            FIRST_DILATION - dilation_factor,
            1,
        )
        border_gradient = passed_along(joined_taps_gradient[:, :FIRST_DILATION], "seq", -1)
        input_gradient_rows = tap_gradient[1] + joined_taps_gradient[:, FIRST_DILATION:]
        input_gradient_rows = input_gradient_rows.at[:, block_length_rows - FIRST_DILATION :].add(
            border_gradient
        )
        resid_back, conv_term, weight_term, table_term = (
            resid_grad * root_half + input_gradient_rows,
            conv_term,
            weight_term,
            table_term,
        )
        conv_acc = conv_acc + conv_term
        out_acc = out_acc + weight_term
        table_acc = table_acc + table_term
        input_grads.append(resid_back)
        if tick_num < micro_count:
            recv_grad = passed_along(resid_back, "section", -1)
    grad_in = jnp.stack(
        [
            jnp.where(leading_section, input_grads[m_idx + 1], input_grads[m_idx])
            for m_idx in range(micro_count)
        ]
    )[None]
    conv_total, out_total, table_total = lax.psum((conv_acc, out_acc, table_acc), "seq")
    conv_grad = conv_total.reshape(conv_weight.shape)
    out_grad = out_total.reshape(out_weight.shape)
    table_grad = table_total.reshape(speaker_table.shape)
    conv_new, conv_m_new, conv_v_new = adamw(conv_weight, conv_m, conv_v, conv_grad, 0.03)
    out_new, out_m_new, out_v_new = adamw(out_weight, out_m, out_v, out_grad, 0.1)
    table_new, table_m_new, table_v_new = adamw(speaker_table, table_m, table_v, table_grad, 0.3)
    return (
        res_out,
        skip_out,
        grad_in,
        rms_out,
        conv_grad,
        conv_new,
        conv_m_new,
        conv_v_new,
        out_grad,
        out_new,
        out_m_new,
        out_v_new,
        table_grad,
        table_new,
        table_m_new,
        table_v_new,
    )


def solution(mesh):
    in_specs = (
        P(None, "mp", "seq"),
        P(None, "mp", "seq"),
        P(None, "mp", "seq"),
        P(None, "mp", "seq"),
        P(),
        P(),
        P("section", None, None, None, "mp"),
        P("section", None, None, None, "mp"),
        P("section", None, None, None, "mp"),
        P("section", "mp", None),
        P("section", "mp", None),
        P("section", "mp", None),
        P("section", None, None, "mp"),
        P("section", None, None, "mp"),
        P("section", None, None, "mp"),
    )
    out_specs = (
        P("section", None, "mp", "seq"),
        P("section", None, "mp", "seq"),
        P("section", None, "mp", "seq"),
        P("section", None),
        P("section", None, None, None, "mp"),
        P("section", None, None, None, "mp"),
        P("section", None, None, None, "mp"),
        P("section", None, None, None, "mp"),
        P("section", "mp", None),
        P("section", "mp", None),
        P("section", "mp", None),
        P("section", "mp", None),
        P("section", None, None, "mp"),
        P("section", None, None, "mp"),
        P("section", None, None, "mp"),
        P("section", None, None, "mp"),
    )
    n_seq = mesh.shape["seq"]
    fits = mesh.shape["mp"] == 2 and n_seq in (4, 8, 16)
    return jax.shard_map(
        functools.partial(fast_shards, n_seq) if fits else shards,
        mesh=mesh,
        in_specs=in_specs,
        out_specs=out_specs,
        check_vma=False,
    )
```

```python
import functools
import math

import jax
import jax.numpy as jnp
from jax import lax
from jax.experimental import pallas as pl
from jax.experimental.pallas import tpu as pltpu
from jax.sharding import PartitionSpec as P

FIRST_DILATION = 512
STEP = 10
MESH = pl.DeviceIdType.MESH
TILE = 256
UNITS = 3
Z_FIRST = 1

beta_one = 0.9
beta_two = 0.999
adam_eps = 1e-08
decay_rate = 0.01
root_half = math.sqrt(0.5)


def passed_along(value, axis, steps):
    count = lax.axis_size(axis)
    first, last = (max(0, -steps), min(count, count - steps))
    return lax.ppermute(value, axis, [(source, source + steps) for source in range(first, last)])


def adamw(weight, moment, second, gradient, step_rate):
    moment_new = beta_one * moment + (1.0 - beta_one) * gradient
    second_new = beta_two * second + (1.0 - beta_two) * gradient * gradient
    corr_one = 1.0 - beta_one**STEP
    corr_two = 1.0 - beta_two**STEP
    update = moment_new / corr_one / (jnp.sqrt(second_new / corr_two) + adam_eps)
    weight_new = weight - step_rate * (update + decay_rate * weight)
    return (weight_new, moment_new, second_new)


def dot(left, right):
    return jnp.dot(left, right, preferred_element_type=jnp.float32)


def dot_last(left, right):
    return lax.dot_general(
        left, right, (((1,), (1,)), ((), ())), preferred_element_type=jnp.float32
    )


def rows_at(start, size):
    return pl.ds(start if isinstance(start, int) else pl.multiple_of(start, 16), size)


def cols_at(start, size):
    return pl.ds(start if isinstance(start, int) else pl.multiple_of(start, 128), size)


def layers_kernel(
    sizes,
    x_ref,
    skip_ref,
    cot_res_ref,
    cot_skip_ref,
    lengths_ref,
    speakers_ref,
    conv_ref,
    out_ref,
    table_ref,
    res_ref,
    skipped_ref,
    grad_ref,
    weight_ref,
    small_ref,
    conv_wide,
    out_wide,
    table_wide,
    xf,
    wc,
    wct,
    wo,
    wot,
    et,
    in1,
    next_out,
    next_in,
    past1,
    act_f,
    act_q,
    hid,
    dproj,
    dres0,
    dpre,
    grad1,
    past_grad1,
    edge_out,
    edge_in,
    res0,
    skip_sum,
    cot_a,
    cot_b,
    skip_low,
    res_low,
    grad1_low,
    grad0,
    past0_out,
    past0_in,
    grad0_low,
    stats,
    acc,
    from_core,
    down,
    final,
    small,
    small_in,
    small_sum,
    send_sem,
    recv_sem,
    local_sem,
):
    full, local, gates, span, n_seq = sizes
    gate_local = gates // 2
    width = 2 * gate_local
    halo = FIRST_DILATION
    n_z = n_seq // 2
    c = lax.axis_index("section")
    s = lax.axis_index("seq")
    x = lax.axis_index("mp")
    z, y = s // 2, s % 2
    oc, ox = 1 - c, 1 - x
    bf16, f32 = jnp.bfloat16, jnp.float32
    counts = {"send": 0, "recv": 0, "local": 0}
    pending = []
    inside = [None]

    def take(kind, amount=1):
        counts[kind] += amount
        return counts[kind] - amount

    def when(cond, action):
        if cond is None:
            action()
        else:
            pl.when(cond)(action)

    def on(cond, action):
        inside[0] = cond
        pl.when(cond)(lambda: action())
        inside[0] = None

    def send(source, target, device, recv_at, cond=None):
        at = take("send")

        def make():
            return pltpu.make_async_remote_copy(
                src_ref=source(),
                dst_ref=target(),
                send_sem=send_sem.at[at],
                recv_sem=recv_sem.at[recv_at()],
                device_id=device(),
                device_id_type=MESH,
            )

        when(cond, lambda: make().start())
        pending.append((lambda: make().wait_send(), inside[0] if cond is None else cond))

    def arrive(target, recv_at, cond=None):
        when(
            cond,
            lambda: pltpu.make_async_remote_copy(
                src_ref=target,
                dst_ref=target,
                send_sem=send_sem.at[0],
                recv_sem=recv_sem.at[recv_at],
                device_id={"section": oc},
                device_id_type=MESH,
            ).wait_recv(),
        )

    def fetch(source, target, cond=None):
        copy = pltpu.make_async_copy(source, target, local_sem.at[take("local")])
        when(cond, copy.start)
        return copy

    def to(axis, index):
        return lambda: {axis: index()}

    core_dev = to("section", lambda: 1 - c)
    mp_dev = to("mp", lambda: 1 - x)
    y_dev = to("seq", lambda: z * 2 + 1 - y)
    prev_dev, next_dev = to("seq", lambda: s - 1), to("seq", lambda: s + 1)
    has_prev, has_next = s > 0, s < n_seq - 1

    z_seqs = [lax.rem(z + step, n_z) * 2 + y for step in range(n_z)]

    def z_seq(step):
        return z_seqs[step]

    def z_dev(step):
        return to("seq", lambda: z_seq(step))

    bits = [y] + [(z // (1 << bit)) % 2 for bit in range((n_seq // 2).bit_length() - 1)]
    pairs = [z * 2 + 1 - y] + [
        (z + (1 - 2 * bits[bit + 1]) * (1 << bit)) * 2 + y for bit in range(len(bits) - 1)
    ]
    depth = len(bits)
    pair_devs = [to("seq", lambda way=way: pairs[way]) for way in range(depth)]

    barrier = pltpu.get_barrier_semaphore()
    for device in [core_dev, mp_dev, y_dev, *[z_dev(step) for step in range(1, n_z)]]:
        pl.semaphore_signal(barrier, inc=1, device_id=device(), device_id_type=MESH)
    before, after = (y == 0) & (z > 0), (y == 1) & (z < n_z - 1)

    @pl.when(before)
    def _():
        pl.semaphore_signal(barrier, inc=1, device_id=prev_dev(), device_id_type=MESH)

    @pl.when(after)
    def _():
        pl.semaphore_signal(barrier, inc=1, device_id=next_dev(), device_id_type=MESH)

    own_rows, other_rows = rows_at(x * local, local), rows_at(ox * local, local)
    got_conv = fetch(conv_ref, conv_wide)
    chunks = span // halo
    got_x = [
        fetch(x_ref.at[c, :, pl.ds(chunk * halo, halo)], xf.at[chunk + 1, own_rows])
        for chunk in reversed(range(chunks))
    ]
    got_table = fetch(table_ref, table_wide)
    got_out = fetch(out_ref, out_wide)

    def cast_conv(step, carry):
        for block in range(width // 128):
            half, lane = block // (gate_local // 128), block % (gate_local // 128)
            first = step * 256 * (width // 128) + lane * 2 + half
            wc[c, x, rows_at(step * 256, 256), pl.ds(block * 128, 128)] = conv_wide[
                pl.ds(first, 256, stride=width // 128), :
            ].astype(bf16)
        return carry

    got_conv.wait()
    got_cot_a = fetch(cot_res_ref.at[c], cot_a)
    got_cot_b = fetch(cot_skip_ref.at[c], cot_b)
    got_skip = fetch(skip_ref.at[c], skip_sum)
    lax.fori_loop(0, 2 * full // 256, cast_conv, None)
    got_table.wait()
    marks = lax.broadcasted_iota(jnp.int32, (16, width), 0)
    emb = jnp.zeros((16, width), f32)
    for micro in range(2):
        rows = table_wide[speakers_ref[micro]]
        row = jnp.concatenate([rows[0:1, :], rows[1:2, :]], axis=1)
        emb = jnp.where(marks == micro, row, emb)
    wc[c, x, 2 * full : 2 * full + 16, :] = emb.astype(bf16)
    got_out.wait()
    wo[c, rows_at(x * gate_local, gate_local), :] = out_wide[...].astype(bf16)

    @pl.when(before | after)
    def _():
        pl.semaphore_wait(barrier, 3 + n_z)

    @pl.when(jnp.logical_not(before | after))
    def _():
        pl.semaphore_wait(barrier, 2 + n_z)

    conv_rows, out_rows = 2 * full // n_seq, gate_local // n_seq
    conv_at, conv_core_at = take("recv", n_seq), take("recv", n_seq)
    out_at, emb_at = take("recv", n_seq), take("recv")

    def conv_slice(index, layer, block):
        return wc.at[layer, block, rows_at(index * conv_rows, conv_rows)]

    def out_slice(index, layer, block):
        return wo.at[layer, rows_at(block * gate_local + index * out_rows, out_rows)]

    def emb_part(layer, block):
        return wc.at[layer, block, 2 * full : 2 * full + 16]

    def conv_block(layer, block):
        return wc.at[layer, block, 0 : 2 * full]

    def out_block(layer, block):
        return wo.at[layer, rows_at(block * gate_local, gate_local)]

    def send_same(ref, device, recv_at, cond=None):
        send(ref, ref, device, recv_at, cond)

    def cross_weights():
        send_same(lambda: conv_slice(s, c, x), mp_dev, lambda: conv_at + s)
        send_same(lambda: emb_part(c, x), mp_dev, lambda: emb_at)
        send_same(lambda: out_slice(s, c, x), mp_dev, lambda: out_at + s)

    on(c == 0, cross_weights)
    x_at = [take("recv") for _ in range(chunks)]
    for copy in got_x:
        copy.wait()
    for chunk in reversed(range(chunks)):
        send_same(
            lambda chunk=chunk: xf.at[chunk + 1, own_rows], mp_dev, lambda chunk=chunk: x_at[chunk]
        )
    on(c == 1, cross_weights)
    halo_at = [take("recv"), take("recv")]
    send(
        lambda: xf.at[chunks, own_rows],
        lambda: xf.at[0, own_rows],
        next_dev,
        lambda: halo_at[0],
        has_next,
    )
    core_at = [take("recv") for _ in range(5)]
    send_same(lambda: conv_block(c, x), core_dev, lambda: core_at[0])
    send_same(lambda: emb_part(c, x), core_dev, lambda: core_at[1])
    send_same(lambda: out_block(c, x), core_dev, lambda: core_at[2])

    @pl.when(s == 0)
    def _():
        xf[0] = jnp.zeros((full, halo), bf16)
        next_in[...] = jnp.zeros(next_in.shape, bf16)

    @pl.when(s == n_seq - 1)
    def _():
        past0_in[...] = jnp.zeros(past0_in.shape, bf16)
        edge_in[...] = jnp.zeros(edge_in.shape, bf16)

    stats[...] = jnp.zeros(stats.shape, f32)
    length = lengths_ref[c]

    def valid_at(start, size):
        at = s * span + start + lax.broadcasted_iota(jnp.int32, (1, size), 1)
        return jnp.where(at < length, 1.0, 0.0).astype(f32)

    def cast_cotangents(step, carry):
        at = cols_at(step * TILE, TILE)
        valid = valid_at(step * TILE, TILE)
        dproj[step, own_rows, :] = (cot_a[:, at] * valid * root_half).astype(bf16)
        dproj[step, rows_at(full + x * local, local), :] = (cot_b[:, at] * valid).astype(bf16)
        return carry

    tiles = span // TILE
    got_cot_a.wait()
    got_cot_b.wait()
    lax.fori_loop(0, tiles, cast_cotangents, None)
    cot_at = take("recv", 2 * tiles)

    def cot_piece(tile, part, block):
        return dproj.at[tile, rows_at(part * full + block * local, local)]

    for tile in range(tiles):
        for part in range(2):
            send_same(
                functools.partial(cot_piece, tile, part, x),
                mp_dev,
                lambda tile=tile, part=part: cot_at + tile * 2 + part,
            )

    def turn_conv(layer, block, first, rows):
        wct[layer, rows_at(block * width, width), cols_at(first, rows)] = wc[
            layer, block, rows_at(first, rows), :
        ].T

    def turn_rest(layer, block):
        values = wc[layer, block, 2 * full : 2 * full + 16, :].astype(f32)
        mark_row = lax.broadcasted_iota(jnp.int32, values.shape, 0)
        picked = jnp.sum(jnp.where(mark_row == c, values, 0.0), axis=0, keepdims=True)
        et[layer, rows_at(block * width, width), :] = jnp.broadcast_to(picked, (128, width)).T

        for part, start in enumerate((x * local, full + x * local, ox * local)):
            wot[layer, part * local : (part + 1) * local, cols_at(block * gate_local, gate_local)] = wo[
                layer, rows_at(block * gate_local, gate_local), cols_at(start, local)
            ].T

    def turn_all(layer, block):
        for step in range(2 * full // TILE):
            turn_conv(layer, block, step * TILE, TILE)
        turn_rest(layer, block)

    def spread_first():
        arrive(conv_slice(s, c, ox), conv_at + s)
        for step in range(1, n_z):
            send_same(lambda: conv_slice(s, c, ox), z_dev(step), lambda: conv_at + s)
        send_same(lambda: conv_slice(s, c, ox), y_dev, lambda: conv_at + s)
        send_same(lambda: conv_slice(s, c, ox), core_dev, lambda: conv_core_at + s)
        arrive(emb_part(c, ox), emb_at)
        send_same(lambda: emb_part(c, ox), core_dev, lambda: core_at[3])
        arrive(out_slice(s, c, ox), out_at + s)
        for step in range(1, n_z):
            send_same(lambda: out_slice(s, c, ox), z_dev(step), lambda: out_at + s)
        send_same(lambda: out_slice(s, c, ox), y_dev, lambda: out_at + s)

    def spread_conv():
        for step in range(1, n_z):
            arrive(conv_slice(z_seq(step), c, ox), conv_at + z_seq(step))
            here = functools.partial(lambda step: conv_slice(z_seq(step), c, ox), step)
            send_same(here, y_dev, lambda step=step: conv_at + z_seq(step))
            send_same(here, core_dev, lambda step=step: conv_core_at + z_seq(step))

    def spread_out():
        for step in range(1, n_z):
            arrive(out_slice(z_seq(step), c, ox), out_at + z_seq(step))
            here = functools.partial(lambda step: out_slice(z_seq(step), c, ox), step)
            send_same(here, y_dev, lambda step=step: out_at + z_seq(step))

    def spread_last():
        for step in range(n_z):
            arrive(conv_slice(z_seq(step) + 1 - 2 * y, c, ox), conv_at + z_seq(step) + 1 - 2 * y)
            here = functools.partial(
                lambda step: conv_slice(z_seq(step) + 1 - 2 * y, c, ox), step
            )
            send_same(here, core_dev, lambda step=step: conv_core_at + z_seq(step) + 1 - 2 * y)
        for step in range(n_z):
            arrive(out_slice(z_seq(step) + 1 - 2 * y, c, ox), out_at + z_seq(step) + 1 - 2 * y)
        send_same(lambda: out_block(c, ox), core_dev, lambda: core_at[4])

    def all_from_core():
        for step in range(n_seq):
            arrive(conv_slice(step, oc, ox), conv_core_at + step)
        arrive(emb_part(oc, ox), core_at[3])
        arrive(out_block(oc, ox), core_at[4])

    on(c == 0, spread_first)

    @pl.when(c == 0)
    def _():
        turn_all(0, x)

    arrive(xf.at[chunks, other_rows], x_at[chunks - 1])
    send(
        lambda: xf.at[chunks, other_rows],
        lambda: xf.at[0, other_rows],
        next_dev,
        lambda: halo_at[1],
        has_next,
    )
    on(c == 0, spread_conv)
    arrive(conv_block(oc, x), core_at[0])
    arrive(emb_part(oc, x), core_at[1])
    arrive(out_block(oc, x), core_at[2])

    @pl.when(c == 1)
    def _():
        turn_all(0, x)

    on(c == 0, spread_out)
    turn_all(1, x)
    on(c == 0, spread_last)

    on(c == 1, all_from_core)
    turn_all(0, ox)

    def fold(values):
        total = jnp.sum(values.reshape(local // 8, 8, TILE), axis=0)
        return sum(total[:, part * 128 : (part + 1) * 128] for part in range(TILE // 128))

    def gated(layer, pre, at):
        halves = []
        for block in range(2):
            base = block * width
            shift = et[layer, base : base + width, :]
            shift = jnp.concatenate([shift] * (TILE // 128), axis=1)
            f = jnp.tanh(pre[base : base + gate_local] + shift[:gate_local])
            q = 0.5 * jnp.tanh(
                0.5 * (pre[base + gate_local : base + width] + shift[gate_local:])
            ) + 0.5
            rows = slice(block * gate_local, (block + 1) * gate_local)
            act_f[layer, rows, at] = f
            act_q[layer, rows, at] = q
            halves.append((f * q).astype(bf16))
            hid[layer, rows, at] = halves[-1]
        return jnp.concatenate(halves, axis=0)

    def forward0(step):
        start = step * TILE
        at = cols_at(start, TILE)
        chunk, inner = start // halo, pl.ds(start % halo, TILE)
        pre = dot(wct[0], jnp.concatenate([xf[chunk, :, inner], xf[chunk + 1, :, inner]], axis=0))
        hidden = gated(0, pre, at)
        valid = valid_at(start, TILE)
        proj = dot(wot[0], hidden)
        branch = proj[0:local]
        res = (xf[chunk + 1, own_rows, inner].astype(f32) + branch) * root_half
        res0[:, at] = res
        in1[own_rows, at] = res.astype(bf16)
        stats[0, 0] += fold(valid * res * res)
        stats[0, 1] += fold(valid * branch * branch)
        res = (xf[chunk + 1, other_rows, inner].astype(f32) + proj[2 * local :]) * root_half
        in1[other_rows, at] = res.astype(bf16)
        total = skip_sum[:, at] + proj[local : 2 * local]
        skip_sum[:, at] = total
        skip_low[0, :, at] = total.astype(bf16)

    late_tiles = (span - halo) // TILE
    got_skip.wait()
    for chunk in range(chunks - 1):
        arrive(xf.at[chunk + 1, other_rows], x_at[chunk])
    on(c == 1, spread_first)
    for step in range(late_tiles, tiles):
        forward0(step)
    in1_at = take("recv")
    next_out[...] = in1[:, span - 128 : span]
    send(
        lambda: next_out,
        lambda: next_in,
        next_dev,
        lambda: in1_at,
        has_next,
    )
    on(c == 1, spread_conv)
    on(c == 1, spread_out)
    arrive(xf.at[0, own_rows], halo_at[0], has_prev)
    arrive(xf.at[0, other_rows], halo_at[1], has_prev)
    for step in range(late_tiles):
        forward0(step)
    on(c == 1, spread_last)

    result_at = [take("recv") for _ in range(3)]
    locals_pending = []

    def give(layer, kind, source, target):
        copy = fetch(source, target.at[c], c == layer)
        locals_pending.append((copy, c == layer))
        send(lambda: source, lambda: target.at[c], core_dev, lambda: result_at[kind], c != layer)

    give(0, 0, in1.at[own_rows], res_ref)
    give(0, 1, skip_low.at[0], skipped_ref)

    on(c == 0, all_from_core)
    turn_all(1, ox)

    def forward1(step):
        start = step * TILE
        at = cols_at(start, TILE)
        for base in range(0, full, 256):
            rows = slice(base, base + 256)
            if start == 0:
                wide = jnp.concatenate([next_in[rows, :], in1[rows, 0:TILE]], axis=1).astype(f32)
            else:
                wide = in1[rows, start - 128 : start + TILE].astype(f32)
            past1[base : base + 256, at] = pltpu.roll(wide, 1, 1)[:, 128:].astype(bf16)
        pre = dot(wct[1], jnp.concatenate([past1[:, at], in1[:, at]], axis=0))
        hidden = gated(1, pre, at)
        valid = valid_at(start, TILE)
        proj = dot(wot[1, 0 : 2 * local], hidden)
        branch = proj[0:local]
        res = (res0[:, at] + branch) * root_half
        res_low[:, at] = res.astype(bf16)
        stats[1, 0] += fold(valid * res * res)
        stats[1, 1] += fold(valid * branch * branch)
        total = skip_sum[:, at] + proj[local:]
        skip_low[1, :, at] = total.astype(bf16)

    arrive(next_in, in1_at, has_prev)
    for step in range(tiles):
        forward1(step)
    give(1, 0, res_low, res_ref)
    give(1, 1, skip_low.at[1], skipped_ref)

    def through_gates(layer, dhidden, at):
        for block in range(2):
            rows = slice(block * gate_local, (block + 1) * gate_local)
            f, q = act_f[layer, rows, at], act_q[layer, rows, at]
            d = dhidden[rows] * q
            base = block * width
            dpre[layer, base : base + gate_local, at] = (d * (1.0 - f * f)).astype(bf16)
            dpre[layer, base + gate_local : base + width, at] = (d * f * (1.0 - q)).astype(bf16)

    def backward1(step):
        at = cols_at(step * TILE, TILE)
        through_gates(1, dot(wo[1], dproj[step]), at)
        both = jnp.concatenate([wc[1, block, 0 : 2 * full, :] for block in range(2)], axis=1)
        taps = dot(both, dpre[1, :, at])
        past_grad1[:, at] = taps[0:full]
        grad1[:, at] = taps[full:] + dproj[step, 0:full, :].astype(f32)

    def join1(step):
        start = step * TILE
        at = cols_at(start, TILE)
        for base in range(0, full, 256):
            rows = slice(base, base + 256)
            wide = past_grad1[rows, cols_at(start, TILE + 128)]
            total = grad1[rows, at] + pltpu.roll(wide, TILE + 127, 1)[:, 0:TILE]
            grad1[rows, at] = total
            dres0[rows, at] = (root_half * total).astype(bf16)
        own = grad1[own_rows, at]
        grad1_low[:, at] = own.astype(bf16)
        grad0[:, at] = root_half * own

    def backward0(step):
        start = step * TILE
        at = cols_at(start, TILE)
        dhidden = dot(wo[0], jnp.concatenate([dres0[:, at], dproj[step, full:, :]], axis=0))
        through_gates(0, dhidden, at)
        own = [
            jnp.concatenate([wc[0, block, rows, :] for block in range(2)], axis=1)
            for rows in (own_rows, rows_at(full + x * local, local))
        ]
        taps = dot(jnp.concatenate(own, axis=0), dpre[0, :, at])
        grad0[:, at] += taps[local:]
        return taps[0:local]

    edge_at, past0_at = take("recv"), take("recv")
    early_tiles = halo // TILE

    for step in range(tiles):
        for part in range(2):
            arrive(cot_piece(step, part, ox), cot_at + step * 2 + part)
        tile = step - (tiles - early_tiles)
        if tile >= 0:
            join1(tile)
        backward1(step)
        if tile >= 0:
            past0_out[:, cols_at(tile * TILE, TILE)] = backward0(tile).astype(bf16)
        if step == 0:
            edge_out[...] = past_grad1[:, 0:128].astype(bf16)
            send(lambda: edge_out, lambda: edge_in, prev_dev, lambda: edge_at, has_prev)
    send(lambda: past0_out, lambda: past0_in, prev_dev, lambda: past0_at, has_prev)

    total_rows = 3 * full
    unit_rows = total_rows // UNITS
    unit_core_at = [take("recv") for _ in range(UNITS)]
    down_at = [[take("recv") for _ in range(depth)] for _ in range(UNITS)]
    up_at = [[take("recv") for _ in range(depth)] for _ in range(UNITS)]
    small_at = [take("recv") for _ in range(2 + depth)]
    stored_at = take("local", UNITS + 1)

    def to_core(layer, first, size):
        for unit in range(first // unit_rows, (first + size) // unit_rows):
            rows = pl.ds(unit * unit_rows, unit_rows)
            send(
                lambda rows=rows: acc.at[layer, rows],
                lambda rows=rows: from_core.at[rows],
                core_dev,
                lambda unit=unit: unit_core_at[unit],
                c != layer,
            )

    def unit_conv(layer, past, now):
        taps = jnp.concatenate([past, now, jnp.ones((16, span), bf16)], axis=0)
        product = dot_last(taps, dpre[layer, rows_at(x * width, width), :])
        acc[layer, 0 : 2 * full, :] = product[0 : 2 * full].astype(bf16)
        sums = product[2 * full : 2 * full + 8]
        mark = lax.broadcasted_iota(jnp.int32, sums.shape, 0)
        small[layer, 0:8, :] = jnp.where(mark == c, sums, 0.0)
        small[layer, 8:16, :] = jnp.zeros((8, width), f32)
        small[layer, 8:16, 0:128] = stats[layer, 0]
        small[layer, 8:16, 128:256] = stats[layer, 1]
        to_core(layer, 0, 2 * full)
        send(
            lambda: small.at[layer],
            lambda: small_in.at[0],
            core_dev,
            lambda: small_at[0],
            c != layer,
        )

    def unit_out(layer, parts):
        hidden = hid[layer, rows_at(x * gate_local, gate_local), :]
        product = dot_last(jnp.concatenate(parts, axis=0), hidden)
        for part in range(2):
            acc[layer, pl.ds(2 * full, full), pl.ds(part * gate_local, gate_local)] = product[
                part * full : (part + 1) * full
            ].astype(bf16)
        to_core(layer, 2 * full, full)

    n_stages = 2 * depth + 1

    def order(unit):
        ways = list(range(depth))
        return [1, 0, *ways[2:]] if unit == Z_FIRST and depth > 1 else ways

    def kept(unit, level, flip=False):
        start, size = unit * unit_rows, unit_rows
        for step in range(level):
            size //= 2
            bit = bits[order(unit)[step]]
            if flip and step == level - 1:
                bit = 1 - bit
            start = start + bit * size
        return rows_at(start, size)

    def landing(unit, level):
        size = unit_rows >> level
        return pl.ds(unit * unit_rows + unit_rows - 2 * size, size)

    def unit_stage(layer, unit, stage):
        ways = order(unit)
        if stage <= depth:
            here = kept(unit, stage)
            if stage == 0:
                arrive(from_core.at[here], unit_core_at[unit])
                other = from_core[here, :]
            else:
                place = landing(unit, stage)
                arrive(down.at[place], down_at[unit][stage - 1])
                other = down[place, :]
            total = (acc[layer, here, :].astype(f32) + other.astype(f32)).astype(bf16)
            if stage < depth:
                acc[layer, here, :] = total
                send(
                    lambda: acc.at[layer, kept(unit, stage + 1, True)],
                    lambda: down.at[landing(unit, stage + 1)],
                    pair_devs[ways[stage]],
                    lambda: down_at[unit][stage],
                )
                return
            final[here, :] = total
        if stage > depth:
            level = 2 * depth + 1 - stage
            arrive(final.at[kept(unit, level, True)], up_at[unit][level - 1])
        level = 2 * depth - stage
        if level > 0:
            send_same(
                lambda: final.at[kept(unit, level)],
                pair_devs[ways[level - 1]],
                lambda: up_at[unit][level - 1],
            )
        else:
            here = pl.ds(unit * unit_rows, unit_rows)
            pltpu.make_async_copy(
                final.at[here], weight_ref.at[here], local_sem.at[stored_at + unit]
            ).start()

    def small_stage(layer, stage):
        names = [core_dev, mp_dev, *pair_devs]
        arrive(small_in.at[stage], small_at[stage])
        if stage == 0:
            small_sum[0] = small[layer] + small_in[0]
        else:
            sums = small_sum[stage - 1, 0:8, :]
            small_sum[stage, 0:8, :] = sums if stage == 1 else sums + small_in[stage, 0:8, :]
            small_sum[stage, 8:16, :] = small_sum[stage - 1, 8:16, :] + small_in[stage, 8:16, :]
        if stage < len(names) - 1:
            send(
                lambda: small_sum.at[stage],
                lambda: small_in.at[stage + 1],
                names[stage + 1],
                lambda: small_at[stage + 1],
            )
        else:
            pltpu.make_async_copy(
                small_sum.at[stage], small_ref, local_sem.at[stored_at + UNITS]
            ).start()

    def in_order_of_arrival(layer, first_stage, units):
        ready = [(float(at), at, unit, first_stage) for at, unit in enumerate(units)]
        free = [0.0] * depth
        clock, small_next = 0.0, 0
        while ready:
            ready.sort()
            at, rank, unit, stage = ready.pop(0)
            unit_stage(layer, unit, stage)
            clock = max(clock, at) + 0.25
            if stage < n_stages - 1:
                way = order(unit)[min(stage, 2 * depth - 1 - stage)]
                level = min(stage, 2 * depth - 1 - stage)
                free[way] = max(free[way], clock) + 3.0 / 2**level * (2 if way == 2 else 1)
                ready.append((free[way] + 1.0, rank, unit, stage + 1))
            if stage == n_stages - 1 or stage == 2:
                if small_next < 2 + depth:
                    small_stage(layer, small_next)
                    small_next += 1
        for stage in range(small_next, 2 + depth):
            small_stage(layer, stage)

    unit_order = [2, 0, 1]

    def all_times(first):
        rows = slice(first, first + full)
        return jnp.concatenate([dproj[tile, rows, :] for tile in range(tiles)], axis=1)

    unit_out(1, [all_times(0), all_times(full)])
    unit_conv(1, past1[...], in1[...])

    arrive(edge_in, edge_at, has_next)
    past_grad1[:, span : span + 128] = edge_in[...].astype(f32)

    def start_sums(layer):
        for unit in unit_order:
            unit_stage(layer, unit, 0)

    for step in range(early_tiles, tiles):
        join1(step)
    for step in range(early_tiles, tiles):
        grad0[:, cols_at(step * TILE - halo, TILE)] += backward0(step)
        if step == early_tiles:
            on(c == 1, lambda: start_sums(1))
    give(1, 2, grad1_low, grad_ref)
    unit_out(0, [dres0[...], all_times(full)])
    unit_conv(
        0,
        jnp.concatenate([xf[chunk] for chunk in range(chunks)], axis=1),
        jnp.concatenate([xf[chunk + 1] for chunk in range(chunks)], axis=1),
    )

    arrive(past0_in, past0_at, has_next)

    def join0(step, carry):
        at = cols_at(step * TILE, TILE)
        grad0_low[:, at] = grad0[:, at].astype(bf16)
        return carry

    lax.fori_loop(0, (span - halo) // TILE, join0, None)

    def join0_late(step, carry):
        at = cols_at(step * TILE + span - halo, TILE)
        grad0_low[:, at] = (
            grad0[:, at] + past0_in[:, cols_at(step * TILE, TILE)].astype(f32)
        ).astype(bf16)
        return carry

    lax.fori_loop(0, halo // TILE, join0_late, None)
    give(0, 2, grad0_low, grad_ref)

    on(c == 0, lambda: start_sums(0))
    for wait, cond in pending:
        when(cond, wait)
    pending.clear()
    on(c == 0, lambda: in_order_of_arrival(0, 1, unit_order))
    on(c == 1, lambda: in_order_of_arrival(1, 1, unit_order))
    for unit in range(UNITS):
        here = pl.ds(unit * unit_rows, unit_rows)
        pltpu.make_async_copy(
            final.at[here], weight_ref.at[here], local_sem.at[stored_at + unit]
        ).wait()
    pltpu.make_async_copy(
        small_sum.at[1 + depth], small_ref, local_sem.at[stored_at + UNITS]
    ).wait()
    for kind, target in enumerate((res_ref, skipped_ref, grad_ref)):
        arrive(target.at[oc], result_at[kind])
    for copy, cond in locals_pending:
        when(cond, copy.wait)
    for wait, cond in pending:
        when(cond, wait)
    assert counts["send"] <= send_sem.shape[0], counts
    assert counts["recv"] <= recv_sem.shape[0], counts
    assert counts["local"] <= local_sem.shape[0], counts


def run_layers(
    x_in, skip_in, cot_res, cot_skip, lengths, speakers, conv_view, out_weight, table, n_seq
):
    micro, local, span = x_in.shape
    full = out_weight.shape[1] // 2
    gate_local = out_weight.shape[0]
    gates = 2 * gate_local
    bf16, f32 = jnp.bfloat16, jnp.float32
    halo = FIRST_DILATION
    rows = 3 * full
    depth = (n_seq // 2).bit_length()
    width = 2 * gate_local
    any_spec = pl.BlockSpec(memory_space=pl.ANY)
    scratch = [
        (conv_view.shape, f32),
        (out_weight.shape, f32),
        (table.shape, f32),
        ((span // halo + 1, full, halo), bf16),
        ((2, 2, 2 * full + 16, width), bf16),
        ((2, 2 * width, 2 * full), bf16),
        ((2, gates, 2 * full), bf16),
        ((2, 3 * local, gates), bf16),
        ((2, 2 * width, 128), f32),
        ((full, span), bf16),
        ((full, 128), bf16),
        ((full, 128), bf16),
        ((full, span), bf16),
        ((2, gates, span), f32),
        ((2, gates, span), f32),
        ((2, gates, span), bf16),
        ((span // TILE, 2 * full, TILE), bf16),
        ((full, span), bf16),
        ((2, 2 * width, span), bf16),
        ((full, span), f32),
        ((full, span + 128), f32),
        ((full, 128), bf16),
        ((full, 128), bf16),
        ((local, span), f32),
        ((local, span), f32),
        ((local, span), f32),
        ((local, span), f32),
        ((2, local, span), bf16),
        ((local, span), bf16),
        ((local, span), bf16),
        ((local, span), f32),
        ((local, halo), bf16),
        ((local, halo), bf16),
        ((local, span), bf16),
        ((2, 2, 8, 128), f32),
        ((2, rows, width), bf16),
        ((rows, width), bf16),
        ((rows, width), bf16),
        ((rows, width), bf16),
        ((2, 16, width), f32),
        ((2 + depth, 16, width), f32),
        ((2 + depth, 16, width), f32),
    ]
    result = jax.ShapeDtypeStruct((micro, local, span), bf16)
    return pl.pallas_call(
        functools.partial(layers_kernel, (full, local, gates, span, n_seq)),
        out_shape=(
            result,
            result,
            result,
            jax.ShapeDtypeStruct((rows, width), bf16),
            jax.ShapeDtypeStruct((16, width), f32),
        ),
        in_specs=[any_spec] * 4 + [pl.BlockSpec(memory_space=pltpu.SMEM)] * 2 + [any_spec] * 3,
        out_specs=[any_spec] * 5,
        scratch_shapes=[pltpu.VMEM(shape, kind) for shape, kind in scratch]
        + [
            pltpu.SemaphoreType.DMA((224,)),
            pltpu.SemaphoreType.DMA((144,)),
            pltpu.SemaphoreType.DMA((32,)),
        ],
        compiler_params=pltpu.CompilerParams(
            collective_id=0, has_side_effects=True, vmem_limit_bytes=62 * 1024 * 1024
        ),
        cost_estimate=pl.CostEstimate(
            flops=14_000_000_000, bytes_accessed=20_000_000, transcendentals=2_000_000
        ),
    )(x_in, skip_in, cot_res, cot_skip, lengths, speakers, conv_view, out_weight, table)


def lane_view(value):
    _, taps, full, halves, gate_local = value.shape
    blocks = gate_local // 128
    value = value.reshape(taps * full, halves, blocks, 128).transpose(0, 2, 1, 3)
    return value.reshape(taps * full * halves * blocks, 128)


def lane_back(value, shape):
    _, taps, full, halves, gate_local = shape
    blocks = gate_local // 128
    value = value.reshape(taps * full, blocks, halves, 128).transpose(0, 2, 1, 3)
    return value.reshape(shape)


def update_kernel(
    full,
    lengths_ref,
    speakers_ref,
    small_ref,
    conv_grad_in,
    out_grad_in,
    conv_w,
    conv_m,
    conv_v,
    out_w,
    out_m,
    out_v,
    table_w,
    table_m,
    table_v,
    res_in,
    skip_in,
    grad_in,
    res_out,
    skip_out,
    grad_out,
    rms_out,
    conv_g,
    conv_w_new,
    conv_m_new,
    conv_v_new,
    out_g,
    out_w_new,
    out_m_new,
    out_v_new,
    table_g,
    table_w_new,
    table_m_new,
    table_v_new,
):
    f32 = jnp.float32

    def update(gradient, weight, moment, second, rate, targets):
        new = adamw(weight[...], moment[...], second[...], gradient, rate)
        for target, value in zip(targets, new):
            target[...] = value

    for source, target in ((res_in, res_out), (skip_in, skip_out), (grad_in, grad_out)):
        target[...] = source[...].astype(f32)

    taps, width = conv_grad_in.shape
    blocks = width // 128
    for block in range(blocks):
        half, lane = block // (blocks // 2), block % (blocks // 2)
        conv_g[pl.ds(lane * 2 + half, taps, stride=blocks), :] = conv_grad_in[
            :, block * 128 : (block + 1) * 128
        ].astype(f32)
    update(conv_g[...], conv_w, conv_m, conv_v, 0.03, (conv_w_new, conv_m_new, conv_v_new))

    out_g[...] = out_grad_in[...].astype(f32).T
    update(out_g[...], out_w, out_m, out_v, 0.1, (out_w_new, out_m_new, out_v_new))

    half = width // 2
    row = lax.broadcasted_iota(jnp.int32, table_w.shape, 0) + pl.program_id(0) * table_w.shape[0]
    total = jnp.zeros(table_w.shape, f32)
    for micro in range(2):
        sums = jnp.concatenate(
            [small_ref[micro : micro + 1, 0:half], small_ref[micro : micro + 1, half:]], axis=0
        )
        total = total + jnp.where(row == speakers_ref[micro], sums[None], 0.0)
    table_g[...] = total
    update(total, table_w, table_m, table_v, 0.3, (table_w_new, table_m_new, table_v_new))

    @pl.when(pl.program_id(0) == 0)
    def _():
        counted = (lengths_ref[0] + lengths_ref[1]).astype(f32) * full
        squares = [
            jnp.sum(small_ref[8:16, part * 128 : (part + 1) * 128], axis=(0, 1), keepdims=True)
            for part in range(2)
        ]
        at = lax.broadcasted_iota(jnp.int32, (1, 2), 1)
        rms_out[...] = jnp.sqrt(jnp.where(at == 0, squares[0], squares[1]) / counted)


def run_update(lengths, speakers, small, weights, conv_parts, out_parts, table_parts, results):
    steps = 8
    width = weights.shape[1]
    gate_local, full = out_parts[0].shape[0], out_parts[0].shape[1] // 2
    f32 = jnp.float32

    def rows(value, axis=0):
        shape = list(value.shape)
        shape[axis] = pl.cdiv(shape[axis], steps)
        return pl.BlockSpec(tuple(shape), lambda i: tuple(i if at == axis else 0 for at in range(len(shape))))

    def whole(shape):
        return pl.BlockSpec(tuple(shape), lambda i: (0,) * len(shape))

    conv_block, out_block = 2 * full // steps, 2 * full // steps
    out_first = 2 * full // out_block
    smem = pl.BlockSpec(memory_space=pltpu.SMEM)
    like = [jax.ShapeDtypeStruct(value.shape, f32) for value in (results[0], conv_parts[0], out_parts[0], table_parts[0])]
    specs = [rows(results[0], 1), rows(conv_parts[0]), rows(out_parts[0], 1), rows(table_parts[0])]
    return pl.pallas_call(
        functools.partial(update_kernel, full),
        grid=(steps,),
        out_shape=(
            *[like[0]] * 3,
            jax.ShapeDtypeStruct((1, 2), f32),
            *[like[1]] * 4,
            *[like[2]] * 4,
            *[like[3]] * 4,
        ),
        in_specs=[
            smem,
            smem,
            whole(small.shape),
            pl.BlockSpec((conv_block, width), lambda i: (i, 0)),
            pl.BlockSpec(
                (out_block, gate_local),
                lambda i: (out_first + i % (steps // 2), i // (steps // 2)),
            ),
            *[specs[1]] * 3,
            *[specs[2]] * 3,
            *[specs[3]] * 3,
            *[specs[0]] * 3,
        ],
        out_specs=(
            *[specs[0]] * 3,
            whole((1, 2)),
            *[specs[1]] * 4,
            *[specs[2]] * 4,
            *[specs[3]] * 4,
        ),
        compiler_params=pltpu.CompilerParams(
            dimension_semantics=("arbitrary",), vmem_limit_bytes=62 * 1024 * 1024
        ),
        cost_estimate=pl.CostEstimate(
            flops=20_000_000, bytes_accessed=32_000_000, transcendentals=1_000_000
        ),
    )(
        lengths,
        speakers,
        small,
        weights,
        weights,
        *conv_parts,
        *out_parts,
        *table_parts,
        *results,
    )


def fast_shards(
    n_seq,
    x_in,
    skip_in,
    cot_res,
    cot_skip,
    lengths,
    speakers,
    conv_weight,
    conv_m,
    conv_v,
    out_weight,
    out_m,
    out_v,
    speaker_table,
    table_m,
    table_v,
):
    views = [lane_view(value) for value in (conv_weight, conv_m, conv_v)]
    res, skipped, grads, weights, small = run_layers(
        x_in,
        skip_in,
        cot_res,
        cot_skip,
        lengths,
        speakers,
        views[0],
        out_weight[0],
        speaker_table[0],
        n_seq,
    )
    results = run_update(
        lengths,
        speakers,
        small,
        weights,
        views,
        [out_weight[0], out_m[0], out_v[0]],
        [speaker_table[0], table_m[0], table_v[0]],
        [res, skipped, grads],
    )
    wide, rms_out = results[0:3], results[3]
    conv_parts = [lane_back(value, conv_weight.shape) for value in results[4:8]]
    return (
        *[value[None] for value in wide],
        rms_out,
        *conv_parts,
        *[value[None] for value in results[8:12]],
        *[value[None] for value in results[12:16]],
    )


def shards(
    x_in,
    skip_in,
    cot_res,
    cot_skip,
    lengths,
    speakers,
    conv_weight,
    conv_m,
    conv_v,
    out_weight,
    out_m,
    out_v,
    speaker_table,
    table_m,
    table_v,
):
    micro_count, residual_local, block_length_rows = x_in.shape
    leading_section = lax.axis_index("section") == 0
    seq_index = lax.axis_index("seq")
    dilation_factor = jnp.where(leading_section, FIRST_DILATION, 1).astype(jnp.int32)
    conv_low = conv_weight[0].astype(jnp.bfloat16)
    full_res = conv_low.shape[1]
    gate_dev = conv_low.shape[3]
    speaker_rows = speaker_table.shape[1]
    conv_matrix = conv_low.reshape(2 * full_res, 2 * gate_dev)
    output_low = out_weight[0].astype(jnp.bfloat16)
    table_low = speaker_table[0].astype(jnp.bfloat16).reshape(speaker_rows, 2 * gate_dev)
    positions = seq_index * block_length_rows + jnp.arange(block_length_rows)
    contract_first = (((0,), (0,)), ((), ()))
    contract_last = (((1,), (1,)), ((), ()))
    recv_resid = jnp.zeros((residual_local, block_length_rows), jnp.float32)
    recv_skip = jnp.zeros((residual_local, block_length_rows), jnp.float32)
    kept_list = []
    resid_list = []
    skip_list = []
    square_res = jnp.float32(0.0)
    square_branch = jnp.float32(0.0)
    counted = jnp.float32(0.0)
    for tick_num in range(micro_count + 1):
        index_zero = min(tick_num, micro_count - 1)
        index_one = max(tick_num - 1, 0)
        batch_idx = jnp.where(leading_section, index_zero, index_one)
        is_live = jnp.where(leading_section, tick_num < micro_count, tick_num >= 1).astype(
            jnp.float32
        )
        residual_stream = jnp.where(
            leading_section, x_in[index_zero].astype(jnp.float32), recv_resid
        )
        skip_accumulated = jnp.where(leading_section, skip_in[index_zero], recv_skip)
        onehot = (jnp.arange(speaker_rows) == speakers[batch_idx]).astype(jnp.bfloat16)
        input_signal = residual_stream.astype(jnp.bfloat16)
        preceding_state = passed_along(
            input_signal[:, block_length_rows - FIRST_DILATION :], "seq", 1
        )
        joined_taps = jnp.concatenate([preceding_state, input_signal], axis=1)
        delayed_tap = lax.dynamic_slice_in_dim(
            joined_taps, FIRST_DILATION - dilation_factor, block_length_rows, 1
        )
        tap_rows = jnp.stack([delayed_tap, input_signal], axis=0)
        forward_tap_full = lax.all_gather(tap_rows, "mp", axis=1, tiled=True).reshape(
            2 * full_res, block_length_rows
        )
        embedding = jnp.dot(onehot, table_low, preferred_element_type=jnp.float32)
        forward_preact = (
            lax.dot_general(
                conv_matrix, forward_tap_full, contract_first, preferred_element_type=jnp.float32
            )
            + embedding[:, None]
        )
        hidden = (
            jnp.tanh(forward_preact[:gate_dev]) * jax.nn.sigmoid(forward_preact[gate_dev:])
        ).astype(jnp.bfloat16)
        partial_sums = lax.dot_general(
            output_low, hidden, contract_first, preferred_element_type=jnp.float32
        ).reshape(2, full_res, block_length_rows)
        projected = lax.psum_scatter(partial_sums, "mp", scatter_dimension=1, tiled=True)
        branch = projected[0]
        new_resid = (residual_stream + branch) * root_half
        new_skip = skip_accumulated + projected[1]
        new_resid, new_skip, branch, kept_data = (
            new_resid,
            new_skip,
            branch,
            (forward_tap_full, forward_preact, hidden),
        )
        valid_rows = (positions < lengths[batch_idx]).astype(jnp.float32)[None, :] * is_live
        square_res = square_res + jnp.sum(valid_rows * new_resid * new_resid)
        square_branch = square_branch + jnp.sum(valid_rows * branch * branch)
        counted = counted + jnp.sum(valid_rows) * residual_local
        kept_list.append(kept_data)
        resid_list.append(new_resid)
        skip_list.append(new_skip)
        if tick_num < micro_count:
            recv_resid, recv_skip = passed_along((new_resid, new_skip), "section", 1)
    square_res, square_branch, counted = lax.psum(
        (square_res, square_branch, counted), ("seq", "mp")
    )
    rms_out = jnp.stack([jnp.sqrt(square_res / counted), jnp.sqrt(square_branch / counted)])[None]
    res_out = jnp.stack(
        [
            jnp.where(leading_section, resid_list[m_idx], resid_list[m_idx + 1])
            for m_idx in range(micro_count)
        ]
    )[None]
    skip_out = jnp.stack(
        [
            jnp.where(leading_section, skip_list[m_idx], skip_list[m_idx + 1])
            for m_idx in range(micro_count)
        ]
    )[None]
    conv_acc = jnp.zeros((2 * full_res, 2 * gate_dev), jnp.float32)
    table_acc = jnp.zeros((speaker_rows, 2 * gate_dev), jnp.float32)
    out_acc = jnp.zeros((gate_dev, 2 * full_res), jnp.float32)
    recv_grad = jnp.zeros((residual_local, block_length_rows), jnp.float32)
    input_grads = []
    for tick_num in range(micro_count + 1):
        index_one = min(tick_num, micro_count - 1)
        index_zero = max(tick_num - 1, 0)
        batch_idx = jnp.where(leading_section, index_zero, index_one)
        is_live = jnp.where(leading_section, tick_num >= 1, tick_num < micro_count).astype(
            jnp.float32
        )
        valid_rows = (positions < lengths[batch_idx]).astype(jnp.float32)[None, :] * is_live
        onehot = (jnp.arange(speaker_rows) == speakers[batch_idx]).astype(jnp.bfloat16)
        kept_data = jax.tree.map(
            lambda zero_side, one_side: jnp.where(leading_section, zero_side, one_side),
            kept_list[index_zero],
            kept_list[index_one + 1],
        )
        skip_grad = (
            jnp.where(leading_section, cot_skip[index_zero], cot_skip[index_one]) * valid_rows
        )
        resid_grad = jnp.where(
            leading_section, recv_grad * is_live, cot_res[index_one] * valid_rows
        )
        tap_full, preact, hidden_used = kept_data
        proj_grad = jnp.stack([resid_grad * root_half, skip_grad], axis=0).astype(jnp.bfloat16)
        full_grad = lax.all_gather(proj_grad, "mp", axis=1, tiled=True).reshape(
            2 * full_res, block_length_rows
        )
        hidden_grad = jnp.dot(output_low, full_grad, preferred_element_type=jnp.float32)
        weight_term = lax.dot_general(
            hidden_used, full_grad, contract_last, preferred_element_type=jnp.float32
        )
        filter_act = jnp.tanh(preact[:gate_dev])
        gate_act = jax.nn.sigmoid(preact[gate_dev:])
        filter_grad = hidden_grad * gate_act * (1.0 - filter_act * filter_act)
        gate_grad = hidden_grad * filter_act * gate_act * (1.0 - gate_act)
        preact_grad = jnp.concatenate([filter_grad, gate_grad], axis=0).astype(jnp.bfloat16)
        conv_term = lax.dot_general(
            tap_full, preact_grad, contract_last, preferred_element_type=jnp.float32
        )
        column_sums = jnp.sum(preact_grad.astype(jnp.float32), axis=1)
        table_term = onehot.astype(jnp.float32)[:, None] * column_sums[None, :]
        tap_terms = jnp.dot(conv_matrix, preact_grad, preferred_element_type=jnp.float32)
        tap_gradient = lax.psum_scatter(
            tap_terms.reshape(2, full_res, block_length_rows), "mp", scatter_dimension=1, tiled=True
        )
        joined_taps_gradient = lax.dynamic_update_slice_in_dim(
            jnp.zeros((residual_local, FIRST_DILATION + block_length_rows), jnp.float32),
            tap_gradient[0],
            FIRST_DILATION - dilation_factor,
            1,
        )
        border_gradient = passed_along(joined_taps_gradient[:, :FIRST_DILATION], "seq", -1)
        input_gradient_rows = tap_gradient[1] + joined_taps_gradient[:, FIRST_DILATION:]
        input_gradient_rows = input_gradient_rows.at[:, block_length_rows - FIRST_DILATION :].add(
            border_gradient
        )
        resid_back, conv_term, weight_term, table_term = (
            resid_grad * root_half + input_gradient_rows,
            conv_term,
            weight_term,
            table_term,
        )
        conv_acc = conv_acc + conv_term
        out_acc = out_acc + weight_term
        table_acc = table_acc + table_term
        input_grads.append(resid_back)
        if tick_num < micro_count:
            recv_grad = passed_along(resid_back, "section", -1)
    grad_in = jnp.stack(
        [
            jnp.where(leading_section, input_grads[m_idx + 1], input_grads[m_idx])
            for m_idx in range(micro_count)
        ]
    )[None]
    conv_total, out_total, table_total = lax.psum((conv_acc, out_acc, table_acc), "seq")
    conv_grad = conv_total.reshape(conv_weight.shape)
    out_grad = out_total.reshape(out_weight.shape)
    table_grad = table_total.reshape(speaker_table.shape)
    conv_new, conv_m_new, conv_v_new = adamw(conv_weight, conv_m, conv_v, conv_grad, 0.03)
    out_new, out_m_new, out_v_new = adamw(out_weight, out_m, out_v, out_grad, 0.1)
    table_new, table_m_new, table_v_new = adamw(speaker_table, table_m, table_v, table_grad, 0.3)
    return (
        res_out,
        skip_out,
        grad_in,
        rms_out,
        conv_grad,
        conv_new,
        conv_m_new,
        conv_v_new,
        out_grad,
        out_new,
        out_m_new,
        out_v_new,
        table_grad,
        table_new,
        table_m_new,
        table_v_new,
    )


def solution(mesh):
    in_specs = (
        P(None, "mp", "seq"),
        P(None, "mp", "seq"),
        P(None, "mp", "seq"),
        P(None, "mp", "seq"),
        P(),
        P(),
        P("section", None, None, None, "mp"),
        P("section", None, None, None, "mp"),
        P("section", None, None, None, "mp"),
        P("section", "mp", None),
        P("section", "mp", None),
        P("section", "mp", None),
        P("section", None, None, "mp"),
        P("section", None, None, "mp"),
        P("section", None, None, "mp"),
    )
    out_specs = (
        P("section", None, "mp", "seq"),
        P("section", None, "mp", "seq"),
        P("section", None, "mp", "seq"),
        P("section", None),
        P("section", None, None, None, "mp"),
        P("section", None, None, None, "mp"),
        P("section", None, None, None, "mp"),
        P("section", None, None, None, "mp"),
        P("section", "mp", None),
        P("section", "mp", None),
        P("section", "mp", None),
        P("section", "mp", None),
        P("section", None, None, "mp"),
        P("section", None, None, "mp"),
        P("section", None, None, "mp"),
        P("section", None, None, "mp"),
    )
    n_seq = mesh.shape["seq"]
    fits = mesh.shape["mp"] == 2 and n_seq in (4, 8, 16)
    return jax.shard_map(
        functools.partial(fast_shards, n_seq) if fits else shards,
        mesh=mesh,
        in_specs=in_specs,
        out_specs=out_specs,
        check_vma=False,
    )
```

```python
import functools
import math

import jax
import jax.numpy as jnp
from jax import lax
from jax.experimental import pallas as pl
from jax.experimental.pallas import tpu as pltpu
from jax.sharding import PartitionSpec as P

FIRST_DILATION = 512
STEP = 10
MESH = pl.DeviceIdType.MESH
TILE = 256
UNITS = 3
Z_FIRST = 1

beta_one = 0.9
beta_two = 0.999
adam_eps = 1e-08
decay_rate = 0.01
root_half = math.sqrt(0.5)


def passed_along(value, axis, steps):
    count = lax.axis_size(axis)
    first, last = (max(0, -steps), min(count, count - steps))
    return lax.ppermute(value, axis, [(source, source + steps) for source in range(first, last)])


def adamw(weight, moment, second, gradient, step_rate):
    moment_new = beta_one * moment + (1.0 - beta_one) * gradient
    second_new = beta_two * second + (1.0 - beta_two) * gradient * gradient
    corr_one = 1.0 - beta_one**STEP
    corr_two = 1.0 - beta_two**STEP
    update = moment_new / corr_one / (jnp.sqrt(second_new / corr_two) + adam_eps)
    weight_new = weight - step_rate * (update + decay_rate * weight)
    return (weight_new, moment_new, second_new)


def dot(left, right):
    return jnp.dot(left, right, preferred_element_type=jnp.float32)


def dot_last(left, right):
    return lax.dot_general(
        left, right, (((1,), (1,)), ((), ())), preferred_element_type=jnp.float32
    )


def rows_at(start, size):
    return pl.ds(start if isinstance(start, int) else pl.multiple_of(start, 16), size)


def cols_at(start, size):
    return pl.ds(start if isinstance(start, int) else pl.multiple_of(start, 128), size)


def layers_kernel(
    sizes,
    x_ref,
    skip_ref,
    cot_res_ref,
    cot_skip_ref,
    lengths_ref,
    speakers_ref,
    conv_ref,
    out_ref,
    table_ref,
    res_ref,
    skipped_ref,
    grad_ref,
    weight_ref,
    small_ref,
    conv_wide,
    out_wide,
    table_wide,
    xf,
    wc,
    wct,
    wo,
    wot,
    et,
    in1,
    next_out,
    next_in,
    past1,
    act_f,
    act_q,
    hid,
    dproj,
    dres0,
    dpre,
    grad1,
    past_grad1,
    edge_out,
    edge_in,
    res0,
    skip_sum,
    cot_a,
    cot_b,
    skip_low,
    res_low,
    grad1_low,
    grad0,
    past0_out,
    past0_in,
    grad0_low,
    stats,
    acc,
    from_core,
    down,
    final,
    small,
    small_in,
    small_sum,
    send_sem,
    recv_sem,
    local_sem,
):
    full, local, gates, span, n_seq = sizes
    gate_local = gates // 2
    width = 2 * gate_local
    halo = FIRST_DILATION
    n_z = n_seq // 2
    c = lax.axis_index("section")
    s = lax.axis_index("seq")
    x = lax.axis_index("mp")
    z, y = s // 2, s % 2
    oc, ox = 1 - c, 1 - x
    bf16, f32 = jnp.bfloat16, jnp.float32
    counts = {"send": 0, "recv": 0, "local": 0}
    pending = []
    inside = [None]

    def take(kind, amount=1):
        counts[kind] += amount
        return counts[kind] - amount

    def when(cond, action):
        if cond is None:
            action()
        else:
            pl.when(cond)(action)

    def on(cond, action):
        inside[0] = cond
        pl.when(cond)(lambda: action())
        inside[0] = None

    def send(source, target, device, recv_at, cond=None):
        at = take("send")

        def make():
            return pltpu.make_async_remote_copy(
                src_ref=source(),
                dst_ref=target(),
                send_sem=send_sem.at[at],
                recv_sem=recv_sem.at[recv_at()],
                device_id=device(),
                device_id_type=MESH,
            )

        when(cond, lambda: make().start())
        pending.append((lambda: make().wait_send(), inside[0] if cond is None else cond))

    def arrive(target, recv_at, cond=None):
        when(
            cond,
            lambda: pltpu.make_async_remote_copy(
                src_ref=target,
                dst_ref=target,
                send_sem=send_sem.at[0],
                recv_sem=recv_sem.at[recv_at],
                device_id={"section": oc},
                device_id_type=MESH,
            ).wait_recv(),
        )

    def fetch(source, target, cond=None):
        copy = pltpu.make_async_copy(source, target, local_sem.at[take("local")])
        when(cond, copy.start)
        return copy

    def to(axis, index):
        return lambda: {axis: index()}

    core_dev = to("section", lambda: 1 - c)
    mp_dev = to("mp", lambda: 1 - x)
    y_dev = to("seq", lambda: z * 2 + 1 - y)
    prev_dev, next_dev = to("seq", lambda: s - 1), to("seq", lambda: s + 1)
    has_prev, has_next = s > 0, s < n_seq - 1

    z_seqs = [lax.rem(z + step, n_z) * 2 + y for step in range(n_z)]

    def z_seq(step):
        return z_seqs[step]

    def z_dev(step):
        return to("seq", lambda: z_seq(step))

    bits = [y] + [(z // (1 << bit)) % 2 for bit in range((n_seq // 2).bit_length() - 1)]
    pairs = [z * 2 + 1 - y] + [
        (z + (1 - 2 * bits[bit + 1]) * (1 << bit)) * 2 + y for bit in range(len(bits) - 1)
    ]
    depth = len(bits)
    pair_devs = [to("seq", lambda way=way: pairs[way]) for way in range(depth)]

    barrier = pltpu.get_barrier_semaphore()
    for device in [core_dev, mp_dev, y_dev, *[z_dev(step) for step in range(1, n_z)]]:
        pl.semaphore_signal(barrier, inc=1, device_id=device(), device_id_type=MESH)
    before, after = (y == 0) & (z > 0), (y == 1) & (z < n_z - 1)

    @pl.when(before)
    def _():
        pl.semaphore_signal(barrier, inc=1, device_id=prev_dev(), device_id_type=MESH)

    @pl.when(after)
    def _():
        pl.semaphore_signal(barrier, inc=1, device_id=next_dev(), device_id_type=MESH)

    own_rows, other_rows = rows_at(x * local, local), rows_at(ox * local, local)
    got_conv = fetch(conv_ref, conv_wide)
    chunks = span // halo
    got_x = [
        fetch(x_ref.at[c, :, pl.ds(chunk * halo, halo)], xf.at[chunk + 1, own_rows])
        for chunk in reversed(range(chunks))
    ]
    got_table = fetch(table_ref, table_wide)
    got_out = fetch(out_ref, out_wide)

    def cast_conv(step, carry):
        for block in range(width // 128):
            half, lane = block // (gate_local // 128), block % (gate_local // 128)
            first = step * 256 * (width // 128) + lane * 2 + half
            wc[c, x, rows_at(step * 256, 256), pl.ds(block * 128, 128)] = conv_wide[
                pl.ds(first, 256, stride=width // 128), :
            ].astype(bf16)
        return carry

    got_conv.wait()
    got_cot_a = fetch(cot_res_ref.at[c], cot_a)
    got_cot_b = fetch(cot_skip_ref.at[c], cot_b)
    got_skip = fetch(skip_ref.at[c], skip_sum)
    lax.fori_loop(0, 2 * full // 256, cast_conv, None)
    got_table.wait()
    marks = lax.broadcasted_iota(jnp.int32, (16, width), 0)
    emb = jnp.zeros((16, width), f32)
    for micro in range(2):
        rows = table_wide[speakers_ref[micro]]
        row = jnp.concatenate([rows[0:1, :], rows[1:2, :]], axis=1)
        emb = jnp.where(marks == micro, row, emb)
    wc[c, x, 2 * full : 2 * full + 16, :] = emb.astype(bf16)
    got_out.wait()
    wo[c, rows_at(x * gate_local, gate_local), :] = out_wide[...].astype(bf16)

    @pl.when(before | after)
    def _():
        pl.semaphore_wait(barrier, 3 + n_z)

    @pl.when(jnp.logical_not(before | after))
    def _():
        pl.semaphore_wait(barrier, 2 + n_z)

    conv_rows, out_rows = 2 * full // n_seq, gate_local // n_seq
    conv_at, conv_core_at = take("recv", n_seq), take("recv", n_seq)
    out_at, emb_at = take("recv", n_seq), take("recv")

    def conv_slice(index, layer, block):
        return wc.at[layer, block, rows_at(index * conv_rows, conv_rows)]

    def out_slice(index, layer, block):
        return wo.at[layer, rows_at(block * gate_local + index * out_rows, out_rows)]

    def emb_part(layer, block):
        return wc.at[layer, block, 2 * full : 2 * full + 16]

    def conv_block(layer, block):
        return wc.at[layer, block, 0 : 2 * full]

    def out_block(layer, block):
        return wo.at[layer, rows_at(block * gate_local, gate_local)]

    def send_same(ref, device, recv_at, cond=None):
        send(ref, ref, device, recv_at, cond)

    def cross_weights():
        send_same(lambda: conv_slice(s, c, x), mp_dev, lambda: conv_at + s)
        send_same(lambda: emb_part(c, x), mp_dev, lambda: emb_at)
        send_same(lambda: out_slice(s, c, x), mp_dev, lambda: out_at + s)

    on(c == 0, cross_weights)
    x_at = [take("recv") for _ in range(chunks)]
    for copy in got_x:
        copy.wait()
    for chunk in reversed(range(chunks)):
        send_same(
            lambda chunk=chunk: xf.at[chunk + 1, own_rows], mp_dev, lambda chunk=chunk: x_at[chunk]
        )
    on(c == 1, cross_weights)
    halo_at = [take("recv"), take("recv")]
    send(
        lambda: xf.at[chunks, own_rows],
        lambda: xf.at[0, own_rows],
        next_dev,
        lambda: halo_at[0],
        has_next,
    )
    core_at = [take("recv") for _ in range(5)]
    send_same(lambda: conv_block(c, x), core_dev, lambda: core_at[0])
    send_same(lambda: emb_part(c, x), core_dev, lambda: core_at[1])
    send_same(lambda: out_block(c, x), core_dev, lambda: core_at[2])

    @pl.when(s == 0)
    def _():
        xf[0] = jnp.zeros((full, halo), bf16)
        next_in[...] = jnp.zeros(next_in.shape, bf16)

    @pl.when(s == n_seq - 1)
    def _():
        past0_in[...] = jnp.zeros(past0_in.shape, bf16)
        edge_in[...] = jnp.zeros(edge_in.shape, bf16)

    stats[...] = jnp.zeros(stats.shape, f32)
    length = lengths_ref[c]

    def valid_at(start, size):
        at = s * span + start + lax.broadcasted_iota(jnp.int32, (1, size), 1)
        return jnp.where(at < length, 1.0, 0.0).astype(f32)

    def cast_cotangents(step, carry):
        at = cols_at(step * TILE, TILE)
        valid = valid_at(step * TILE, TILE)
        dproj[step, own_rows, :] = (cot_a[:, at] * valid * root_half).astype(bf16)
        dproj[step, rows_at(full + x * local, local), :] = (cot_b[:, at] * valid).astype(bf16)
        return carry

    tiles = span // TILE
    got_cot_a.wait()
    got_cot_b.wait()
    lax.fori_loop(0, tiles, cast_cotangents, None)
    cot_at = take("recv", 2 * tiles)

    def cot_piece(tile, part, block):
        return dproj.at[tile, rows_at(part * full + block * local, local)]

    for tile in range(tiles):
        for part in range(2):
            send_same(
                functools.partial(cot_piece, tile, part, x),
                mp_dev,
                lambda tile=tile, part=part: cot_at + tile * 2 + part,
            )

    def turn_conv(layer, block, first, rows):
        wct[layer, rows_at(block * width, width), cols_at(first, rows)] = wc[
            layer, block, rows_at(first, rows), :
        ].T

    def turn_rest(layer, block):
        values = wc[layer, block, 2 * full : 2 * full + 16, :].astype(f32)
        mark_row = lax.broadcasted_iota(jnp.int32, values.shape, 0)
        picked = jnp.sum(jnp.where(mark_row == c, values, 0.0), axis=0, keepdims=True)
        et[layer, rows_at(block * width, width), :] = jnp.broadcast_to(picked, (128, width)).T

        for part, start in enumerate((x * local, full + x * local, ox * local)):
            wot[layer, part * local : (part + 1) * local, cols_at(block * gate_local, gate_local)] = wo[
                layer, rows_at(block * gate_local, gate_local), cols_at(start, local)
            ].T

    def turn_all(layer, block):
        for step in range(2 * full // TILE):
            turn_conv(layer, block, step * TILE, TILE)
        turn_rest(layer, block)

    def spread_first():
        arrive(conv_slice(s, c, ox), conv_at + s)
        for step in range(1, n_z):
            send_same(lambda: conv_slice(s, c, ox), z_dev(step), lambda: conv_at + s)
        send_same(lambda: conv_slice(s, c, ox), y_dev, lambda: conv_at + s)
        send_same(lambda: conv_slice(s, c, ox), core_dev, lambda: conv_core_at + s)
        arrive(emb_part(c, ox), emb_at)
        send_same(lambda: emb_part(c, ox), core_dev, lambda: core_at[3])
        arrive(out_slice(s, c, ox), out_at + s)
        for step in range(1, n_z):
            send_same(lambda: out_slice(s, c, ox), z_dev(step), lambda: out_at + s)
        send_same(lambda: out_slice(s, c, ox), y_dev, lambda: out_at + s)

    def spread_conv():
        for step in range(1, n_z):
            arrive(conv_slice(z_seq(step), c, ox), conv_at + z_seq(step))
            here = functools.partial(lambda step: conv_slice(z_seq(step), c, ox), step)
            send_same(here, y_dev, lambda step=step: conv_at + z_seq(step))
            send_same(here, core_dev, lambda step=step: conv_core_at + z_seq(step))

    def spread_out():
        for step in range(1, n_z):
            arrive(out_slice(z_seq(step), c, ox), out_at + z_seq(step))
            here = functools.partial(lambda step: out_slice(z_seq(step), c, ox), step)
            send_same(here, y_dev, lambda step=step: out_at + z_seq(step))

    def spread_last():
        for step in range(n_z):
            arrive(conv_slice(z_seq(step) + 1 - 2 * y, c, ox), conv_at + z_seq(step) + 1 - 2 * y)
            here = functools.partial(
                lambda step: conv_slice(z_seq(step) + 1 - 2 * y, c, ox), step
            )
            send_same(here, core_dev, lambda step=step: conv_core_at + z_seq(step) + 1 - 2 * y)
        for step in range(n_z):
            arrive(out_slice(z_seq(step) + 1 - 2 * y, c, ox), out_at + z_seq(step) + 1 - 2 * y)
        send_same(lambda: out_block(c, ox), core_dev, lambda: core_at[4])

    def all_from_core():
        for step in range(n_seq):
            arrive(conv_slice(step, oc, ox), conv_core_at + step)
        arrive(emb_part(oc, ox), core_at[3])
        arrive(out_block(oc, ox), core_at[4])

    on(c == 0, spread_first)

    @pl.when(c == 0)
    def _():
        turn_all(0, x)

    arrive(xf.at[chunks, other_rows], x_at[chunks - 1])
    send(
        lambda: xf.at[chunks, other_rows],
        lambda: xf.at[0, other_rows],
        next_dev,
        lambda: halo_at[1],
        has_next,
    )
    on(c == 0, spread_conv)
    arrive(conv_block(oc, x), core_at[0])
    arrive(emb_part(oc, x), core_at[1])
    arrive(out_block(oc, x), core_at[2])

    @pl.when(c == 1)
    def _():
        turn_all(0, x)

    on(c == 0, spread_out)
    turn_all(1, x)
    on(c == 0, spread_last)

    on(c == 1, all_from_core)
    turn_all(0, ox)

    def fold(values):
        total = jnp.sum(values.reshape(local // 8, 8, TILE), axis=0)
        return sum(total[:, part * 128 : (part + 1) * 128] for part in range(TILE // 128))

    def gated(layer, pre, at):
        halves = []
        for block in range(2):
            base = block * width
            shift = et[layer, base : base + width, :]
            shift = jnp.concatenate([shift] * (TILE // 128), axis=1)
            f = jnp.tanh(pre[base : base + gate_local] + shift[:gate_local])
            q = 0.5 * jnp.tanh(
                0.5 * (pre[base + gate_local : base + width] + shift[gate_local:])
            ) + 0.5
            rows = slice(block * gate_local, (block + 1) * gate_local)
            act_f[layer, rows, at] = f
            act_q[layer, rows, at] = q
            halves.append((f * q).astype(bf16))
            hid[layer, rows, at] = halves[-1]
        return jnp.concatenate(halves, axis=0)

    def forward0(step):
        start = step * TILE
        at = cols_at(start, TILE)
        chunk, inner = start // halo, pl.ds(start % halo, TILE)
        pre = dot(wct[0], jnp.concatenate([xf[chunk, :, inner], xf[chunk + 1, :, inner]], axis=0))
        hidden = gated(0, pre, at)
        valid = valid_at(start, TILE)
        proj = dot(wot[0], hidden)
        branch = proj[0:local]
        res = (xf[chunk + 1, own_rows, inner].astype(f32) + branch) * root_half
        res0[:, at] = res
        in1[own_rows, at] = res.astype(bf16)
        stats[0, 0] += fold(valid * res * res)
        stats[0, 1] += fold(valid * branch * branch)
        res = (xf[chunk + 1, other_rows, inner].astype(f32) + proj[2 * local :]) * root_half
        in1[other_rows, at] = res.astype(bf16)
        total = skip_sum[:, at] + proj[local : 2 * local]
        skip_sum[:, at] = total
        skip_low[0, :, at] = total.astype(bf16)

    late_tiles = (span - halo) // TILE
    got_skip.wait()
    for chunk in range(chunks - 1):
        arrive(xf.at[chunk + 1, other_rows], x_at[chunk])
    on(c == 1, spread_first)
    for step in range(late_tiles, tiles):
        forward0(step)
    in1_at = take("recv")
    next_out[...] = in1[:, span - 128 : span]
    send(
        lambda: next_out,
        lambda: next_in,
        next_dev,
        lambda: in1_at,
        has_next,
    )
    on(c == 1, spread_conv)
    on(c == 1, spread_out)
    arrive(xf.at[0, own_rows], halo_at[0], has_prev)
    arrive(xf.at[0, other_rows], halo_at[1], has_prev)
    for step in range(late_tiles):
        forward0(step)
    on(c == 1, spread_last)

    result_at = [take("recv") for _ in range(3)]
    locals_pending = []

    def give(layer, kind, source, target):
        copy = fetch(source, target.at[c], c == layer)
        locals_pending.append((copy, c == layer))
        send(lambda: source, lambda: target.at[c], core_dev, lambda: result_at[kind], c != layer)

    give(0, 0, in1.at[own_rows], res_ref)
    give(0, 1, skip_low.at[0], skipped_ref)

    on(c == 0, all_from_core)
    turn_all(1, ox)

    def forward1(step):
        start = step * TILE
        at = cols_at(start, TILE)
        for base in range(0, full, 256):
            rows = slice(base, base + 256)
            if start == 0:
                wide = jnp.concatenate([next_in[rows, :], in1[rows, 0:TILE]], axis=1).astype(f32)
            else:
                wide = in1[rows, start - 128 : start + TILE].astype(f32)
            past1[base : base + 256, at] = pltpu.roll(wide, 1, 1)[:, 128:].astype(bf16)
        pre = dot(wct[1], jnp.concatenate([past1[:, at], in1[:, at]], axis=0))
        hidden = gated(1, pre, at)
        valid = valid_at(start, TILE)
        proj = dot(wot[1, 0 : 2 * local], hidden)
        branch = proj[0:local]
        res = (res0[:, at] + branch) * root_half
        res_low[:, at] = res.astype(bf16)
        stats[1, 0] += fold(valid * res * res)
        stats[1, 1] += fold(valid * branch * branch)
        total = skip_sum[:, at] + proj[local:]
        skip_low[1, :, at] = total.astype(bf16)

    arrive(next_in, in1_at, has_prev)
    for step in range(tiles):
        forward1(step)
    give(1, 0, res_low, res_ref)
    give(1, 1, skip_low.at[1], skipped_ref)

    def through_gates(layer, dhidden, at):
        for block in range(2):
            rows = slice(block * gate_local, (block + 1) * gate_local)
            f, q = act_f[layer, rows, at], act_q[layer, rows, at]
            d = dhidden[rows] * q
            base = block * width
            dpre[layer, base : base + gate_local, at] = (d * (1.0 - f * f)).astype(bf16)
            dpre[layer, base + gate_local : base + width, at] = (d * f * (1.0 - q)).astype(bf16)

    def backward1(step):
        at = cols_at(step * TILE, TILE)
        through_gates(1, dot(wo[1], dproj[step]), at)
        both = jnp.concatenate([wc[1, block, 0 : 2 * full, :] for block in range(2)], axis=1)
        taps = dot(both, dpre[1, :, at])
        past_grad1[:, at] = taps[0:full]
        grad1[:, at] = taps[full:] + dproj[step, 0:full, :].astype(f32)

    def join1(step):
        start = step * TILE
        at = cols_at(start, TILE)
        for base in range(0, full, 256):
            rows = slice(base, base + 256)
            wide = past_grad1[rows, cols_at(start, TILE + 128)]
            total = grad1[rows, at] + pltpu.roll(wide, TILE + 127, 1)[:, 0:TILE]
            grad1[rows, at] = total
            dres0[rows, at] = (root_half * total).astype(bf16)
        own = grad1[own_rows, at]
        grad1_low[:, at] = own.astype(bf16)
        grad0[:, at] = root_half * own

    def backward0(step):
        start = step * TILE
        at = cols_at(start, TILE)
        dhidden = dot(wo[0], jnp.concatenate([dres0[:, at], dproj[step, full:, :]], axis=0))
        through_gates(0, dhidden, at)
        own = [
            jnp.concatenate([wc[0, block, rows, :] for block in range(2)], axis=1)
            for rows in (own_rows, rows_at(full + x * local, local))
        ]
        taps = dot(jnp.concatenate(own, axis=0), dpre[0, :, at])
        grad0[:, at] += taps[local:]
        return taps[0:local]

    edge_at, past0_at = take("recv"), take("recv")
    early_tiles = halo // TILE

    for step in range(tiles):
        for part in range(2):
            arrive(cot_piece(step, part, ox), cot_at + step * 2 + part)
        tile = step - (tiles - early_tiles)
        if tile >= 0:
            join1(tile)
        backward1(step)
        if tile >= 0:
            past0_out[:, cols_at(tile * TILE, TILE)] = backward0(tile).astype(bf16)
        if step == 0:
            edge_out[...] = past_grad1[:, 0:128].astype(bf16)
            send(lambda: edge_out, lambda: edge_in, prev_dev, lambda: edge_at, has_prev)
    send(lambda: past0_out, lambda: past0_in, prev_dev, lambda: past0_at, has_prev)

    total_rows = 3 * full
    unit_rows = total_rows // UNITS
    unit_core_at = [take("recv") for _ in range(UNITS)]
    down_at = [[take("recv") for _ in range(depth)] for _ in range(UNITS)]
    up_at = [[take("recv") for _ in range(depth)] for _ in range(UNITS)]
    small_at = [take("recv") for _ in range(2 + depth)]
    stored_at = take("local", UNITS + 1)

    def to_core(layer, first, size):
        for unit in range(first // unit_rows, (first + size) // unit_rows):
            rows = pl.ds(unit * unit_rows, unit_rows)
            send(
                lambda rows=rows: acc.at[layer, rows],
                lambda rows=rows: from_core.at[rows],
                core_dev,
                lambda unit=unit: unit_core_at[unit],
                c != layer,
            )

    def unit_conv(layer, past, now, between=None):
        def part(first, taps):
            product = dot_last(taps, dpre[layer, rows_at(x * width, width), :])
            acc[layer, pl.ds(first, full), :] = product[0:full].astype(bf16)
            to_core(layer, first, full)
            return product

        part(0, past)
        if between is not None:
            between()
        product = part(full, jnp.concatenate([now, jnp.ones((16, span), bf16)], axis=0))
        sums = product[full : full + 8]
        mark = lax.broadcasted_iota(jnp.int32, sums.shape, 0)
        small[layer, 0:8, :] = jnp.where(mark == c, sums, 0.0)
        small[layer, 8:16, :] = jnp.zeros((8, width), f32)
        small[layer, 8:16, 0:128] = stats[layer, 0]
        small[layer, 8:16, 128:256] = stats[layer, 1]
        send(
            lambda: small.at[layer],
            lambda: small_in.at[0],
            core_dev,
            lambda: small_at[0],
            c != layer,
        )

    def unit_out(layer, parts):
        hidden = hid[layer, rows_at(x * gate_local, gate_local), :]
        product = dot_last(jnp.concatenate(parts, axis=0), hidden)
        for part in range(2):
            acc[layer, pl.ds(2 * full, full), pl.ds(part * gate_local, gate_local)] = product[
                part * full : (part + 1) * full
            ].astype(bf16)
        to_core(layer, 2 * full, full)

    n_stages = 2 * depth + 1

    def order(unit):
        ways = list(range(depth))
        return [1, 0, *ways[2:]] if unit == Z_FIRST and depth > 1 else ways

    def kept(unit, level, flip=False):
        start, size = unit * unit_rows, unit_rows
        for step in range(level):
            size //= 2
            bit = bits[order(unit)[step]]
            if flip and step == level - 1:
                bit = 1 - bit
            start = start + bit * size
        return rows_at(start, size)

    def landing(unit, level):
        size = unit_rows >> level
        return pl.ds(unit * unit_rows + unit_rows - 2 * size, size)

    def unit_stage(layer, unit, stage):
        ways = order(unit)
        if stage <= depth:
            here = kept(unit, stage)
            if stage == 0:
                arrive(from_core.at[here], unit_core_at[unit])
                other = from_core[here, :]
            else:
                place = landing(unit, stage)
                arrive(down.at[place], down_at[unit][stage - 1])
                other = down[place, :]
            total = (acc[layer, here, :].astype(f32) + other.astype(f32)).astype(bf16)
            if stage < depth:
                acc[layer, here, :] = total
                send(
                    lambda: acc.at[layer, kept(unit, stage + 1, True)],
                    lambda: down.at[landing(unit, stage + 1)],
                    pair_devs[ways[stage]],
                    lambda: down_at[unit][stage],
                )
                return
            final[here, :] = total
        if stage > depth:
            level = 2 * depth + 1 - stage
            arrive(final.at[kept(unit, level, True)], up_at[unit][level - 1])
        level = 2 * depth - stage
        if level > 0:
            send_same(
                lambda: final.at[kept(unit, level)],
                pair_devs[ways[level - 1]],
                lambda: up_at[unit][level - 1],
            )
        else:
            here = pl.ds(unit * unit_rows, unit_rows)
            pltpu.make_async_copy(
                final.at[here], weight_ref.at[here], local_sem.at[stored_at + unit]
            ).start()

    def small_stage(layer, stage):
        names = [core_dev, mp_dev, *pair_devs]
        arrive(small_in.at[stage], small_at[stage])
        if stage == 0:
            small_sum[0] = small[layer] + small_in[0]
        else:
            sums = small_sum[stage - 1, 0:8, :]
            small_sum[stage, 0:8, :] = sums if stage == 1 else sums + small_in[stage, 0:8, :]
            small_sum[stage, 8:16, :] = small_sum[stage - 1, 8:16, :] + small_in[stage, 8:16, :]
        if stage < len(names) - 1:
            send(
                lambda: small_sum.at[stage],
                lambda: small_in.at[stage + 1],
                names[stage + 1],
                lambda: small_at[stage + 1],
            )
        else:
            pltpu.make_async_copy(
                small_sum.at[stage], small_ref, local_sem.at[stored_at + UNITS]
            ).start()

    def in_order_of_arrival(layer, first_stage, units):
        ready = [(float(at), at, unit, first_stage) for at, unit in enumerate(units)]
        free = [0.0] * depth
        clock, small_next = 0.0, 0
        while ready:
            ready.sort()
            at, rank, unit, stage = ready.pop(0)
            unit_stage(layer, unit, stage)
            clock = max(clock, at) + 0.25
            if stage < n_stages - 1:
                way = order(unit)[min(stage, 2 * depth - 1 - stage)]
                level = min(stage, 2 * depth - 1 - stage)
                free[way] = max(free[way], clock) + 3.0 / 2**level * (2 if way == 2 else 1)
                ready.append((free[way] + 1.0, rank, unit, stage + 1))
            if stage == n_stages - 1 or stage == 2:
                if small_next < 2 + depth:
                    small_stage(layer, small_next)
                    small_next += 1
        for stage in range(small_next, 2 + depth):
            small_stage(layer, stage)

    unit_order = [2, 0, 1]

    def all_times(first):
        rows = slice(first, first + full)
        return jnp.concatenate([dproj[tile, rows, :] for tile in range(tiles)], axis=1)

    unit_out(1, [all_times(0), all_times(full)])
    unit_conv(1, past1[...], in1[...])

    arrive(edge_in, edge_at, has_next)
    past_grad1[:, span : span + 128] = edge_in[...].astype(f32)

    def start_sums(layer, units):
        for unit in units:
            unit_stage(layer, unit, 0)

    for step in range(early_tiles, tiles):
        join1(step)
    for step in range(early_tiles, tiles):
        grad0[:, cols_at(step * TILE - halo, TILE)] += backward0(step)
        if step == early_tiles:
            on(c == 1, lambda: start_sums(1, unit_order))
    give(1, 2, grad1_low, grad_ref)
    unit_out(0, [dres0[...], all_times(full)])
    unit_conv(
        0,
        jnp.concatenate([xf[chunk] for chunk in range(chunks)], axis=1),
        jnp.concatenate([xf[chunk + 1] for chunk in range(chunks)], axis=1),
        lambda: on(c == 0, lambda: start_sums(0, unit_order[:1])),
    )

    arrive(past0_in, past0_at, has_next)

    def join0(step, carry):
        at = cols_at(step * TILE, TILE)
        grad0_low[:, at] = grad0[:, at].astype(bf16)
        return carry

    lax.fori_loop(0, (span - halo) // TILE, join0, None)

    def join0_late(step, carry):
        at = cols_at(step * TILE + span - halo, TILE)
        grad0_low[:, at] = (
            grad0[:, at] + past0_in[:, cols_at(step * TILE, TILE)].astype(f32)
        ).astype(bf16)
        return carry

    lax.fori_loop(0, halo // TILE, join0_late, None)
    give(0, 2, grad0_low, grad_ref)

    on(c == 0, lambda: start_sums(0, unit_order[1:]))
    for wait, cond in pending:
        when(cond, wait)
    pending.clear()
    on(c == 0, lambda: in_order_of_arrival(0, 1, unit_order))
    on(c == 1, lambda: in_order_of_arrival(1, 1, unit_order))
    for unit in range(UNITS):
        here = pl.ds(unit * unit_rows, unit_rows)
        pltpu.make_async_copy(
            final.at[here], weight_ref.at[here], local_sem.at[stored_at + unit]
        ).wait()
    pltpu.make_async_copy(
        small_sum.at[1 + depth], small_ref, local_sem.at[stored_at + UNITS]
    ).wait()
    for kind, target in enumerate((res_ref, skipped_ref, grad_ref)):
        arrive(target.at[oc], result_at[kind])
    for copy, cond in locals_pending:
        when(cond, copy.wait)
    for wait, cond in pending:
        when(cond, wait)
    assert counts["send"] <= send_sem.shape[0], counts
    assert counts["recv"] <= recv_sem.shape[0], counts
    assert counts["local"] <= local_sem.shape[0], counts


def run_layers(
    x_in, skip_in, cot_res, cot_skip, lengths, speakers, conv_view, out_weight, table, n_seq
):
    micro, local, span = x_in.shape
    full = out_weight.shape[1] // 2
    gate_local = out_weight.shape[0]
    gates = 2 * gate_local
    bf16, f32 = jnp.bfloat16, jnp.float32
    halo = FIRST_DILATION
    rows = 3 * full
    depth = (n_seq // 2).bit_length()
    width = 2 * gate_local
    any_spec = pl.BlockSpec(memory_space=pl.ANY)
    scratch = [
        (conv_view.shape, f32),
        (out_weight.shape, f32),
        (table.shape, f32),
        ((span // halo + 1, full, halo), bf16),
        ((2, 2, 2 * full + 16, width), bf16),
        ((2, 2 * width, 2 * full), bf16),
        ((2, gates, 2 * full), bf16),
        ((2, 3 * local, gates), bf16),
        ((2, 2 * width, 128), f32),
        ((full, span), bf16),
        ((full, 128), bf16),
        ((full, 128), bf16),
        ((full, span), bf16),
        ((2, gates, span), f32),
        ((2, gates, span), f32),
        ((2, gates, span), bf16),
        ((span // TILE, 2 * full, TILE), bf16),
        ((full, span), bf16),
        ((2, 2 * width, span), bf16),
        ((full, span), f32),
        ((full, span + 128), f32),
        ((full, 128), bf16),
        ((full, 128), bf16),
        ((local, span), f32),
        ((local, span), f32),
        ((local, span), f32),
        ((local, span), f32),
        ((2, local, span), bf16),
        ((local, span), bf16),
        ((local, span), bf16),
        ((local, span), f32),
        ((local, halo), bf16),
        ((local, halo), bf16),
        ((local, span), bf16),
        ((2, 2, 8, 128), f32),
        ((2, rows, width), bf16),
        ((rows, width), bf16),
        ((rows, width), bf16),
        ((rows, width), bf16),
        ((2, 16, width), f32),
        ((2 + depth, 16, width), f32),
        ((2 + depth, 16, width), f32),
    ]
    result = jax.ShapeDtypeStruct((micro, local, span), bf16)
    return pl.pallas_call(
        functools.partial(layers_kernel, (full, local, gates, span, n_seq)),
        out_shape=(
            result,
            result,
            result,
            jax.ShapeDtypeStruct((rows, width), bf16),
            jax.ShapeDtypeStruct((16, width), f32),
        ),
        in_specs=[any_spec] * 4 + [pl.BlockSpec(memory_space=pltpu.SMEM)] * 2 + [any_spec] * 3,
        out_specs=[any_spec] * 5,
        scratch_shapes=[pltpu.VMEM(shape, kind) for shape, kind in scratch]
        + [
            pltpu.SemaphoreType.DMA((224,)),
            pltpu.SemaphoreType.DMA((144,)),
            pltpu.SemaphoreType.DMA((32,)),
        ],
        compiler_params=pltpu.CompilerParams(
            collective_id=0, has_side_effects=True, vmem_limit_bytes=62 * 1024 * 1024
        ),
        cost_estimate=pl.CostEstimate(
            flops=14_000_000_000, bytes_accessed=20_000_000, transcendentals=2_000_000
        ),
    )(x_in, skip_in, cot_res, cot_skip, lengths, speakers, conv_view, out_weight, table)


def lane_view(value):
    _, taps, full, halves, gate_local = value.shape
    blocks = gate_local // 128
    value = value.reshape(taps * full, halves, blocks, 128).transpose(0, 2, 1, 3)
    return value.reshape(taps * full * halves * blocks, 128)


def lane_back(value, shape):
    _, taps, full, halves, gate_local = shape
    blocks = gate_local // 128
    value = value.reshape(taps * full, blocks, halves, 128).transpose(0, 2, 1, 3)
    return value.reshape(shape)


def update_kernel(
    full,
    lengths_ref,
    speakers_ref,
    small_ref,
    conv_grad_in,
    out_grad_in,
    conv_w,
    conv_m,
    conv_v,
    out_w,
    out_m,
    out_v,
    table_w,
    table_m,
    table_v,
    res_in,
    skip_in,
    grad_in,
    res_out,
    skip_out,
    grad_out,
    rms_out,
    conv_g,
    conv_w_new,
    conv_m_new,
    conv_v_new,
    out_g,
    out_w_new,
    out_m_new,
    out_v_new,
    table_g,
    table_w_new,
    table_m_new,
    table_v_new,
):
    f32 = jnp.float32

    def update(gradient, weight, moment, second, rate, targets):
        new = adamw(weight[...], moment[...], second[...], gradient, rate)
        for target, value in zip(targets, new):
            target[...] = value

    for source, target in ((res_in, res_out), (skip_in, skip_out), (grad_in, grad_out)):
        target[...] = source[...].astype(f32)

    taps, width = conv_grad_in.shape
    blocks = width // 128
    for block in range(blocks):
        half, lane = block // (blocks // 2), block % (blocks // 2)
        conv_g[pl.ds(lane * 2 + half, taps, stride=blocks), :] = conv_grad_in[
            :, block * 128 : (block + 1) * 128
        ].astype(f32)
    update(conv_g[...], conv_w, conv_m, conv_v, 0.03, (conv_w_new, conv_m_new, conv_v_new))

    out_g[...] = out_grad_in[...].astype(f32).T
    update(out_g[...], out_w, out_m, out_v, 0.1, (out_w_new, out_m_new, out_v_new))

    half = width // 2
    row = lax.broadcasted_iota(jnp.int32, table_w.shape, 0) + pl.program_id(0) * table_w.shape[0]
    total = jnp.zeros(table_w.shape, f32)
    for micro in range(2):
        sums = jnp.concatenate(
            [small_ref[micro : micro + 1, 0:half], small_ref[micro : micro + 1, half:]], axis=0
        )
        total = total + jnp.where(row == speakers_ref[micro], sums[None], 0.0)
    table_g[...] = total
    update(total, table_w, table_m, table_v, 0.3, (table_w_new, table_m_new, table_v_new))

    @pl.when(pl.program_id(0) == 0)
    def _():
        counted = (lengths_ref[0] + lengths_ref[1]).astype(f32) * full
        squares = [
            jnp.sum(small_ref[8:16, part * 128 : (part + 1) * 128], axis=(0, 1), keepdims=True)
            for part in range(2)
        ]
        at = lax.broadcasted_iota(jnp.int32, (1, 2), 1)
        rms_out[...] = jnp.sqrt(jnp.where(at == 0, squares[0], squares[1]) / counted)


def run_update(lengths, speakers, small, weights, conv_parts, out_parts, table_parts, results):
    steps = 8
    width = weights.shape[1]
    gate_local, full = out_parts[0].shape[0], out_parts[0].shape[1] // 2
    f32 = jnp.float32

    def rows(value, axis=0):
        shape = list(value.shape)
        shape[axis] = pl.cdiv(shape[axis], steps)
        return pl.BlockSpec(tuple(shape), lambda i: tuple(i if at == axis else 0 for at in range(len(shape))))

    def whole(shape):
        return pl.BlockSpec(tuple(shape), lambda i: (0,) * len(shape))

    conv_block, out_block = 2 * full // steps, 2 * full // steps
    out_first = 2 * full // out_block
    smem = pl.BlockSpec(memory_space=pltpu.SMEM)
    like = [jax.ShapeDtypeStruct(value.shape, f32) for value in (results[0], conv_parts[0], out_parts[0], table_parts[0])]
    specs = [rows(results[0], 1), rows(conv_parts[0]), rows(out_parts[0], 1), rows(table_parts[0])]
    return pl.pallas_call(
        functools.partial(update_kernel, full),
        grid=(steps,),
        out_shape=(
            *[like[0]] * 3,
            jax.ShapeDtypeStruct((1, 2), f32),
            *[like[1]] * 4,
            *[like[2]] * 4,
            *[like[3]] * 4,
        ),
        in_specs=[
            smem,
            smem,
            whole(small.shape),
            pl.BlockSpec((conv_block, width), lambda i: (i, 0)),
            pl.BlockSpec(
                (out_block, gate_local),
                lambda i: (out_first + i % (steps // 2), i // (steps // 2)),
            ),
            *[specs[1]] * 3,
            *[specs[2]] * 3,
            *[specs[3]] * 3,
            *[specs[0]] * 3,
        ],
        out_specs=(
            *[specs[0]] * 3,
            whole((1, 2)),
            *[specs[1]] * 4,
            *[specs[2]] * 4,
            *[specs[3]] * 4,
        ),
        compiler_params=pltpu.CompilerParams(
            dimension_semantics=("arbitrary",), vmem_limit_bytes=62 * 1024 * 1024
        ),
        cost_estimate=pl.CostEstimate(
            flops=20_000_000, bytes_accessed=32_000_000, transcendentals=1_000_000
        ),
    )(
        lengths,
        speakers,
        small,
        weights,
        weights,
        *conv_parts,
        *out_parts,
        *table_parts,
        *results,
    )


def fast_shards(
    n_seq,
    x_in,
    skip_in,
    cot_res,
    cot_skip,
    lengths,
    speakers,
    conv_weight,
    conv_m,
    conv_v,
    out_weight,
    out_m,
    out_v,
    speaker_table,
    table_m,
    table_v,
):
    views = [lane_view(value) for value in (conv_weight, conv_m, conv_v)]
    res, skipped, grads, weights, small = run_layers(
        x_in,
        skip_in,
        cot_res,
        cot_skip,
        lengths,
        speakers,
        views[0],
        out_weight[0],
        speaker_table[0],
        n_seq,
    )
    results = run_update(
        lengths,
        speakers,
        small,
        weights,
        views,
        [out_weight[0], out_m[0], out_v[0]],
        [speaker_table[0], table_m[0], table_v[0]],
        [res, skipped, grads],
    )
    wide, rms_out = results[0:3], results[3]
    conv_parts = [lane_back(value, conv_weight.shape) for value in results[4:8]]
    return (
        *[value[None] for value in wide],
        rms_out,
        *conv_parts,
        *[value[None] for value in results[8:12]],
        *[value[None] for value in results[12:16]],
    )


def shards(
    x_in,
    skip_in,
    cot_res,
    cot_skip,
    lengths,
    speakers,
    conv_weight,
    conv_m,
    conv_v,
    out_weight,
    out_m,
    out_v,
    speaker_table,
    table_m,
    table_v,
):
    micro_count, residual_local, block_length_rows = x_in.shape
    leading_section = lax.axis_index("section") == 0
    seq_index = lax.axis_index("seq")
    dilation_factor = jnp.where(leading_section, FIRST_DILATION, 1).astype(jnp.int32)
    conv_low = conv_weight[0].astype(jnp.bfloat16)
    full_res = conv_low.shape[1]
    gate_dev = conv_low.shape[3]
    speaker_rows = speaker_table.shape[1]
    conv_matrix = conv_low.reshape(2 * full_res, 2 * gate_dev)
    output_low = out_weight[0].astype(jnp.bfloat16)
    table_low = speaker_table[0].astype(jnp.bfloat16).reshape(speaker_rows, 2 * gate_dev)
    positions = seq_index * block_length_rows + jnp.arange(block_length_rows)
    contract_first = (((0,), (0,)), ((), ()))
    contract_last = (((1,), (1,)), ((), ()))
    recv_resid = jnp.zeros((residual_local, block_length_rows), jnp.float32)
    recv_skip = jnp.zeros((residual_local, block_length_rows), jnp.float32)
    kept_list = []
    resid_list = []
    skip_list = []
    square_res = jnp.float32(0.0)
    square_branch = jnp.float32(0.0)
    counted = jnp.float32(0.0)
    for tick_num in range(micro_count + 1):
        index_zero = min(tick_num, micro_count - 1)
        index_one = max(tick_num - 1, 0)
        batch_idx = jnp.where(leading_section, index_zero, index_one)
        is_live = jnp.where(leading_section, tick_num < micro_count, tick_num >= 1).astype(
            jnp.float32
        )
        residual_stream = jnp.where(
            leading_section, x_in[index_zero].astype(jnp.float32), recv_resid
        )
        skip_accumulated = jnp.where(leading_section, skip_in[index_zero], recv_skip)
        onehot = (jnp.arange(speaker_rows) == speakers[batch_idx]).astype(jnp.bfloat16)
        input_signal = residual_stream.astype(jnp.bfloat16)
        preceding_state = passed_along(
            input_signal[:, block_length_rows - FIRST_DILATION :], "seq", 1
        )
        joined_taps = jnp.concatenate([preceding_state, input_signal], axis=1)
        delayed_tap = lax.dynamic_slice_in_dim(
            joined_taps, FIRST_DILATION - dilation_factor, block_length_rows, 1
        )
        tap_rows = jnp.stack([delayed_tap, input_signal], axis=0)
        forward_tap_full = lax.all_gather(tap_rows, "mp", axis=1, tiled=True).reshape(
            2 * full_res, block_length_rows
        )
        embedding = jnp.dot(onehot, table_low, preferred_element_type=jnp.float32)
        forward_preact = (
            lax.dot_general(
                conv_matrix, forward_tap_full, contract_first, preferred_element_type=jnp.float32
            )
            + embedding[:, None]
        )
        hidden = (
            jnp.tanh(forward_preact[:gate_dev]) * jax.nn.sigmoid(forward_preact[gate_dev:])
        ).astype(jnp.bfloat16)
        partial_sums = lax.dot_general(
            output_low, hidden, contract_first, preferred_element_type=jnp.float32
        ).reshape(2, full_res, block_length_rows)
        projected = lax.psum_scatter(partial_sums, "mp", scatter_dimension=1, tiled=True)
        branch = projected[0]
        new_resid = (residual_stream + branch) * root_half
        new_skip = skip_accumulated + projected[1]
        new_resid, new_skip, branch, kept_data = (
            new_resid,
            new_skip,
            branch,
            (forward_tap_full, forward_preact, hidden),
        )
        valid_rows = (positions < lengths[batch_idx]).astype(jnp.float32)[None, :] * is_live
        square_res = square_res + jnp.sum(valid_rows * new_resid * new_resid)
        square_branch = square_branch + jnp.sum(valid_rows * branch * branch)
        counted = counted + jnp.sum(valid_rows) * residual_local
        kept_list.append(kept_data)
        resid_list.append(new_resid)
        skip_list.append(new_skip)
        if tick_num < micro_count:
            recv_resid, recv_skip = passed_along((new_resid, new_skip), "section", 1)
    square_res, square_branch, counted = lax.psum(
        (square_res, square_branch, counted), ("seq", "mp")
    )
    rms_out = jnp.stack([jnp.sqrt(square_res / counted), jnp.sqrt(square_branch / counted)])[None]
    res_out = jnp.stack(
        [
            jnp.where(leading_section, resid_list[m_idx], resid_list[m_idx + 1])
            for m_idx in range(micro_count)
        ]
    )[None]
    skip_out = jnp.stack(
        [
            jnp.where(leading_section, skip_list[m_idx], skip_list[m_idx + 1])
            for m_idx in range(micro_count)
        ]
    )[None]
    conv_acc = jnp.zeros((2 * full_res, 2 * gate_dev), jnp.float32)
    table_acc = jnp.zeros((speaker_rows, 2 * gate_dev), jnp.float32)
    out_acc = jnp.zeros((gate_dev, 2 * full_res), jnp.float32)
    recv_grad = jnp.zeros((residual_local, block_length_rows), jnp.float32)
    input_grads = []
    for tick_num in range(micro_count + 1):
        index_one = min(tick_num, micro_count - 1)
        index_zero = max(tick_num - 1, 0)
        batch_idx = jnp.where(leading_section, index_zero, index_one)
        is_live = jnp.where(leading_section, tick_num >= 1, tick_num < micro_count).astype(
            jnp.float32
        )
        valid_rows = (positions < lengths[batch_idx]).astype(jnp.float32)[None, :] * is_live
        onehot = (jnp.arange(speaker_rows) == speakers[batch_idx]).astype(jnp.bfloat16)
        kept_data = jax.tree.map(
            lambda zero_side, one_side: jnp.where(leading_section, zero_side, one_side),
            kept_list[index_zero],
            kept_list[index_one + 1],
        )
        skip_grad = (
            jnp.where(leading_section, cot_skip[index_zero], cot_skip[index_one]) * valid_rows
        )
        resid_grad = jnp.where(
            leading_section, recv_grad * is_live, cot_res[index_one] * valid_rows
        )
        tap_full, preact, hidden_used = kept_data
        proj_grad = jnp.stack([resid_grad * root_half, skip_grad], axis=0).astype(jnp.bfloat16)
        full_grad = lax.all_gather(proj_grad, "mp", axis=1, tiled=True).reshape(
            2 * full_res, block_length_rows
        )
        hidden_grad = jnp.dot(output_low, full_grad, preferred_element_type=jnp.float32)
        weight_term = lax.dot_general(
            hidden_used, full_grad, contract_last, preferred_element_type=jnp.float32
        )
        filter_act = jnp.tanh(preact[:gate_dev])
        gate_act = jax.nn.sigmoid(preact[gate_dev:])
        filter_grad = hidden_grad * gate_act * (1.0 - filter_act * filter_act)
        gate_grad = hidden_grad * filter_act * gate_act * (1.0 - gate_act)
        preact_grad = jnp.concatenate([filter_grad, gate_grad], axis=0).astype(jnp.bfloat16)
        conv_term = lax.dot_general(
            tap_full, preact_grad, contract_last, preferred_element_type=jnp.float32
        )
        column_sums = jnp.sum(preact_grad.astype(jnp.float32), axis=1)
        table_term = onehot.astype(jnp.float32)[:, None] * column_sums[None, :]
        tap_terms = jnp.dot(conv_matrix, preact_grad, preferred_element_type=jnp.float32)
        tap_gradient = lax.psum_scatter(
            tap_terms.reshape(2, full_res, block_length_rows), "mp", scatter_dimension=1, tiled=True
        )
        joined_taps_gradient = lax.dynamic_update_slice_in_dim(
            jnp.zeros((residual_local, FIRST_DILATION + block_length_rows), jnp.float32),
            tap_gradient[0],
            FIRST_DILATION - dilation_factor,
            1,
        )
        border_gradient = passed_along(joined_taps_gradient[:, :FIRST_DILATION], "seq", -1)
        input_gradient_rows = tap_gradient[1] + joined_taps_gradient[:, FIRST_DILATION:]
        input_gradient_rows = input_gradient_rows.at[:, block_length_rows - FIRST_DILATION :].add(
            border_gradient
        )
        resid_back, conv_term, weight_term, table_term = (
            resid_grad * root_half + input_gradient_rows,
            conv_term,
            weight_term,
            table_term,
        )
        conv_acc = conv_acc + conv_term
        out_acc = out_acc + weight_term
        table_acc = table_acc + table_term
        input_grads.append(resid_back)
        if tick_num < micro_count:
            recv_grad = passed_along(resid_back, "section", -1)
    grad_in = jnp.stack(
        [
            jnp.where(leading_section, input_grads[m_idx + 1], input_grads[m_idx])
            for m_idx in range(micro_count)
        ]
    )[None]
    conv_total, out_total, table_total = lax.psum((conv_acc, out_acc, table_acc), "seq")
    conv_grad = conv_total.reshape(conv_weight.shape)
    out_grad = out_total.reshape(out_weight.shape)
    table_grad = table_total.reshape(speaker_table.shape)
    conv_new, conv_m_new, conv_v_new = adamw(conv_weight, conv_m, conv_v, conv_grad, 0.03)
    out_new, out_m_new, out_v_new = adamw(out_weight, out_m, out_v, out_grad, 0.1)
    table_new, table_m_new, table_v_new = adamw(speaker_table, table_m, table_v, table_grad, 0.3)
    return (
        res_out,
        skip_out,
        grad_in,
        rms_out,
        conv_grad,
        conv_new,
        conv_m_new,
        conv_v_new,
        out_grad,
        out_new,
        out_m_new,
        out_v_new,
        table_grad,
        table_new,
        table_m_new,
        table_v_new,
    )


def solution(mesh):
    in_specs = (
        P(None, "mp", "seq"),
        P(None, "mp", "seq"),
        P(None, "mp", "seq"),
        P(None, "mp", "seq"),
        P(),
        P(),
        P("section", None, None, None, "mp"),
        P("section", None, None, None, "mp"),
        P("section", None, None, None, "mp"),
        P("section", "mp", None),
        P("section", "mp", None),
        P("section", "mp", None),
        P("section", None, None, "mp"),
        P("section", None, None, "mp"),
        P("section", None, None, "mp"),
    )
    out_specs = (
        P("section", None, "mp", "seq"),
        P("section", None, "mp", "seq"),
        P("section", None, "mp", "seq"),
        P("section", None),
        P("section", None, None, None, "mp"),
        P("section", None, None, None, "mp"),
        P("section", None, None, None, "mp"),
        P("section", None, None, None, "mp"),
        P("section", "mp", None),
        P("section", "mp", None),
        P("section", "mp", None),
        P("section", "mp", None),
        P("section", None, None, "mp"),
        P("section", None, None, "mp"),
        P("section", None, None, "mp"),
        P("section", None, None, "mp"),
    )
    n_seq = mesh.shape["seq"]
    fits = mesh.shape["mp"] == 2 and n_seq in (4, 8, 16)
    return jax.shard_map(
        functools.partial(fast_shards, n_seq) if fits else shards,
        mesh=mesh,
        in_specs=in_specs,
        out_specs=out_specs,
        check_vma=False,
    )
```
